128 devices in a mesh: row: 8 (over x, z_hi), col: 16 (over z_lo, y, core).
Axes of the slice: x: 4, y: 4, z: 4 (z_hi: 2, z_lo: 2; z = z_hi * 2 + z_lo), core: 2. Of those that a mesh axis runs over, the one named last changes fastest.
Arguments:
- fine_qkv: bfloat16 [3, 128, 256, 384], P(None, 'row', 'col'), may hold values from -256 to 256
- coarse_qkv: bfloat16 [3, 128, 64, 1536], P(None, 'col', None, 'row'), may hold values from -256 to 256
- grad_coarse: bfloat16 [128, 64, 1536], P('col', None, 'row'), may hold values from -256 to 256
- merge_weight: bfloat16 [1536, 1536], replicated, may hold values from -0.15625 to 0.15625
- qkv_weight: bfloat16 [3, 1536, 1536], P(None, None, 'row'), may hold values from -0.15625 to 0.15625
Outputs:
- grad_query_fine: bfloat16 [128, 256, 384], P('row', 'col')
- grad_key_fine: bfloat16 [128, 256, 384], P('row', 'col')
- grad_value_fine: bfloat16 [128, 256, 384], P('row', 'col')
The draws below stay inside these ranges and needn't reach their ends.
All inputs are finite; a program needn't handle non-finite values.
Results may differ from the reference program's by a relative error of at most 0.025.
Values may be sent and summed in bfloat16 or wider, within the bound.
No kernel may reach another device: no remote copies, remote signals or barrier semaphores. Data moves between devices by JAX's collectives and lax.ppermute only.
A program may use at most 320 MiB of HBM per device.

```python
import math
import jax
import jax.numpy as jnp
from jax import lax

D1 = 384
D2 = 1536
HD = 64
RADIUS = 7
FROWS = 128
FCOLS = 256
CROWS = 64
CCOLS = 128


def scaled_triple(key, rows, columns, width, query_scale):
    pieces = jax.random.split(key, 2)
    unit = jax.random.normal(pieces[0], (3, rows, columns, width), jnp.float32)
    spread = jnp.exp(jax.random.uniform(pieces[1], (3, rows, columns, 1), jnp.float32, -1.2039728, 1.0986123))
    factor = jnp.array([query_scale, 1.0, 1.0], jnp.float32).reshape(3, 1, 1, 1)
    return jnp.clip(unit * spread * factor, -256.0, 256.0).astype(jnp.bfloat16)


def draw_fine_qkv(key, part):
    key = jax.random.fold_in(key, 5)
    return scaled_triple(key, FROWS, FCOLS, D1, 1.0)


def draw_coarse_qkv(key, part):
    own = jax.random.fold_in(key, 9)
    return scaled_triple(own, CCOLS, CROWS, D2, 0.0625)


def draw_grad_coarse(key, part):
    own = jax.random.fold_in(key, 13)
    level = 0.25 * math.sqrt(CCOLS * CROWS)
    unit = jax.random.normal(own, (CCOLS, CROWS, D2), jnp.float32)
    return jnp.clip(level * unit, -6.0 * level, 6.0 * level).astype(jnp.bfloat16)


def shard_levels(own_key, extent, cuts, least, top_value):
    def one(axis_at, shards_of):
        heights = jax.random.uniform(jax.random.fold_in(jax.random.fold_in(own_key, 6), axis_at), (shards_of,), jnp.float32, least / len(cuts), top_value / len(cuts))
        return jnp.repeat(jnp.exp(heights), extent[axis_at] // shards_of).reshape((-1,) + (1,) * (len(extent) - axis_at - 1))

    gain = one(*cuts[0])
    for cut in cuts[1:]:
        gain = gain * one(*cut)
    return gain


def centred(stream_key, shape, scale, reach, shards=(), kind=jnp.bfloat16):
    values = scale * jax.random.normal(stream_key, shape, jnp.float32)
    if shards:
        values = values * shard_levels(stream_key, shape, shards, -0.22, 0.18)
    return jnp.clip(values, -reach, reach).astype(kind)


def setup_inputs(seed: int = 0) -> dict:
    splits = jax.random.split(jax.random.key(seed), 6)
    fine_qkv = draw_fine_qkv(jax.random.fold_in(splits[5], 71), 0)
    coarse_qkv = draw_coarse_qkv(jax.random.fold_in(splits[5], 71), 0)
    grad_coarse = draw_grad_coarse(jax.random.fold_in(splits[5], 71), 0)
    merge_weight = centred(splits[3], (4 * D1, D2), (4 * D1) ** -0.5, 0.15625)
    qkv_weight = centred(splits[4], (3, D2, D2), D2 ** -0.5, 0.15625, ((2, 8),))
    return dict(fine_qkv=fine_qkv, coarse_qkv=coarse_qkv, grad_coarse=grad_coarse, merge_weight=merge_weight, qkv_weight=qkv_weight)


def coarse_head(query, key, value, upstream):
    scale = HD ** -0.5
    raw = jnp.dot(query, key.T, preferred_element_type=jnp.float32) * scale
    log_total = jax.nn.logsumexp(raw, axis=1)
    shares = jnp.exp(raw - log_total[:, None])
    product = jnp.dot(upstream, value.T, preferred_element_type=jnp.float32)
    delta = jnp.sum(shares * product, axis=1)
    score_grads = (shares * (product - delta[:, None])).astype(jnp.bfloat16)
    probs = shares.astype(jnp.bfloat16)
    query_grad = (jnp.dot(score_grads, key, preferred_element_type=jnp.float32) * scale).astype(jnp.bfloat16)
    key_grad = (jnp.dot(score_grads.T, query, preferred_element_type=jnp.float32) * scale).astype(jnp.bfloat16)
    value_grad = jnp.dot(probs.T, upstream, preferred_element_type=jnp.float32).astype(jnp.bfloat16)
    return query_grad, key_grad, value_grad


def fine_grads(fine_qkv, out_grads):
    scale = HD ** -0.5
    heads = D1 // HD
    span = 2 * RADIUS + 1
    zero = jnp.zeros((), jnp.int32)
    border = ((RADIUS, RADIUS), (RADIUS, RADIUS), (0, 0), (0, 0))
    query = fine_qkv[0].astype(jnp.float32).reshape(FROWS, FCOLS, heads, HD)
    key_pad = jnp.pad(fine_qkv[1].astype(jnp.float32).reshape(FROWS, FCOLS, heads, HD), border)
    value_pad = jnp.pad(fine_qkv[2].astype(jnp.float32).reshape(FROWS, FCOLS, heads, HD), border)
    upstream = out_grads.astype(jnp.float32).reshape(FROWS, FCOLS, heads, HD)
    inside = jnp.pad(jnp.ones((FROWS, FCOLS), jnp.float32), RADIUS)
    offsets = jnp.arange(span * span, dtype=jnp.int32)

    def shifted(array, offset):
        return lax.dynamic_slice(array, (offset // span, offset % span, zero, zero), (FROWS, FCOLS, heads, HD))

    def score(offset):
        mask = lax.dynamic_slice(inside, (offset // span, offset % span), (FROWS, FCOLS))
        raw = jnp.einsum("abhd,abhd->hab", query, shifted(key_pad, offset)) * scale
        return jnp.where(mask[None] > 0, raw, -jnp.inf)

    def dots(offset):
        return jnp.einsum("abhd,abhd->hab", upstream, shifted(value_pad, offset))

    scores = lax.map(score, offsets)
    log_total = jax.nn.logsumexp(scores, axis=0)
    shares = jnp.exp(scores - log_total[None])
    products = lax.map(dots, offsets)
    delta = jnp.sum(shares * products, axis=0)
    score_grads = (shares * (products - delta[None])).astype(jnp.bfloat16)
    probs = shares.astype(jnp.bfloat16)

    def accumulate(carry, offset):
        query_acc, key_acc, value_acc = carry
        start = (offset // span, offset % span, zero, zero)
        weight = score_grads[offset].astype(jnp.float32)
        prob = probs[offset].astype(jnp.float32)
        query_acc = query_acc + jnp.einsum("hab,abhd->abhd", weight, shifted(key_pad, offset))
        key_piece = lax.dynamic_slice(key_acc, start, (FROWS, FCOLS, heads, HD)) + jnp.einsum("hab,abhd->abhd", weight, query)
        key_acc = lax.dynamic_update_slice(key_acc, key_piece, start)
        value_piece = lax.dynamic_slice(value_acc, start, (FROWS, FCOLS, heads, HD)) + jnp.einsum("hab,abhd->abhd", prob, upstream)
        value_acc = lax.dynamic_update_slice(value_acc, value_piece, start)
        return (query_acc, key_acc, value_acc), None

    starting = (jnp.zeros((FROWS, FCOLS, heads, HD), jnp.float32), jnp.zeros_like(key_pad), jnp.zeros_like(value_pad))
    (query_acc, key_acc, value_acc), _ = lax.scan(accumulate, starting, offsets)
    key_crop = key_acc[RADIUS:RADIUS + FROWS, RADIUS:RADIUS + FCOLS]
    value_crop = value_acc[RADIUS:RADIUS + FROWS, RADIUS:RADIUS + FCOLS]
    grad_query = (query_acc * scale).reshape(FROWS, FCOLS, D1).astype(jnp.bfloat16)
    grad_key = (key_crop * scale).reshape(FROWS, FCOLS, D1).astype(jnp.bfloat16)
    grad_value = value_crop.reshape(FROWS, FCOLS, D1).astype(jnp.bfloat16)
    return grad_query, grad_key, grad_value


def reference(fine_qkv, coarse_qkv, grad_coarse, merge_weight, qkv_weight):
    tokens = CCOLS * CROWS
    heads = D2 // HD

    def split_heads(array):
        return array.reshape(tokens, heads, HD).transpose(1, 0, 2)

    def join_heads(array):
        return array.transpose(1, 0, 2).reshape(tokens, D2)

    def one_head(inputs):
        return coarse_head(inputs[0], inputs[1], inputs[2], inputs[3])

    query_grad, key_grad, value_grad = lax.map(one_head, (split_heads(coarse_qkv[0]), split_heads(coarse_qkv[1]), split_heads(coarse_qkv[2]), split_heads(grad_coarse)))
    hidden = jnp.dot(join_heads(query_grad), qkv_weight[0].T, preferred_element_type=jnp.float32)
    hidden = hidden + jnp.dot(join_heads(key_grad), qkv_weight[1].T, preferred_element_type=jnp.float32)
    hidden = hidden + jnp.dot(join_heads(value_grad), qkv_weight[2].T, preferred_element_type=jnp.float32)
    hidden_grads = hidden.astype(jnp.bfloat16)
    hidden_grid = hidden_grads.reshape(CCOLS, CROWS, D2).transpose(1, 0, 2).reshape(CROWS * CCOLS, D2)
    merged_grads = jnp.dot(hidden_grid, merge_weight.T, preferred_element_type=jnp.float32).astype(jnp.bfloat16)
    out_grads = merged_grads.reshape(CROWS, CCOLS, 2, 2, D1).transpose(0, 2, 1, 3, 4).reshape(FROWS, FCOLS, D1)
    return fine_grads(fine_qkv, out_grads)
```

```python
import jax
import jax.numpy as jnp
from jax import lax
from jax.experimental import pallas as pl
from jax.experimental.pallas import tpu as pltpu
from jax.sharding import Mesh
from jax.sharding import PartitionSpec as P

HD = 64
RADIUS = 7
SCALE = 0.125
SIDE = 32
HIDDEN = -1e30
ROW = ("x", "zh")
COL = ("zl", "y", "c")
F32 = jnp.float32
BF16 = jnp.bfloat16
VMEM = 60 << 20


def nt(left, right):
    return lax.dot_general(left, right, (((1,), (1,)), ((), ())), preferred_element_type=F32)


def nn(left, right):
    return lax.dot_general(left, right, (((1,), (0,)), ((), ())), preferred_element_type=F32)


def half(pair, which):
    lane = lax.broadcasted_iota(jnp.int32, pair.shape, 1)
    return jnp.where((lane < HD) == (which == 0), pair, jnp.zeros_like(pair))


def cost(flops, bytes_accessed, exps):
    return pl.CostEstimate(flops=flops, bytes_accessed=bytes_accessed, transcendentals=exps)


def coarse_stats(key_value, query_up, query_tile, key_tile, unroll):
    heads, keys, _ = key_value.shape
    queries = query_up.shape[1]

    def body(kv_ref, qu_ref, out_ref):
        query = half(qu_ref[0], 0) * BF16(SCALE)
        upstream = half(qu_ref[0], 1)

        def step(i, carry):
            peak, total, weighted = carry
            tile = kv_ref[0, pl.ds(pl.multiple_of(i * key_tile, key_tile), key_tile), :]
            score = nt(tile, query)
            product = nt(tile, upstream)
            new_peak = jnp.maximum(peak, jnp.max(score, axis=0, keepdims=True))
            decay = jnp.exp(peak - new_peak)
            share = jnp.exp(score - new_peak)
            return (
                new_peak,
                total * decay + jnp.sum(share, axis=0, keepdims=True),
                weighted * decay + jnp.sum(share * product, axis=0, keepdims=True),
            )

        zero = jnp.zeros((1, query_tile), F32)
        peak, total, weighted = lax.fori_loop(
            0, keys // key_tile, step, (zero - jnp.inf, zero, zero), unroll=unroll
        )
        out_ref[0] = jnp.concatenate([peak + jnp.log(total), weighted / total], axis=0)

    return pl.pallas_call(
        body,
        grid=(heads, queries // query_tile),
        in_specs=[
            pl.BlockSpec((1, keys, 128), lambda h, q: (h, 0, 0)),
            pl.BlockSpec((1, query_tile, 128), lambda h, q: (h, q, 0)),
        ],
        out_specs=pl.BlockSpec((1, 2, query_tile), lambda h, q: (h, 0, q)),
        out_shape=jax.ShapeDtypeStruct((heads, 2, queries), F32),
        name="coarse_stats",
        cost_estimate=cost(4 * heads * keys * queries * 256, 2 << 20, heads * keys * queries),
        compiler_params=pltpu.CompilerParams(vmem_limit_bytes=VMEM),
    )(key_value, query_up)


def coarse_grads(key_value, query_up, stats, query_tile, key_tile, unroll):
    heads, keys, _ = key_value.shape
    queries = query_up.shape[1]
    tiles = queries // query_tile

    def body(kv_ref, qu_ref, stats_ref, kv_out, q_out, acc):
        @pl.when(pl.program_id(1) == 0)
        def _():
            acc[...] = jnp.zeros_like(acc)

        query = half(qu_ref[0], 0) * BF16(SCALE)
        upstream = half(qu_ref[0], 1)
        log_total = stats_ref[0, 0:1, :]
        delta = stats_ref[0, 1:2, :]

        def step(i, carry):
            rows = pl.ds(pl.multiple_of(i * key_tile, key_tile), key_tile)
            tile = kv_ref[0, rows, :]
            share = jnp.exp(nt(tile, query) - log_total)
            grads = (share * (nt(tile, upstream) - delta)).astype(BF16)
            acc[rows, :] += nn(grads, query) + nn(share.astype(BF16), upstream)
            return carry + nn(tile[:, :HD].T, grads)

        found = lax.fori_loop(
            0, keys // key_tile, step, jnp.zeros((HD, query_tile), F32), unroll=unroll
        )
        q_out[...] = (found * SCALE).astype(BF16)

        @pl.when(pl.program_id(1) == tiles - 1)
        def _():
            kv_out[0] = acc[...].astype(BF16)

    return pl.pallas_call(
        body,
        grid=(heads, tiles),
        in_specs=[
            pl.BlockSpec((1, keys, 128), lambda h, q: (h, 0, 0)),
            pl.BlockSpec((1, query_tile, 128), lambda h, q: (h, q, 0)),
            pl.BlockSpec((1, 2, query_tile), lambda h, q: (h, 0, q)),
        ],
        out_specs=[
            pl.BlockSpec((1, keys, 128), lambda h, q: (h, 0, 0)),
            pl.BlockSpec((HD, query_tile), lambda h, q: (h, q)),
        ],
        out_shape=[
            jax.ShapeDtypeStruct((heads, keys, 128), BF16),
            jax.ShapeDtypeStruct((heads * HD, queries), BF16),
        ],
        scratch_shapes=[pltpu.VMEM((keys, 128), F32)],
        name="coarse_grads",
        cost_estimate=cost(10 * heads * keys * queries * 256, 4 << 20, heads * keys * queries),
        compiler_params=pltpu.CompilerParams(vmem_limit_bytes=VMEM),
    )(key_value, query_up, stats)


def whole_call(body, out_shape, name, flops, *operands):
    return pl.pallas_call(
        body,
        out_shape=out_shape,
        name=name,
        cost_estimate=cost(flops, 6 << 20, 1 << 20),
        compiler_params=pltpu.CompilerParams(vmem_limit_bytes=VMEM),
    )(*operands)


def pairs_of(width):
    return [(pair, slice(pair * 128, pair * 128 + 128)) for pair in range(width // 128)]


def fine_forward(own_query, ext_key, ext_value, bias):
    own, width = own_query.shape

    def body(q_ref, k_ref, v_ref, bias_ref, out_ref):
        logs = []
        for _, lanes in pairs_of(width):
            key = k_ref[:, lanes]
            value_t = v_ref[:, lanes].T
            parts = []
            for side in range(2):
                query = half(q_ref[:, lanes], side) * BF16(SCALE)
                score = nt(key, query) + bias_ref[...]
                peak = jnp.max(score, axis=0, keepdims=True)
                share = jnp.exp(score - peak)
                logs.append(peak + jnp.log(jnp.sum(share, axis=0, keepdims=True)))
                rounded = share.astype(BF16)
                total = jnp.sum(rounded.astype(F32), axis=0, keepdims=True)
                parts.append(nn(value_t[side * HD : side * HD + HD], rounded) / total)
            out_ref[:, lanes] = jnp.concatenate(parts, axis=0).T
        logs.append(jnp.zeros((128 - len(logs), own), F32))
        out_ref[:, width:] = jnp.concatenate(logs, axis=0).T

    return whole_call(
        body,
        jax.ShapeDtypeStruct((own, width + 128), F32),
        "fine_forward",
        2 << 30,
        own_query,
        ext_key,
        ext_value,
        bias,
    )


def head_sums(up, out):
    width = up.shape[1]
    head = lax.broadcasted_iota(jnp.int32, (8, width), 0)
    lane = lax.broadcasted_iota(jnp.int32, (8, width), 1)
    pick = jnp.where(lane // HD == head, 1.0, 0.0).astype(F32)
    return lax.dot_general(
        pick,
        up.astype(F32) * out,
        (((1,), (1,)), ((), ())),
        preferred_element_type=F32,
        precision=lax.Precision.HIGHEST,
    )


def fine_query_grads(own_query, ext_key, ext_value, own_up, own_out, bias):
    own, width = own_query.shape

    def body(q_ref, k_ref, v_ref, up_ref, o_ref, bias_ref, out_ref):
        delta = head_sums(up_ref[...], o_ref[:, :width])
        logs = o_ref[:, width:].T
        for pair, lanes in pairs_of(width):
            key = k_ref[:, lanes]
            key_t = key.T
            value = v_ref[:, lanes]
            parts = []
            for side in range(2):
                head = 2 * pair + side
                query = half(q_ref[:, lanes], side) * BF16(SCALE)
                up = half(up_ref[:, lanes], side)
                share = jnp.exp(nt(key, query) + bias_ref[...] - logs[head : head + 1])
                grads = (share * (nt(value, up) - delta[head : head + 1])).astype(BF16)
                parts.append(nn(key_t[side * HD : side * HD + HD], grads))
            out_ref[:, lanes] = (jnp.concatenate(parts, axis=0).T * SCALE).astype(BF16)

    return whole_call(
        body,
        jax.ShapeDtypeStruct((own, width), BF16),
        "fine_query_grads",
        2 << 30,
        own_query,
        ext_key,
        ext_value,
        own_up,
        own_out,
        bias,
    )


def fine_key_grads(own_key, own_value, ext_query, ext_up, ext_out, bias):
    own, width = own_key.shape

    def body(k_ref, v_ref, q_ref, up_ref, o_ref, bias_ref, k_out, v_out):
        delta = head_sums(up_ref[...], o_ref[:, :width])
        logs = o_ref[:, width:].T
        for pair, lanes in pairs_of(width):
            key = k_ref[:, lanes]
            value = v_ref[:, lanes]
            key_sum = jnp.zeros((own, 128), F32)
            value_sum = jnp.zeros((own, 128), F32)
            for side in range(2):
                head = 2 * pair + side
                query = half(q_ref[:, lanes], side) * BF16(SCALE)
                up = half(up_ref[:, lanes], side)
                share = jnp.exp(nt(key, query) + bias_ref[...] - logs[head : head + 1])
                grads = (share * (nt(value, up) - delta[head : head + 1])).astype(BF16)
                key_sum += nn(grads, query)
                value_sum += nn(share.astype(BF16), up)
            k_out[:, lanes] = key_sum.astype(BF16)
            v_out[:, lanes] = value_sum.astype(BF16)

    return whole_call(
        body,
        [jax.ShapeDtypeStruct((own, width), BF16)] * 2,
        "fine_key_grads",
        3 << 30,
        own_key,
        own_value,
        ext_query,
        ext_up,
        ext_out,
        bias,
    )


def shifted(array, axis, step):
    count = lax.axis_size(axis)
    return lax.ppermute(array, axis, [(i, (i + step) % count) for i in range(count)])


def swapped(array, axis):
    return lax.ppermute(array, axis, [(0, 1), (1, 0)])


def with_rim(block, dim):
    for axis, at in ((ROW, dim), (COL, dim + 1)):
        count = lax.axis_size(axis)
        forward = [(i, i + 1) for i in range(count - 1)]
        backward = [(i + 1, i) for i in range(count - 1)]
        size = block.shape[at]
        low = lax.ppermute(
            lax.slice_in_dim(block, size - RADIUS, None, axis=at), axis, forward
        )
        high = lax.ppermute(lax.slice_in_dim(block, 0, RADIUS, axis=at), axis, backward)
        rest = list(block.shape)
        rest[at] = SIDE - size - 2 * RADIUS
        block = jnp.concatenate([low, block, high, jnp.zeros(rest, block.dtype)], axis=at)
    return block.reshape(block.shape[:dim] + (SIDE * SIDE, block.shape[-1]))


def window_bias(rows, columns):
    def near(size, axis):
        place = jnp.arange(SIDE, dtype=jnp.int32)
        whole = place + lax.axis_index(axis) * size - RADIUS
        inside = (whole >= 0) & (whole < lax.axis_size(axis) * size)
        gap = place[:, None] - jnp.arange(size, dtype=jnp.int32)[None, :]
        return (gap >= 0) & (gap <= 2 * RADIUS) & inside[:, None]

    row_near = near(rows, ROW)
    column_near = near(columns, COL)
    both = row_near[:, None, :, None] & column_near[None, :, None, :]
    return jnp.where(both, 0.0, HIDDEN).astype(F32).reshape(SIDE * SIDE, rows * columns)


def by_head(first, second, heads):
    tokens = first.shape[0]
    joined = jnp.concatenate(
        [first.reshape(tokens, heads, HD), second.reshape(tokens, heads, HD)], axis=2
    )
    return joined.transpose(1, 0, 2)


def shards(fine_qkv, coarse_qkv, grad_coarse, merge_weight, qkv_weight):
    rows, columns, width = fine_qkv.shape[1:]
    own = rows * columns
    coarse_columns, coarse_rows, group = grad_coarse.shape
    tokens = coarse_columns * coarse_rows
    heads = group // HD
    wide = merge_weight.shape[0]

    flat = coarse_qkv.reshape(3, tokens, group)
    key_value = by_head(flat[1], flat[2], heads)
    query_up = by_head(flat[0], grad_coarse.reshape(tokens, group), heads)
    across = swapped(key_value, "zl")
    beside = swapped(key_value, "c")
    queries = [query_up] + [shifted(query_up, "y", step) for step in (1, 2, 3)]
    corner = swapped(across, "c")
    all_keys = jnp.concatenate([key_value, beside, across, corner], axis=1)
    all_queries = jnp.concatenate(queries, axis=1)

    weight = qkv_weight.reshape(3, wide, heads, HD)
    weight = jnp.concatenate(
        [
            weight[0].reshape(wide, group),
            jnp.concatenate([weight[1], weight[2]], axis=2).reshape(wide, 2 * group),
        ],
        axis=1,
    )
    joint_weight = lax.dot_general(
        weight, merge_weight, (((0,), (1,)), ((), ())), preferred_element_type=F32
    ).astype(BF16)

    extended = with_rim(fine_qkv, 1)
    bias = window_bias(rows, columns)
    bias_t = bias.T
    own_query = fine_qkv[0].reshape(own, width)
    own_key = fine_qkv[1].reshape(own, width)
    own_value = fine_qkv[2].reshape(own, width)

    part = coarse_stats(all_keys, all_queries, 512, 256, 2).reshape(2 * heads, 4, tokens)
    parts = [part] + [jnp.roll(shifted(part, "y", step), step, axis=1) for step in (1, 2, 3)]
    own_out = fine_forward(own_query, extended[1], extended[2], bias)
    ext_out = with_rim(own_out.reshape(rows, columns, width + 128), 0)
    stacked = jnp.stack(parts).reshape(4, heads, 2, 4 * tokens)
    logs, deltas = stacked[:, :, 0], stacked[:, :, 1]
    peak = jnp.max(logs, axis=0)
    shares = jnp.exp(logs - peak)
    total = jnp.sum(shares, axis=0)
    stats = jnp.stack([peak + jnp.log(total), jnp.sum(shares * deltas, axis=0) / total], axis=1)

    key_value_grads, query_grads = coarse_grads(all_keys, all_queries, stats, 512, 256, 2)
    query_sum = query_grads[:, :tokens].astype(F32)
    for step in (1, 2, 3):
        piece = query_grads[:, step * tokens : (step + 1) * tokens]
        query_sum = query_sum + shifted(piece, "y", -step).astype(F32)
    blocks = key_value_grads.reshape(heads, 2, 2, tokens, 128)
    from_core = swapped(blocks[:, :, 1], "c").astype(F32)
    kept = blocks[:, :, 0].astype(F32) + from_core
    key_value_sum = kept[:, 0] + swapped(kept[:, 1].astype(BF16), "zl").astype(F32)
    hidden = jnp.concatenate(
        [
            query_sum.astype(BF16).T,
            key_value_sum.astype(BF16).transpose(1, 0, 2).reshape(tokens, 2 * group),
        ],
        axis=1,
    )

    count = lax.axis_size(ROW)
    here = coarse_rows // count
    grid = hidden.reshape(coarse_columns, count, here, 3 * group)
    grid = lax.dynamic_slice_in_dim(
        jnp.concatenate([grid, grid], axis=1), lax.axis_index(ROW), count, axis=1
    )
    grid = grid.transpose(1, 0, 2, 3).reshape(tokens, 3 * group)
    partial = nn(grid, joint_weight).astype(BF16).reshape(count, tokens // count, wide)
    merged = partial[0].astype(F32)
    for step in range(1, count):
        merged = merged + shifted(partial[step], ROW, step).astype(F32)
    out_grads = (
        merged.astype(BF16)
        .reshape(coarse_columns, here, 2, 2, width)
        .transpose(1, 2, 0, 3, 4)
        .reshape(rows, columns, width)
    )

    ext_up = with_rim(out_grads, 0)
    grad_query = fine_query_grads(
        own_query, extended[1], extended[2], out_grads.reshape(own, width), own_out, bias
    )
    grad_key, grad_value = fine_key_grads(
        own_key, own_value, extended[0], ext_up, ext_out, bias_t
    )
    shape = (rows, columns, width)
    return grad_query.reshape(shape), grad_key.reshape(shape), grad_value.reshape(shape)


def solution(mesh):
    split = Mesh(mesh.devices.reshape(4, 2, 2, 4, 2), ROW + COL)
    return jax.shard_map(
        shards,
        mesh=split,
        in_specs=(
            P(None, ROW, COL, None),
            P(None, COL, None, ROW),
            P(COL, None, ROW),
            P(),
            P(None, None, ROW),
        ),
        out_specs=(P(ROW, COL, None), P(ROW, COL, None), P(ROW, COL, None)),
        check_vma=False,
    )
```

```python
import jax
import jax.numpy as jnp
from jax import lax
from jax.experimental import pallas as pl
from jax.experimental.pallas import tpu as pltpu
from jax.sharding import Mesh
from jax.sharding import PartitionSpec as P

HD = 64
RADIUS = 7
SCALE = 0.125
SIDE = 32
RIM = 8
HIDDEN = -1e30
ROW = ("x", "zh")
COL = ("zl", "y", "c")
F32 = jnp.float32
BF16 = jnp.bfloat16
VMEM = 60 << 20


def nt(left, right):
    return lax.dot_general(left, right, (((1,), (1,)), ((), ())), preferred_element_type=F32)


def nn(left, right):
    return lax.dot_general(left, right, (((1,), (0,)), ((), ())), preferred_element_type=F32)


def half(pair, which):
    lane = lax.broadcasted_iota(jnp.int32, pair.shape, 1)
    return jnp.where((lane < HD) == (which == 0), pair, jnp.zeros_like(pair))


def cost(flops, bytes_accessed, exps):
    return pl.CostEstimate(flops=flops, bytes_accessed=bytes_accessed, transcendentals=exps)


def coarse_stats(key_value, query_up, query_tile, key_tile, unroll):
    heads, keys, _ = key_value.shape
    queries = query_up.shape[1]

    def body(kv_ref, qu_ref, out_ref):
        query = half(qu_ref[0], 0) * BF16(SCALE)
        upstream = half(qu_ref[0], 1)

        def step(i, carry):
            peak, total, weighted = carry
            tile = kv_ref[0, pl.ds(pl.multiple_of(i * key_tile, key_tile), key_tile), :]
            score = nt(tile, query)
            product = nt(tile, upstream)
            new_peak = jnp.maximum(peak, jnp.max(score, axis=0, keepdims=True))
            decay = jnp.exp(peak - new_peak)
            share = jnp.exp(score - new_peak)
            return (
                new_peak,
                total * decay + jnp.sum(share, axis=0, keepdims=True),
                weighted * decay + jnp.sum(share * product, axis=0, keepdims=True),
            )

        zero = jnp.zeros((1, query_tile), F32)
        peak, total, weighted = lax.fori_loop(
            0, keys // key_tile, step, (zero - jnp.inf, zero, zero), unroll=unroll
        )
        out_ref[0] = jnp.concatenate([peak + jnp.log(total), weighted / total], axis=0)

    return pl.pallas_call(
        body,
        grid=(heads, queries // query_tile),
        in_specs=[
            pl.BlockSpec((1, keys, 128), lambda h, q: (h, 0, 0)),
            pl.BlockSpec((1, query_tile, 128), lambda h, q: (h, q, 0)),
        ],
        out_specs=pl.BlockSpec((1, 2, query_tile), lambda h, q: (h, 0, q)),
        out_shape=jax.ShapeDtypeStruct((heads, 2, queries), F32),
        name="coarse_stats",
        cost_estimate=cost(4 * heads * keys * queries * 256, 2 << 20, heads * keys * queries),
        compiler_params=pltpu.CompilerParams(vmem_limit_bytes=VMEM),
    )(key_value, query_up)


def coarse_grads(key_value, query_up, stats, query_tile, key_tile, unroll):
    heads, keys, _ = key_value.shape
    queries = query_up.shape[1]
    tiles = queries // query_tile

    def body(kv_ref, qu_ref, stats_ref, kv_out, q_out, acc):
        @pl.when(pl.program_id(1) == 0)
        def _():
            acc[...] = jnp.zeros_like(acc)

        query = half(qu_ref[0], 0) * BF16(SCALE)
        upstream = half(qu_ref[0], 1)
        log_total = stats_ref[0, 0:1, :]
        delta = stats_ref[0, 1:2, :]

        def step(i, carry):
            rows = pl.ds(pl.multiple_of(i * key_tile, key_tile), key_tile)
            tile = kv_ref[0, rows, :]
            share = jnp.exp(nt(tile, query) - log_total)
            grads = (share * (nt(tile, upstream) - delta)).astype(BF16)
            acc[rows, :] += nn(grads, query) + nn(share.astype(BF16), upstream)
            return carry + nn(tile[:, :HD].T, grads)

        found = lax.fori_loop(
            0, keys // key_tile, step, jnp.zeros((HD, query_tile), F32), unroll=unroll
        )
        q_out[...] = (found * SCALE).astype(BF16)

        @pl.when(pl.program_id(1) == tiles - 1)
        def _():
            kv_out[0] = acc[...].astype(BF16)

    return pl.pallas_call(
        body,
        grid=(heads, tiles),
        in_specs=[
            pl.BlockSpec((1, keys, 128), lambda h, q: (h, 0, 0)),
            pl.BlockSpec((1, query_tile, 128), lambda h, q: (h, q, 0)),
            pl.BlockSpec((1, 2, query_tile), lambda h, q: (h, 0, q)),
        ],
        out_specs=[
            pl.BlockSpec((1, keys, 128), lambda h, q: (h, 0, 0)),
            pl.BlockSpec((HD, query_tile), lambda h, q: (h, q)),
        ],
        out_shape=[
            jax.ShapeDtypeStruct((heads, keys, 128), BF16),
            jax.ShapeDtypeStruct((heads * HD, queries), BF16),
        ],
        scratch_shapes=[pltpu.VMEM((keys, 128), F32)],
        name="coarse_grads",
        cost_estimate=cost(10 * heads * keys * queries * 256, 4 << 20, heads * keys * queries),
        compiler_params=pltpu.CompilerParams(vmem_limit_bytes=VMEM),
    )(key_value, query_up, stats)


def whole_call(body, out_shape, name, flops, scratch, *operands):
    return pl.pallas_call(
        body,
        out_shape=out_shape,
        scratch_shapes=scratch,
        name=name,
        cost_estimate=cost(flops, 6 << 20, 1 << 20),
        compiler_params=pltpu.CompilerParams(vmem_limit_bytes=VMEM),
    )(*operands)


def pairs_of(width):
    return [(pair, slice(pair * 128, pair * 128 + 128)) for pair in range(width // 128)]


def window_bias(own, rows, columns, transposed):
    shape = (own, SIDE * SIDE) if transposed else (SIDE * SIDE, own)
    ext = lax.broadcasted_iota(jnp.int32, shape, 1 if transposed else 0)
    inner = lax.broadcasted_iota(jnp.int32, shape, 0 if transposed else 1)
    ext_row, ext_column = ext // SIDE, ext % SIDE
    row_gap = ext_row - inner // columns - RIM
    column_gap = ext_column - inner % columns - RIM
    row = ext_row + (lax.axis_index(ROW) * rows - RIM)
    column = ext_column + (lax.axis_index(COL) * columns - RIM)
    seen = (jnp.abs(row_gap) <= RADIUS) & (jnp.abs(column_gap) <= RADIUS)
    seen &= (row >= 0) & (row < lax.axis_size(ROW) * rows)
    seen &= (column >= 0) & (column < lax.axis_size(COL) * columns)
    return jnp.where(seen, 0.0, HIDDEN).astype(F32)


def fine_forward(own_query, ext_key, ext_value, rows, columns):
    own, width = own_query.shape

    def body(q_ref, k_ref, v_ref, out_ref, bias_ref):
        bias_ref[...] = window_bias(own, rows, columns, False)
        logs = []
        for _, lanes in pairs_of(width):
            key = k_ref[:, lanes]
            value_t = v_ref[:, lanes].T
            parts = []
            for side in range(2):
                query = half(q_ref[:, lanes], side) * BF16(SCALE)
                score = nt(key, query) + bias_ref[...]
                peak = jnp.max(score, axis=0, keepdims=True)
                share = jnp.exp(score - peak)
                logs.append(peak + jnp.log(jnp.sum(share, axis=0, keepdims=True)))
                rounded = share.astype(BF16)
                total = jnp.sum(rounded.astype(F32), axis=0, keepdims=True)
                parts.append(nn(value_t[side * HD : side * HD + HD], rounded) / total)
            out_ref[:, lanes] = jnp.concatenate(parts, axis=0).T
        logs.append(jnp.zeros((128 - len(logs), own), F32))
        out_ref[:, width:] = jnp.concatenate(logs, axis=0).T

    return whole_call(
        body,
        jax.ShapeDtypeStruct((own, width + 128), F32),
        "fine_forward",
        2 << 30,
        [pltpu.VMEM((SIDE * SIDE, own), F32)],
        own_query,
        ext_key,
        ext_value,
    )


def head_sums(up, out):
    width = up.shape[1]
    head = lax.broadcasted_iota(jnp.int32, (8, width), 0)
    lane = lax.broadcasted_iota(jnp.int32, (8, width), 1)
    pick = jnp.where(lane // HD == head, 1.0, 0.0).astype(F32)
    return lax.dot_general(
        pick,
        up * out,
        (((1,), (1,)), ((), ())),
        preferred_element_type=F32,
        precision=lax.Precision.HIGHEST,
    )


def fine_query_grads(own_query, ext_key, ext_value, row_up, own_out, rows, columns):
    own, width = own_query.shape
    above = RIM * columns

    def body(q_ref, k_ref, v_ref, up_ref, o_ref, out_ref, bias_ref):
        bias_ref[...] = window_bias(own, rows, columns, False)
        whole_up = up_ref[above : above + own, :]
        delta = head_sums(whole_up.astype(F32), o_ref[:, :width])
        logs = o_ref[:, width:].T
        for pair, lanes in pairs_of(width):
            key = k_ref[:, lanes]
            key_t = key.T
            value = v_ref[:, lanes]
            parts = []
            for side in range(2):
                head = 2 * pair + side
                query = half(q_ref[:, lanes], side) * BF16(SCALE)
                up = half(whole_up[:, lanes], side)
                share = jnp.exp(nt(key, query) + bias_ref[...] - logs[head : head + 1])
                grads = (share * (nt(value, up) - delta[head : head + 1])).astype(BF16)
                parts.append(nn(key_t[side * HD : side * HD + HD], grads))
            out_ref[:, lanes] = (jnp.concatenate(parts, axis=0).T * SCALE).astype(BF16)

    return whole_call(
        body,
        jax.ShapeDtypeStruct((own, width), BF16),
        "fine_query_grads",
        2 << 30,
        [pltpu.VMEM((SIDE * SIDE, own), F32)],
        own_query,
        ext_key,
        ext_value,
        row_up,
        own_out,
    )


def fine_key_grads(own_key, own_value, ext_query, low_up, row_up, high_up, ext_out, rows, columns):
    own, width = own_key.shape

    def body(k_ref, v_ref, q_ref, low_ref, mid_ref, high_ref, o_ref, k_out, v_out, bias_ref, wide, ups):
        bias_ref[...] = window_bias(own, rows, columns, True)
        wide[:, :RIM] = low_ref[...].astype(F32)
        wide[:, RIM : RIM + columns] = mid_ref[...].astype(F32).reshape(SIDE, columns, width)
        wide[:, RIM + columns :] = high_ref[...].astype(F32)
        full = wide[...].reshape(SIDE * SIDE, width)
        ups[...] = full.astype(BF16)
        delta = head_sums(full, o_ref[:, :width])
        logs = o_ref[:, width:].T
        for pair, lanes in pairs_of(width):
            key = k_ref[:, lanes]
            value = v_ref[:, lanes]
            key_sum = jnp.zeros((own, 128), F32)
            value_sum = jnp.zeros((own, 128), F32)
            for side in range(2):
                head = 2 * pair + side
                query = half(q_ref[:, lanes], side) * BF16(SCALE)
                up = half(ups[:, lanes], side)
                share = jnp.exp(nt(key, query) + bias_ref[...] - logs[head : head + 1])
                grads = (share * (nt(value, up) - delta[head : head + 1])).astype(BF16)
                key_sum += nn(grads, query)
                value_sum += nn(share.astype(BF16), up)
            k_out[:, lanes] = key_sum.astype(BF16)
            v_out[:, lanes] = value_sum.astype(BF16)

    return whole_call(
        body,
        [jax.ShapeDtypeStruct((own, width), BF16)] * 2,
        "fine_key_grads",
        3 << 30,
        [
            pltpu.VMEM((own, SIDE * SIDE), F32),
            pltpu.VMEM((SIDE, SIDE, width), F32),
            pltpu.VMEM((SIDE * SIDE, width), BF16),
        ],
        own_key,
        own_value,
        ext_query,
        low_up,
        row_up,
        high_up,
        ext_out,
    )


def row_moves():
    columns, halves = lax.axis_size("x"), lax.axis_size("zh")
    return [(step, flip) for step in range(columns) for flip in range(halves)]


def row_target(index, step, flip):
    halves = lax.axis_size("zh")
    x = (index // halves + step) % lax.axis_size("x")
    return x * halves + (index + flip) % halves


def pack(query_pieces, kept, arrived, rows_each, columns):
    group, tokens = query_pieces[0].shape
    heads = kept.shape[0]
    moves = row_moves()
    over = RIM // 2 * columns
    size = rows_each * columns
    width = 3 * group

    def body(*refs):
        pieces = refs[: len(query_pieces)]
        kept_ref, arrived_ref = refs[len(query_pieces) : len(query_pieces) + 2]
        outs = refs[len(query_pieces) + 2 : -1]
        held = refs[-1]
        held[:over] = jnp.zeros((over, width), BF16)
        held[over + tokens :] = jnp.zeros((over, width), BF16)
        for head in range(heads):
            total = kept_ref[head] + arrived_ref[head].astype(F32)
            held[over : over + tokens, head * 128 : head * 128 + 128] = total.astype(BF16)
        total = pieces[0][...].astype(F32)
        for piece in pieces[1:]:
            total += piece[...].astype(F32)
        held[over : over + tokens, 2 * group :] = total.T.astype(BF16)
        here = lax.axis_index(ROW)
        for out, (step, flip) in zip(outs, moves):
            start = pl.multiple_of(row_target(here, step, flip) * size, size)
            out[...] = held[pl.ds(start, size + 2 * over), :]

    return whole_call(
        body,
        [jax.ShapeDtypeStruct((size + 2 * over, width), BF16)] * len(moves),
        "pack",
        1 << 20,
        [pltpu.VMEM((tokens + 2 * over, width), BF16)],
        *query_pieces,
        kept,
        arrived,
    )


def merge(pieces, own_weights, other_weights, columns):
    tokens, depth = pieces[0].shape
    wide = own_weights[0].shape[-1]
    width = wide // 2
    count = len(pieces)
    pairs = len(own_weights)
    each = count // pairs
    ext = 2 * tokens // columns

    def body(*refs):
        xs = refs[:count]
        weights = refs[count : count + 2 * pairs]
        out, held, sems = refs[count + 2 * pairs :]
        copies = []
        for at in range(pairs):
            for side in range(2):
                copies.append(
                    pltpu.make_async_copy(
                        weights[side * pairs + at], held.at[side, at], sems.at[side, at]
                    )
                )
                copies[-1].start()
        sums = [jnp.zeros((tokens, wide), F32) for _ in range(2)]
        for at in range(pairs):
            for side in range(2):
                copies[2 * at + side].wait()
                for part in range(each):
                    sums[side] += nn(xs[at * each + part][...], held[side, at, part])
        first = lax.axis_index("c") == 0
        own = sums[0].astype(BF16)
        other = sums[1].astype(BF16)
        cells = 2 * tokens
        fine = lax.broadcasted_iota(jnp.int32, (cells, tokens), 0)
        token = lax.broadcasted_iota(jnp.int32, (cells, tokens), 1)
        for parity in range(2):
            chosen = jnp.where(first == (parity == 0), own, other)
            spread = jnp.zeros((cells, width), F32)
            for b in range(2):
                place = jnp.where(fine == 2 * token + b, 1.0, 0.0).astype(BF16)
                spread += nn(place, chosen[:, b * width : (b + 1) * width])
            spread = spread.astype(BF16)
            for row in range(tokens // columns):
                at = (2 * row + parity) * 2 * columns
                out[at : at + 2 * columns, :] = spread[
                    row * 2 * columns : (row + 1) * 2 * columns, :
                ]

    return pl.pallas_call(
        body,
        in_specs=[pl.BlockSpec(memory_space=pltpu.VMEM)] * count
        + [pl.BlockSpec(memory_space=pl.ANY)] * (2 * pairs),
        out_specs=pl.BlockSpec(memory_space=pltpu.VMEM),
        out_shape=jax.ShapeDtypeStruct((4 * tokens, width), BF16),
        scratch_shapes=[
            pltpu.VMEM((2, pairs, each, depth, wide), BF16),
            pltpu.SemaphoreType.DMA((2, pairs)),
        ],
        name="merge",
        cost_estimate=cost(2 << 30, 16 << 20, 0),
        compiler_params=pltpu.CompilerParams(vmem_limit_bytes=VMEM),
    )(*pieces, *own_weights, *other_weights)


def shifted(array, axis, step):
    count = lax.axis_size(axis)
    return lax.ppermute(array, axis, [(i, (i + step) % count) for i in range(count)])


def swapped(array, axis):
    return lax.ppermute(array, axis, [(0, 1), (1, 0)])


def edges(block, axis, at):
    count = lax.axis_size(axis)
    forward = [(i, i + 1) for i in range(count - 1)]
    backward = [(i + 1, i) for i in range(count - 1)]
    size = block.shape[at]
    low = lax.ppermute(lax.slice_in_dim(block, size - RIM, None, axis=at), axis, forward)
    high = lax.ppermute(lax.slice_in_dim(block, 0, RIM, axis=at), axis, backward)
    return low, high


def with_rim(block, dim):
    for axis, at in ((ROW, dim), (COL, dim + 1)):
        low, high = edges(block, axis, at)
        block = jnp.concatenate([low, block, high], axis=at)
    return block.reshape(block.shape[:dim] + (SIDE * SIDE, block.shape[-1]))


def by_head(first, second, heads):
    columns, rows = first.shape[:2]
    joined = jnp.concatenate(
        [
            first.reshape(columns, rows, heads, HD),
            second.reshape(columns, rows, heads, HD),
        ],
        axis=3,
    )
    return joined.transpose(2, 1, 0, 3).reshape(heads, rows * columns, 2 * HD)


def shards(fine_qkv, coarse_qkv, grad_coarse, merge_weight, qkv_weight):
    rows, columns, width = fine_qkv.shape[1:]
    own = rows * columns
    coarse_columns, coarse_rows, group = grad_coarse.shape
    tokens = coarse_columns * coarse_rows
    heads = group // HD
    wide = merge_weight.shape[0]

    key_value = by_head(coarse_qkv[1], coarse_qkv[2], heads)
    query_up = by_head(coarse_qkv[0], grad_coarse, heads)
    across = swapped(key_value, "zl")
    beside = swapped(key_value, "c")
    queries = [query_up] + [shifted(query_up, "y", step) for step in (1, 2, 3)]
    corner = swapped(across, "c")
    all_keys = jnp.concatenate([key_value, beside, across, corner], axis=1)
    all_queries = jnp.concatenate(queries, axis=1)

    weight = qkv_weight.reshape(3, wide, heads, HD)
    weight = jnp.concatenate(
        [
            jnp.concatenate([weight[1], weight[2]], axis=2).reshape(wide, 2 * group),
            weight[0].reshape(wide, group),
        ],
        axis=1,
    )
    half_weight = lax.dynamic_slice_in_dim(
        merge_weight, lax.axis_index("c") * (wide // 2), wide // 2, axis=0
    )
    joint = lax.dot_general(
        weight, half_weight, (((0,), (1,)), ((), ())), preferred_element_type=F32
    ).astype(BF16)
    far = lax.ppermute(joint, ("zh", "zl"), [(0, 3), (3, 0), (1, 2), (2, 1)])
    joint = jnp.stack([joint, far])
    own_weights = [joint] + [shifted(joint, "x", step) for step in (1, 2, 3)]
    other_weights = [swapped(piece, "c") for piece in own_weights]

    extended = with_rim(fine_qkv, 1)
    own_query = fine_qkv[0].reshape(own, width)
    own_key = fine_qkv[1].reshape(own, width)
    own_value = fine_qkv[2].reshape(own, width)

    part = coarse_stats(all_keys, all_queries, 512, 256, 4).reshape(2 * heads, 4, tokens)
    parts = [part] + [jnp.roll(shifted(part, "y", step), step, axis=1) for step in (1, 2, 3)]
    own_out = fine_forward(own_query, extended[1], extended[2], rows, columns)
    stacked = jnp.stack(parts).reshape(4, heads, 2, 4 * tokens)
    logs, deltas = stacked[:, :, 0], stacked[:, :, 1]
    peak = jnp.max(logs, axis=0)
    shares = jnp.exp(logs - peak)
    total = jnp.sum(shares, axis=0)
    stats = jnp.stack([peak + jnp.log(total), jnp.sum(shares * deltas, axis=0) / total], axis=1)
    stats, own_out = lax.optimization_barrier((stats, own_out))
    ext_out = with_rim(own_out.reshape(rows, columns, width + 128), 0)

    key_value_grads, query_grads = coarse_grads(all_keys, all_queries, stats, 512, 512, 4)
    blocks = key_value_grads.reshape(heads, 2, 2, tokens, 128)
    kept = blocks[:, :, 0].astype(F32) + swapped(blocks[:, :, 1], "c").astype(F32)
    query_pieces = [query_grads[:, :tokens]]
    for step in (1, 2, 3):
        piece = query_grads[:, step * tokens : (step + 1) * tokens]
        query_pieces.append(shifted(piece, "y", -step))
    arrived = swapped(kept[:, 1].astype(BF16), "zl")
    here = coarse_rows // lax.axis_size(ROW)
    packed = pack(query_pieces, kept[:, 0], arrived, here, coarse_columns)

    pieces = []
    for piece, (step, flip) in zip(packed, row_moves()):
        if (step, flip) != (0, 0):
            pairs = [(i, row_target(i, step, flip)) for i in range(lax.axis_size(ROW))]
            piece = lax.ppermute(piece, ROW, pairs)
        pieces.append(piece)
    row_up = merge(pieces, own_weights, other_weights, coarse_columns)

    low_up, high_up = edges(row_up.reshape(SIDE, columns, width), COL, 1)
    grad_query = fine_query_grads(
        own_query, extended[1], extended[2], row_up, own_out, rows, columns
    )
    grad_key, grad_value = fine_key_grads(
        own_key, own_value, extended[0], low_up, row_up, high_up, ext_out, rows, columns
    )
    shape = (rows, columns, width)
    return grad_query.reshape(shape), grad_key.reshape(shape), grad_value.reshape(shape)


def solution(mesh):
    split = Mesh(mesh.devices.reshape(4, 2, 2, 4, 2), ROW + COL)
    return jax.shard_map(
        shards,
        mesh=split,
        in_specs=(
            P(None, ROW, COL, None),
            P(None, COL, None, ROW),
            P(COL, None, ROW),
            P(),
            P(None, None, ROW),
        ),
        out_specs=(P(ROW, COL, None), P(ROW, COL, None), P(ROW, COL, None)),
        check_vma=False,
    )
```

```python
import jax
import jax.numpy as jnp
from jax import lax
from jax.experimental import pallas as pl
from jax.experimental.pallas import tpu as pltpu
from jax.sharding import Mesh
from jax.sharding import PartitionSpec as P

HD = 64
RADIUS = 7
SCALE = 0.125
SIDE = 32
RIM = 8
HIDDEN = -1e30
ROW = ("x", "zh")
COL = ("zl", "y", "c")
F32 = jnp.float32
BF16 = jnp.bfloat16
VMEM = 60 << 20


def nt(left, right):
    return lax.dot_general(left, right, (((1,), (1,)), ((), ())), preferred_element_type=F32)


def nn(left, right):
    return lax.dot_general(left, right, (((1,), (0,)), ((), ())), preferred_element_type=F32)


def half(pair, which):
    lane = lax.broadcasted_iota(jnp.int32, pair.shape, 1)
    return jnp.where((lane < HD) == (which == 0), pair, jnp.zeros_like(pair))


def cost(flops, bytes_accessed, exps):
    return pl.CostEstimate(flops=flops, bytes_accessed=bytes_accessed, transcendentals=exps)


def coarse_stats(key_values, query_ups, first, count, key_tile):
    tokens = key_values[0].shape[1]
    blocks = len(query_ups)
    per_block = tokens // key_tile

    def body(*refs):
        kv_refs, qu_refs = refs[:blocks], refs[blocks : 2 * blocks]
        out_ref, held = refs[2 * blocks :]
        for at in range(blocks):

            @pl.when(pl.program_id(1) == at)
            def _():
                held[...] = qu_refs[at][0]

        query = half(held[...], 0) * BF16(SCALE)
        upstream = half(held[...], 1)
        peak = jnp.full((1, tokens), -jnp.inf, F32)
        total = jnp.zeros((1, tokens), F32)
        weighted = jnp.zeros((1, tokens), F32)
        for i in range(blocks * per_block):
            start = (i % per_block) * key_tile
            tile = kv_refs[i // per_block][0, start : start + key_tile, :]
            score = nt(tile, query)
            product = nt(tile, upstream)
            new_peak = jnp.maximum(peak, jnp.max(score, axis=0, keepdims=True))
            decay = jnp.exp(peak - new_peak)
            share = jnp.exp(score - new_peak)
            total = total * decay + jnp.sum(share, axis=0, keepdims=True)
            weighted = weighted * decay + jnp.sum(share * product, axis=0, keepdims=True)
            peak = new_peak
        out_ref[0] = jnp.concatenate([peak + jnp.log(total), weighted / total], axis=0)

    pairs = count * (blocks * tokens) ** 2
    return pl.pallas_call(
        body,
        grid=(count, blocks),
        in_specs=[pl.BlockSpec((1, tokens, 128), lambda h, q: (h + first, 0, 0))] * (2 * blocks),
        out_specs=pl.BlockSpec((1, 2, tokens), lambda h, q: (h, 0, q)),
        out_shape=jax.ShapeDtypeStruct((count, 2, blocks * tokens), F32),
        scratch_shapes=[pltpu.VMEM((tokens, 128), BF16)],
        name="coarse_stats",
        cost_estimate=cost(4 * pairs * 256, 2 << 20, pairs),
        compiler_params=pltpu.CompilerParams(vmem_limit_bytes=VMEM),
    )(*key_values, *query_ups)


def coarse_grads(key_values, query_ups, stats, first, count, before):
    heads, tokens, _ = key_values[0].shape
    blocks = len(query_ups)
    given = 2 * blocks + 1

    def body(*refs):
        kv_refs, qu_refs = refs[:blocks], refs[blocks : 2 * blocks]
        stats_ref = refs[2 * blocks]
        kept_ref, sent_ref = refs[-blocks - 4 : -blocks - 2]
        q_outs = refs[-blocks - 2 : -2]
        acc, held = refs[-2:]
        for at in range(blocks):

            @pl.when(pl.program_id(1) == at)
            def _():
                held[...] = qu_refs[at][0]

        @pl.when(pl.program_id(1) == 0)
        def _():
            acc[...] = jnp.zeros_like(acc)

        query = half(held[...], 0) * BF16(SCALE)
        upstream = half(held[...], 1)
        log_total = stats_ref[0, 0:1, :]
        delta = stats_ref[0, 1:2, :]
        found = jnp.zeros((HD, tokens), F32)
        for i in range(blocks):
            tile = kv_refs[i][0]
            share = jnp.exp(nt(tile, query) - log_total)
            grads = (share * (nt(tile, upstream) - delta)).astype(BF16)
            acc[i] += nn(grads, query) + nn(share.astype(BF16), upstream)
            found += nn(tile[:, :HD].T, grads)
        found = (found * SCALE).astype(BF16)
        for at in range(blocks):

            @pl.when(pl.program_id(1) == at)
            def _():
                q_outs[at][...] = found

        @pl.when(pl.program_id(1) == blocks - 1)
        def _():
            for i in range(blocks // 2):
                kept_ref[0, i] = acc[2 * i].astype(BF16)
                sent_ref[0, i] = acc[2 * i + 1].astype(BF16)

    pairs = count * (blocks * tokens) ** 2
    out_shape = [jax.ShapeDtypeStruct((heads, blocks // 2, tokens, 128), BF16)] * 2
    out_shape += [jax.ShapeDtypeStruct((heads * HD, tokens), BF16)] * blocks
    return pl.pallas_call(
        body,
        grid=(count, blocks),
        in_specs=[pl.BlockSpec((1, tokens, 128), lambda h, q: (h + first, 0, 0))] * (2 * blocks)
        + [pl.BlockSpec((1, 2, tokens), lambda h, q: (h, 0, q))]
        + [pl.BlockSpec(memory_space=pl.ANY)] * len(before),
        out_specs=[
            pl.BlockSpec((1, blocks // 2, tokens, 128), lambda h, q: (h + first, 0, 0, 0))
        ]
        * 2
        + [pl.BlockSpec((HD, tokens), lambda h, q: (h + first, 0))] * blocks,
        out_shape=out_shape,
        scratch_shapes=[
            pltpu.VMEM((blocks, tokens, 128), F32),
            pltpu.VMEM((tokens, 128), BF16),
        ],
        input_output_aliases={given + i: i for i in range(len(before))},
        name="coarse_grads",
        cost_estimate=cost(10 * pairs * 256, 4 << 20, pairs),
        compiler_params=pltpu.CompilerParams(vmem_limit_bytes=VMEM),
    )(*key_values, *query_ups, stats, *before)


def whole_call(body, out_shape, name, flops, scratch, *operands):
    return pl.pallas_call(
        body,
        out_shape=out_shape,
        scratch_shapes=scratch,
        name=name,
        cost_estimate=cost(flops, 6 << 20, 1 << 20),
        compiler_params=pltpu.CompilerParams(vmem_limit_bytes=VMEM),
    )(*operands)


def pairs_of(width):
    return [(pair, slice(pair * 128, pair * 128 + 128)) for pair in range(width // 128)]


def window_bias(own, rows, columns, part, transposed):
    count = SIDE * SIDE // 2
    shape = (own, count) if transposed else (count, own)
    ext = lax.broadcasted_iota(jnp.int32, shape, 1 if transposed else 0)
    inner = lax.broadcasted_iota(jnp.int32, shape, 0 if transposed else 1)
    if part == 0:
        ext_row, ext_column = ext >> 4, (ext & 15) + RIM
    else:
        ext_row = (ext & 255) >> 3
        ext_column = (ext & 7) + jnp.where(ext >= 256, SIDE - RIM, 0)
    row_gap = ext_row - (inner >> 4) - RIM
    column_gap = ext_column - (inner & 15) - RIM
    row = ext_row + (lax.axis_index(ROW) * rows - RIM)
    column = ext_column + (lax.axis_index(COL) * columns - RIM)
    seen = (jnp.abs(row_gap) <= RADIUS) & (jnp.abs(column_gap) <= RADIUS)
    seen &= (row >= 0) & (row < lax.axis_size(ROW) * rows)
    seen &= (column >= 0) & (column < lax.axis_size(COL) * columns)
    return jnp.where(seen, 0.0, HIDDEN).astype(F32)


def fill_bias(bias_ref, own, rows, columns):
    count = SIDE * SIDE // 2
    for part in range(2):
        bias_ref[part * count : (part + 1) * count, :] = window_bias(
            own, rows, columns, part, False
        )


def stacked(refs, which, lanes):
    return jnp.concatenate([ref[which, :, lanes] for ref in refs], axis=0)


def fine_forward(own_qkv, ext_qkv, rows, columns):
    _, own, width = own_qkv.shape

    def body(q_ref, mid_ref, low_ref, high_ref, out_ref, bias_ref):
        fill_bias(bias_ref, own, rows, columns)
        ext = (mid_ref, low_ref, high_ref)
        logs = []
        for _, lanes in pairs_of(width):
            key = stacked(ext, 1, lanes)
            value_t = stacked(ext, 2, lanes).T
            parts = []
            for side in range(2):
                query = half(q_ref[0, :, lanes], side) * BF16(SCALE)
                score = nt(key, query) + bias_ref[...]
                peak = jnp.max(score, axis=0, keepdims=True)
                share = jnp.exp(score - peak)
                logs.append(peak + jnp.log(jnp.sum(share, axis=0, keepdims=True)))
                rounded = share.astype(BF16)
                total = jnp.sum(rounded.astype(F32), axis=0, keepdims=True)
                parts.append(nn(value_t[side * HD : side * HD + HD], rounded) / total)
            out_ref[:, lanes] = jnp.concatenate(parts, axis=0).T
        logs.append(jnp.zeros((128 - len(logs), own), F32))
        out_ref[:, width:] = jnp.concatenate(logs, axis=0).T

    return whole_call(
        body,
        jax.ShapeDtypeStruct((own, width + 128), F32),
        "fine_forward",
        2 << 30,
        [pltpu.VMEM((SIDE * SIDE, own), F32)],
        own_qkv,
        *ext_qkv,
    )


def head_sums(up, out):
    width = up.shape[1]
    head = lax.broadcasted_iota(jnp.int32, (8, width), 0)
    lane = lax.broadcasted_iota(jnp.int32, (8, width), 1)
    pick = jnp.where(lane // HD == head, 1.0, 0.0).astype(F32)
    return lax.dot_general(
        pick,
        up * out,
        (((1,), (1,)), ((), ())),
        preferred_element_type=F32,
        precision=lax.Precision.HIGHEST,
    )


def fine_query_grads(own_qkv, ext_qkv, own_up, own_out, rows, columns):
    _, own, width = own_qkv.shape

    def body(q_ref, mid_ref, low_ref, high_ref, up_ref, o_ref, out_ref, bias_ref):
        fill_bias(bias_ref, own, rows, columns)
        ext = (mid_ref, low_ref, high_ref)
        delta = head_sums(up_ref[...].astype(F32), o_ref[:, :width])
        logs = o_ref[:, width:].T
        for pair, lanes in pairs_of(width):
            key = stacked(ext, 1, lanes)
            key_t = key.T
            value = stacked(ext, 2, lanes)
            parts = []
            for side in range(2):
                head = 2 * pair + side
                query = half(q_ref[0, :, lanes], side) * BF16(SCALE)
                up = half(up_ref[:, lanes], side)
                share = jnp.exp(nt(key, query) + bias_ref[...] - logs[head : head + 1])
                grads = (share * (nt(value, up) - delta[head : head + 1])).astype(BF16)
                parts.append(nn(key_t[side * HD : side * HD + HD], grads))
            out_ref[:, lanes] = (jnp.concatenate(parts, axis=0).T * SCALE).astype(BF16)

    return whole_call(
        body,
        jax.ShapeDtypeStruct((own, width), BF16),
        "fine_query_grads",
        2 << 30,
        [pltpu.VMEM((SIDE * SIDE, own), F32)],
        own_qkv,
        *ext_qkv,
        own_up,
        own_out,
    )


def fine_key_grads(own_qkv, queries, ups, outs, sums, part, rows, columns):
    _, own, width = own_qkv.shape
    count = SIDE * SIDE // 2
    number = len(queries)

    def body(*refs):
        kv_ref = refs[0]
        q_refs = refs[1 : 1 + number]
        up_refs = refs[1 + number : 1 + 2 * number]
        o_refs = refs[1 + 2 * number : 1 + 3 * number]
        sum_refs = refs[1 + 3 * number : -3]
        k_out, v_out, bias_ref = refs[-3:]
        bias_ref[...] = window_bias(own, rows, columns, part, True)
        up_all = jnp.concatenate([ref[...] for ref in up_refs], axis=0)
        out_all = jnp.concatenate([ref[...] for ref in o_refs], axis=0)
        delta = head_sums(up_all.astype(F32), out_all[:, :width])
        logs = out_all[:, width:].T
        for pair, lanes in pairs_of(width):
            key = kv_ref[1, :, lanes]
            value = kv_ref[2, :, lanes]
            if sums:
                key_sum, value_sum = sum_refs[0][:, lanes], sum_refs[1][:, lanes]
            else:
                key_sum = jnp.zeros((own, 128), F32)
                value_sum = jnp.zeros((own, 128), F32)
            for side in range(2):
                head = 2 * pair + side
                query = half(stacked(q_refs, 0, lanes), side) * BF16(SCALE)
                up = half(up_all[:, lanes], side)
                share = jnp.exp(nt(key, query) + bias_ref[...] - logs[head : head + 1])
                grads = (share * (nt(value, up) - delta[head : head + 1])).astype(BF16)
                key_sum += nn(grads, query)
                value_sum += nn(share.astype(BF16), up)
            k_out[:, lanes] = key_sum.astype(k_out.dtype)
            v_out[:, lanes] = value_sum.astype(v_out.dtype)

    return whole_call(
        body,
        [jax.ShapeDtypeStruct((own, width), BF16 if sums else F32)] * 2,
        "fine_key_grads",
        2 << 30,
        [pltpu.VMEM((own, count), F32)],
        own_qkv,
        *queries,
        *ups,
        *outs,
        *sums,
    )


def row_moves():
    columns, halves = lax.axis_size("x"), lax.axis_size("zh")
    return [(step, flip) for step in range(columns) for flip in range(halves)]


def row_target(index, step, flip):
    halves = lax.axis_size("zh")
    x = (index // halves + step) % lax.axis_size("x")
    return x * halves + (index + flip) % halves


def project(query_pieces, kept, from_core, arrived, joint_weight):
    group, tokens = query_pieces[0].shape
    heads = kept.shape[0]
    moves = row_moves()
    size = tokens // len(moves)
    wide = joint_weight.shape[1]

    def body(*refs):
        pieces = refs[: len(query_pieces)]
        kept_ref, core_ref, arrived_ref, weight_ref = refs[len(query_pieces) : -len(moves) - 1]
        outs = refs[-len(moves) - 1 : -1]
        held = refs[-1]
        for head in range(heads):
            total = kept_ref[head, 0].astype(F32) + core_ref[head, 0].astype(F32)
            total += arrived_ref[head].astype(F32)
            held[:, head * 128 : head * 128 + 128] = total.astype(BF16)
        total = pieces[0][...].astype(F32)
        for piece in pieces[1:]:
            total += piece[...].astype(F32)
        held[:, 2 * group :] = total.T.astype(BF16)
        here = lax.axis_index(ROW)
        for out, (step, flip) in zip(outs, moves):
            start = pl.multiple_of(row_target(here, step, flip) * size, size)
            out[...] = nn(held[pl.ds(start, size), :], weight_ref[...]).astype(BF16)

    return whole_call(
        body,
        [jax.ShapeDtypeStruct((size, wide), BF16)] * len(moves),
        "project",
        2 << 30,
        [pltpu.VMEM((tokens, 3 * group), BF16)],
        *query_pieces,
        kept,
        from_core,
        arrived,
        joint_weight,
    )


def spread(pieces, columns):
    tokens, wide = pieces[0].shape
    width = wide // 4

    def body(*refs):
        out = refs[-1]
        total = refs[0][...].astype(F32)
        for ref in refs[1:-1]:
            total += ref[...].astype(F32)
        total = total.astype(BF16)
        cells = 2 * tokens
        fine = lax.broadcasted_iota(jnp.int32, (cells, tokens), 0)
        token = lax.broadcasted_iota(jnp.int32, (cells, tokens), 1)
        for a in range(2):
            grid = jnp.zeros((cells, width), F32)
            for b in range(2):
                place = jnp.where(fine == 2 * token + b, 1.0, 0.0).astype(BF16)
                lanes = slice((2 * a + b) * width, (2 * a + b + 1) * width)
                grid += nn(place, total[:, lanes])
            grid = grid.astype(BF16)
            for row in range(tokens // columns):
                at = (2 * row + a) * 2 * columns
                out[at : at + 2 * columns, :] = grid[row * 2 * columns : (row + 1) * 2 * columns]

    return whole_call(
        body,
        jax.ShapeDtypeStruct((4 * tokens, width), BF16),
        "spread",
        1 << 28,
        [],
        *pieces,
    )


def shifted(array, axis, step):
    count = lax.axis_size(axis)
    return lax.ppermute(array, axis, [(i, (i + step) % count) for i in range(count)])


def swapped(array, axis):
    return lax.ppermute(array, axis, [(0, 1), (1, 0)])


def edges(block, axis, at):
    count = lax.axis_size(axis)
    forward = [(i, i + 1) for i in range(count - 1)]
    backward = [(i + 1, i) for i in range(count - 1)]
    size = block.shape[at]
    low = lax.ppermute(lax.slice_in_dim(block, size - RIM, None, axis=at), axis, forward)
    high = lax.ppermute(lax.slice_in_dim(block, 0, RIM, axis=at), axis, backward)
    return low, high


def with_rows(block, dim):
    low, high = edges(block, ROW, dim)
    return jnp.concatenate([low, block, high], axis=dim)


def with_columns(block, dim):
    low, high = edges(block, COL, dim + 1)
    shape = block.shape[:dim] + (-1, block.shape[-1])
    return block.reshape(shape), low.reshape(shape), high.reshape(shape)


def by_head(first, second, heads):
    columns, rows = first.shape[:2]
    joined = jnp.concatenate(
        [
            first.reshape(columns, rows, heads, HD),
            second.reshape(columns, rows, heads, HD),
        ],
        axis=3,
    )
    return joined.transpose(2, 1, 0, 3).reshape(heads, rows * columns, 2 * HD)


def merged_stats(part, heads, tokens):
    part = part.reshape(2 * heads, 4, tokens)
    parts = [part] + [jnp.roll(shifted(part, "y", step), step, axis=1) for step in (1, 2, 3)]
    parts = jnp.stack(parts).reshape(4, heads, 2, 4 * tokens)
    logs, deltas = parts[:, :, 0], parts[:, :, 1]
    peak = jnp.max(logs, axis=0)
    shares = jnp.exp(logs - peak)
    total = jnp.sum(shares, axis=0)
    return jnp.stack([peak + jnp.log(total), jnp.sum(shares * deltas, axis=0) / total], axis=1)


def shards(fine_qkv, coarse_qkv, grad_coarse, merge_weight, qkv_weight):
    rows, columns, width = fine_qkv.shape[1:]
    own = rows * columns
    coarse_columns, coarse_rows, group = grad_coarse.shape
    tokens = coarse_columns * coarse_rows
    heads = group // HD
    wide = merge_weight.shape[0]

    key_value = by_head(coarse_qkv[1], coarse_qkv[2], heads)
    query_up = by_head(coarse_qkv[0], grad_coarse, heads)
    across = swapped(key_value, "zl")
    beside = swapped(key_value, "c")
    queries = [query_up] + [shifted(query_up, "y", step) for step in (1, 2, 3)]
    corner = swapped(across, "c")
    keys = [key_value, beside, across, corner]

    weight = qkv_weight.reshape(3, wide, heads, HD)
    weight = jnp.concatenate(
        [
            jnp.concatenate([weight[1], weight[2]], axis=2).reshape(wide, 2 * group),
            weight[0].reshape(wide, group),
        ],
        axis=1,
    )
    joint = lax.dot_general(
        weight, merge_weight, (((0,), (1,)), ((), ())), preferred_element_type=F32
    ).astype(BF16)

    own_qkv = fine_qkv.reshape(3, own, width)
    tall = with_rows(fine_qkv, 1)
    queries, joint, tall = lax.optimization_barrier((queries, joint, tall))
    ext_qkv = with_columns(tall, 1)

    part_most = coarse_stats(keys, queries, 0, heads - 1, 256)
    part_most, ext_qkv = lax.optimization_barrier((part_most, ext_qkv))
    own_out = fine_forward(own_qkv, ext_qkv, rows, columns)
    keys, own_out = lax.optimization_barrier((keys, own_out))
    part_last = coarse_stats(keys, queries, heads - 1, 1, 256)
    stats_most = merged_stats(part_most, heads - 1, tokens)
    stats_last = merged_stats(part_last, 1, tokens)
    tall_out = with_rows(own_out.reshape(rows, columns, width + 128), 0)
    stats_most, tall_out = lax.optimization_barrier((stats_most, tall_out))
    ext_out = with_columns(tall_out, 0)

    found = coarse_grads(keys, queries, stats_most, 0, heads - 1, ())
    kept, sent, *query_grads = coarse_grads(keys, queries, stats_last, heads - 1, 1, found)
    from_core = swapped(sent, "c")
    query_pieces = [query_grads[0]]
    for step in (1, 2, 3):
        query_pieces.append(shifted(query_grads[step], "y", -step))
    passed = (kept[:, 1].astype(F32) + from_core[:, 1].astype(F32)).astype(BF16)
    arrived = swapped(passed, "zl")
    projected = project(query_pieces, kept, from_core, arrived, joint)

    pieces = []
    for piece, (step, flip) in zip(projected, row_moves()):
        if (step, flip) != (0, 0):
            pairs = [(i, row_target(i, step, flip)) for i in range(lax.axis_size(ROW))]
            piece = lax.ppermute(piece, ROW, pairs)
        pieces.append(piece)
    own_up = spread(pieces, coarse_columns)

    tall_up = with_rows(own_up.reshape(rows, columns, width), 0)
    grad_query = fine_query_grads(own_qkv, ext_qkv, own_up, own_out, rows, columns)
    tall_up, grad_query = lax.optimization_barrier((tall_up, grad_query))
    ext_up = with_columns(tall_up, 0)
    sums = fine_key_grads(
        own_qkv, ext_qkv[:1], ext_up[:1], ext_out[:1], (), 0, rows, columns
    )
    grad_key, grad_value = fine_key_grads(
        own_qkv, ext_qkv[1:], ext_up[1:], ext_out[1:], sums, 1, rows, columns
    )
    shape = (rows, columns, width)
    return grad_query.reshape(shape), grad_key.reshape(shape), grad_value.reshape(shape)


def solution(mesh):
    split = Mesh(mesh.devices.reshape(4, 2, 2, 4, 2), ROW + COL)
    return jax.shard_map(
        shards,
        mesh=split,
        in_specs=(
            P(None, ROW, COL, None),
            P(None, COL, None, ROW),
            P(COL, None, ROW),
            P(),
            P(None, None, ROW),
        ),
        out_specs=(P(ROW, COL, None), P(ROW, COL, None), P(ROW, COL, None)),
        check_vma=False,
    )
```

```python
import jax
import jax.numpy as jnp
from jax import lax
from jax.experimental import pallas as pl
from jax.experimental.pallas import tpu as pltpu
from jax.sharding import Mesh
from jax.sharding import PartitionSpec as P

HD = 64
RADIUS = 7
SCALE = 0.125
SIDE = 32
RIM = 8
HIDDEN = -1e30
ROW = ("x", "zh")
COL = ("zl", "y", "c")
F32 = jnp.float32
BF16 = jnp.bfloat16
VMEM = 60 << 20


def nt(left, right):
    return lax.dot_general(left, right, (((1,), (1,)), ((), ())), preferred_element_type=F32)


def nn(left, right):
    return lax.dot_general(left, right, (((1,), (0,)), ((), ())), preferred_element_type=F32)


def half(pair, which):
    lane = lax.broadcasted_iota(jnp.int32, pair.shape, 1)
    return jnp.where((lane < HD) == (which == 0), pair, jnp.zeros_like(pair))


def cost(flops, bytes_accessed, exps):
    return pl.CostEstimate(flops=flops, bytes_accessed=bytes_accessed, transcendentals=exps)


def prepare(coarse_qkv, grad_coarse):
    _, tokens, group = coarse_qkv.shape
    heads = group // HD

    def body(qkv_ref, up_ref, kv_out, qu_out):
        for head in range(heads):
            lanes = slice(head * HD, head * HD + HD)
            kv_out[head] = jnp.concatenate([qkv_ref[1, :, lanes], qkv_ref[2, :, lanes]], axis=1)
            qu_out[head] = jnp.concatenate([qkv_ref[0, :, lanes], up_ref[:, lanes]], axis=1)

    return whole_call(
        body,
        [jax.ShapeDtypeStruct((heads, tokens, 2 * HD), BF16)] * 2,
        "prepare",
        1 << 20,
        [],
        coarse_qkv,
        grad_coarse,
    )


def own_block(step, tokens):
    count = lax.axis_size("y")
    owner = (lax.axis_index("y") + count - step) % count
    return pl.ds(pl.multiple_of(owner * tokens, tokens), tokens)


def coarse_stats(key_values, query_ups, key_tile):
    heads, tokens, _ = key_values[0].shape
    blocks = len(query_ups)
    per_block = tokens // key_tile

    def body(*refs):
        kv_refs, qu_refs = refs[:blocks], refs[blocks : 2 * blocks]
        out_ref, held = refs[2 * blocks :]
        for at in range(blocks):

            @pl.when(pl.program_id(1) == at)
            def _():
                held[...] = qu_refs[at][0]

        query = half(held[...], 0) * BF16(SCALE)
        upstream = half(held[...], 1)
        peak = jnp.full((1, tokens), -jnp.inf, F32)
        total = jnp.zeros((1, tokens), F32)
        weighted = jnp.zeros((1, tokens), F32)
        for i in range(blocks * per_block):
            start = (i % per_block) * key_tile
            tile = kv_refs[i // per_block][0, start : start + key_tile, :]
            score = nt(tile, query)
            product = nt(tile, upstream)
            new_peak = jnp.maximum(peak, jnp.max(score, axis=0, keepdims=True))
            decay = jnp.exp(peak - new_peak)
            share = jnp.exp(score - new_peak)
            total = total * decay + jnp.sum(share, axis=0, keepdims=True)
            weighted = weighted * decay + jnp.sum(share * product, axis=0, keepdims=True)
            peak = new_peak
        found = jnp.concatenate([peak + jnp.log(total), weighted / total], axis=0)
        out_ref[0, :, own_block(pl.program_id(1), tokens)] = found

    pairs = heads * (blocks * tokens) ** 2
    return pl.pallas_call(
        body,
        grid=(heads, blocks),
        in_specs=[pl.BlockSpec((1, tokens, 128), lambda h, q: (h, 0, 0))] * (2 * blocks),
        out_specs=pl.BlockSpec((1, 2, blocks * tokens), lambda h, q: (h, 0, 0)),
        out_shape=jax.ShapeDtypeStruct((heads, 2, blocks * tokens), F32),
        scratch_shapes=[pltpu.VMEM((tokens, 128), BF16)],
        name="coarse_stats",
        cost_estimate=cost(4 * pairs * 256, 2 << 20, pairs),
        compiler_params=pltpu.CompilerParams(vmem_limit_bytes=VMEM),
    )(*key_values, *query_ups)


def coarse_grads(key_values, query_ups, stats):
    heads, tokens, _ = key_values[0].shape
    blocks = len(query_ups)
    parts = stats.shape[0]

    def body(*refs):
        kv_refs, qu_refs = refs[:blocks], refs[blocks : 2 * blocks]
        stats_ref, kept_ref, sent_ref = refs[2 * blocks : 2 * blocks + 3]
        q_outs = refs[-blocks - 2 : -2]
        acc, held = refs[-2:]
        for at in range(blocks):

            @pl.when(pl.program_id(1) == at)
            def _():
                held[...] = qu_refs[at][0]

        @pl.when(pl.program_id(1) == 0)
        def _():
            acc[...] = jnp.zeros_like(acc)

        query = half(held[...], 0) * BF16(SCALE)
        upstream = half(held[...], 1)
        found = [stats_ref[i, 0, :, own_block(pl.program_id(1), tokens)] for i in range(parts)]
        peak = found[0][:1]
        for part in found[1:]:
            peak = jnp.maximum(peak, part[:1])
        shares = [jnp.exp(part[:1] - peak) for part in found]
        total = sum(shares)
        log_total = peak + jnp.log(total)
        delta = sum(share * part[1:] for share, part in zip(shares, found)) / total
        found = jnp.zeros((HD, tokens), F32)
        for i in range(blocks):
            tile = kv_refs[i][0]
            share = jnp.exp(nt(tile, query) - log_total)
            grads = (share * (nt(tile, upstream) - delta)).astype(BF16)
            acc[i] += nn(grads, query) + nn(share.astype(BF16), upstream)
            found += nn(tile[:, :HD].T, grads)
        found = (found * SCALE).astype(BF16)
        for at in range(blocks):

            @pl.when(pl.program_id(1) == at)
            def _():
                q_outs[at][...] = found

        @pl.when(pl.program_id(1) == blocks - 1)
        def _():
            for i in range(blocks // 2):
                kept_ref[0, i] = acc[2 * i].astype(BF16)
                sent_ref[0, i] = acc[2 * i + 1].astype(BF16)

    pairs = heads * (blocks * tokens) ** 2
    out_shape = [jax.ShapeDtypeStruct((heads, blocks // 2, tokens, 128), BF16)] * 2
    out_shape += [jax.ShapeDtypeStruct((heads * HD, tokens), BF16)] * blocks
    return pl.pallas_call(
        body,
        grid=(heads, blocks),
        in_specs=[pl.BlockSpec((1, tokens, 128), lambda h, q: (h, 0, 0))] * (2 * blocks)
        + [pl.BlockSpec((parts, 1, 2, blocks * tokens), lambda h, q: (0, h, 0, 0))],
        out_specs=[pl.BlockSpec((1, blocks // 2, tokens, 128), lambda h, q: (h, 0, 0, 0))] * 2
        + [pl.BlockSpec((HD, tokens), lambda h, q: (h, 0))] * blocks,
        out_shape=out_shape,
        scratch_shapes=[
            pltpu.VMEM((blocks, tokens, 128), F32),
            pltpu.VMEM((tokens, 128), BF16),
        ],
        name="coarse_grads",
        cost_estimate=cost(10 * pairs * 256, 4 << 20, pairs),
        compiler_params=pltpu.CompilerParams(vmem_limit_bytes=VMEM),
    )(*key_values, *query_ups, stats)


def whole_call(body, out_shape, name, flops, scratch, *operands):
    return pl.pallas_call(
        body,
        out_shape=out_shape,
        scratch_shapes=scratch,
        name=name,
        cost_estimate=cost(flops, 6 << 20, 1 << 20),
        compiler_params=pltpu.CompilerParams(vmem_limit_bytes=VMEM),
    )(*operands)


def pairs_of(width):
    return [(pair, slice(pair * 128, pair * 128 + 128)) for pair in range(width // 128)]


def window_bias(own, rows, columns, part, transposed):
    count = SIDE * SIDE // 2
    shape = (own, count) if transposed else (count, own)
    ext = lax.broadcasted_iota(jnp.int32, shape, 1 if transposed else 0)
    inner = lax.broadcasted_iota(jnp.int32, shape, 0 if transposed else 1)
    if part == 0:
        ext_row, ext_column = ext >> 4, (ext & 15) + RIM
    else:
        ext_row = (ext & 255) >> 3
        ext_column = (ext & 7) + jnp.where(ext >= 256, SIDE - RIM, 0)
    row_gap = ext_row - (inner >> 4) - RIM
    column_gap = ext_column - (inner & 15) - RIM
    row = ext_row + (lax.axis_index(ROW) * rows - RIM)
    column = ext_column + (lax.axis_index(COL) * columns - RIM)
    seen = (jnp.abs(row_gap) <= RADIUS) & (jnp.abs(column_gap) <= RADIUS)
    seen &= (row >= 0) & (row < lax.axis_size(ROW) * rows)
    seen &= (column >= 0) & (column < lax.axis_size(COL) * columns)
    return jnp.where(seen, 0.0, HIDDEN).astype(F32)


def fill_bias(bias_ref, own, rows, columns):
    count = SIDE * SIDE // 2
    for part in range(2):
        bias_ref[part * count : (part + 1) * count, :] = window_bias(
            own, rows, columns, part, False
        )


def stacked(refs, which, lanes):
    return jnp.concatenate([ref[which, :, lanes] for ref in refs], axis=0)


def fine_grads(own_qkv, ext_kv, own_up, rows, columns):
    _, own, width = own_qkv.shape
    sizes = [ref.shape[1] for ref in ext_kv]
    places = [sum(sizes[:i]) for i in range(len(sizes))]

    def body(q_ref, mid_ref, low_ref, high_ref, up_ref, q_out, mid_out, low_out, high_out, bias_ref):
        fill_bias(bias_ref, own, rows, columns)
        ext = (mid_ref, low_ref, high_ref)
        outs = (mid_out, low_out, high_out)
        for pair, lanes in pairs_of(width):
            key = stacked(ext, 0, lanes)
            key_t = key.T
            value = stacked(ext, 1, lanes)
            parts = []
            key_sum = jnp.zeros((SIDE * SIDE, 128), F32)
            value_sum = jnp.zeros((SIDE * SIDE, 128), F32)
            for side in range(2):
                query = half(q_ref[0, :, lanes], side) * BF16(SCALE)
                up = half(up_ref[:, lanes], side)
                score = nt(key, query) + bias_ref[...]
                product = nt(value, up)
                share = jnp.exp(score - jnp.max(score, axis=0, keepdims=True))
                total = jnp.sum(share, axis=0, keepdims=True)
                delta = jnp.sum(share * product, axis=0, keepdims=True) / total
                share = share * (1.0 / total)
                grads = (share * (product - delta)).astype(BF16)
                key_sum += nn(grads, query)
                value_sum += nn(share.astype(BF16), up)
                parts.append(nn(key_t[side * HD : side * HD + HD], grads))
            q_out[:, lanes] = (jnp.concatenate(parts, axis=0).T * SCALE).astype(BF16)
            for out, place, size in zip(outs, places, sizes):
                right = slice(width + pair * 128, width + pair * 128 + 128)
                out[:, lanes] = key_sum[place : place + size].astype(out.dtype)
                out[:, right] = value_sum[place : place + size].astype(out.dtype)

    return whole_call(
        body,
        [jax.ShapeDtypeStruct((own, width), BF16)]
        + [
            jax.ShapeDtypeStruct((size, 2 * width), BF16 if i else F32)
            for i, size in enumerate(sizes)
        ],
        "fine_grads",
        2 << 30,
        [pltpu.VMEM((SIDE * SIDE, own), F32)],
        own_qkv,
        *ext_kv,
        own_up,
    )


def add_columns(mid, from_left, from_right, columns):
    cells, wide = mid.shape
    tall = cells // columns
    edge = RIM * columns

    def body(mid_ref, left_ref, right_ref, top_out, own_out, bottom_out):
        left = left_ref[...].astype(F32).reshape(tall, RIM, wide)
        right = right_ref[...].astype(F32).reshape(tall, RIM, wide)
        both = jnp.concatenate([left, right], axis=1).reshape(cells, wide)
        total = mid_ref[...] + both
        top_out[...] = total[:edge].astype(BF16)
        own_out[...] = total[edge : cells - edge]
        bottom_out[...] = total[cells - edge :].astype(BF16)

    return whole_call(
        body,
        [
            jax.ShapeDtypeStruct((edge, wide), BF16),
            jax.ShapeDtypeStruct((cells - 2 * edge, wide), F32),
            jax.ShapeDtypeStruct((edge, wide), BF16),
        ],
        "add_columns",
        1 << 20,
        [],
        mid,
        from_left,
        from_right,
    )


def add_rows(own, from_above, from_below):
    cells, wide = own.shape
    width = wide // 2

    def body(own_ref, above_ref, below_ref, k_out, v_out):
        arrived = jnp.concatenate([above_ref[...], below_ref[...]], axis=0)
        total = own_ref[...] + arrived.astype(F32)
        k_out[...] = total[:, :width].astype(BF16)
        v_out[...] = total[:, width:].astype(BF16)

    return whole_call(
        body,
        [jax.ShapeDtypeStruct((cells, width), BF16)] * 2,
        "add_rows",
        1 << 20,
        [],
        own,
        from_above,
        from_below,
    )


def project(query_pieces, kept, from_core, arrived, joint, columns, count):
    group, tokens = query_pieces[0].shape
    heads = kept.shape[0]
    rows = tokens // columns
    each = rows // count
    size = each * columns
    wide = joint.shape[2]

    def body(*refs):
        pieces = refs[: len(query_pieces)]
        kept_ref, core_ref, arrived_ref, joint_ref, out, held, weight = refs[len(query_pieces) :]
        for head in range(heads):
            total = kept_ref[head, 0].astype(F32) + core_ref[head, 0].astype(F32)
            held[:, head * 128 : head * 128 + 128] = total + arrived_ref[head].astype(F32)
            for part in range(2):
                at = head * 128 + part * HD
                weight[at : at + HD, :] = joint_ref[1 + part, head * HD : head * HD + HD, :]
        weight[2 * group :, :] = joint_ref[0]
        total = pieces[0][...].astype(F32)
        for piece in pieces[1:]:
            total += piece[...].astype(F32)
        held[:, 2 * group :] = total.T
        for at in range(count):
            taken = [
                held[c * rows + at * each : c * rows + (at + 1) * each, :] for c in range(columns)
            ]
            chosen = jnp.concatenate(taken, axis=0).astype(BF16)
            out[at] = nn(chosen, weight[...]).astype(BF16)

    return whole_call(
        body,
        jax.ShapeDtypeStruct((count, size, wide), BF16),
        "project",
        2 << 30,
        [pltpu.VMEM((tokens, 3 * group), F32), pltpu.VMEM((3 * group, wide), BF16)],
        *query_pieces,
        kept,
        from_core,
        arrived,
        joint,
    )


def spread(pieces, columns):
    count, tokens, wide = pieces.shape
    width = wide // 4

    def body(in_ref, out):
        total = in_ref[0].astype(F32)
        for at in range(1, count):
            total += in_ref[at].astype(F32)
        total = total.astype(BF16)
        cells = 2 * tokens
        fine = lax.broadcasted_iota(jnp.int32, (cells, tokens), 0)
        token = lax.broadcasted_iota(jnp.int32, (cells, tokens), 1)
        cell = (token & 7) * 2 * columns + (token >> 3) * 2
        for a in range(2):
            grid = jnp.zeros((cells, width), F32)
            for b in range(2):
                place = jnp.where(fine == cell + b, 1.0, 0.0).astype(BF16)
                lanes = slice((2 * a + b) * width, (2 * a + b + 1) * width)
                grid += nn(place, total[:, lanes])
            grid = grid.astype(BF16)
            for row in range(tokens // columns):
                at = (2 * row + a) * 2 * columns
                out[at : at + 2 * columns, :] = grid[row * 2 * columns : (row + 1) * 2 * columns]

    return whole_call(
        body,
        jax.ShapeDtypeStruct((4 * tokens, width), BF16),
        "spread",
        1 << 28,
        [],
        pieces,
    )


def shifted(array, axis, step):
    count = lax.axis_size(axis)
    return lax.ppermute(array, axis, [(i, (i + step) % count) for i in range(count)])


def swapped(array, axis):
    return lax.ppermute(array, axis, [(0, 1), (1, 0)])


def onward(low, high, axis):
    count = lax.axis_size(axis)
    forward = [(i, i + 1) for i in range(count - 1)]
    backward = [(i + 1, i) for i in range(count - 1)]
    return lax.ppermute(low, axis, forward), lax.ppermute(high, axis, backward)


def edges(block, axis, at):
    size = block.shape[at]
    return onward(
        lax.slice_in_dim(block, size - RIM, None, axis=at),
        lax.slice_in_dim(block, 0, RIM, axis=at),
        axis,
    )


def with_rows(block, dim):
    low, high = edges(block, ROW, dim)
    return jnp.concatenate([low, block, high], axis=dim)


def with_columns(block, dim):
    low, high = edges(block, COL, dim + 1)
    shape = block.shape[:dim] + (-1, block.shape[-1])
    return block.reshape(shape), low.reshape(shape), high.reshape(shape)


def shards(fine_qkv, coarse_qkv, grad_coarse, merge_weight, qkv_weight):
    rows, columns, width = fine_qkv.shape[1:]
    own = rows * columns
    coarse_columns, coarse_rows, group = grad_coarse.shape
    tokens = coarse_columns * coarse_rows

    key_value, query_up = prepare(
        coarse_qkv.reshape(3, tokens, group), grad_coarse.reshape(tokens, group)
    )
    across = swapped(key_value, "zl")
    beside = swapped(key_value, "c")
    queries = [query_up] + [shifted(query_up, "y", step) for step in (1, 3, 2)]
    queries = [queries[i] for i in (0, 1, 3, 2)]
    corner = swapped(across, "c")
    keys = [key_value, beside, across, corner]

    own_qkv = fine_qkv.reshape(3, own, width)
    tall = with_rows(fine_qkv[1:], 1)
    queries, tall = lax.optimization_barrier((queries, tall))
    ext_kv = with_columns(tall, 1)

    part = coarse_stats(keys, queries, 256)
    stats = lax.all_gather(part, "y", axis=0)
    kept, sent, *query_grads = coarse_grads(keys, queries, stats)

    sent, merge_weight = lax.optimization_barrier((sent, merge_weight))
    from_core = swapped(sent, "c")
    query_pieces = [query_grads[0]]
    for step in (1, 2, 3):
        query_pieces.append(shifted(query_grads[step], "y", -step))
    passed = (kept[:, 1].astype(F32) + from_core[:, 1].astype(F32)).astype(BF16)
    arrived = swapped(passed, "zl")
    joint = lax.dot_general(
        qkv_weight, merge_weight, (((1,), (1,)), ((), ())), preferred_element_type=F32
    ).astype(BF16)
    count = lax.axis_size(ROW)
    projected = project(
        query_pieces, kept, from_core, arrived, joint, coarse_columns, count
    )
    pieces = lax.all_to_all(projected, ROW, 0, 0)
    own_up = spread(pieces, coarse_columns)

    grad_query, mid, low, high = fine_grads(own_qkv, ext_kv, own_up, rows, columns)
    from_left, from_right = onward(high, low, COL)
    top, middle, bottom = add_columns(mid, from_left, from_right, columns)
    from_above, from_below = onward(bottom, top, ROW)
    grad_key, grad_value = add_rows(middle, from_above, from_below)
    shape = (rows, columns, width)
    return grad_query.reshape(shape), grad_key.reshape(shape), grad_value.reshape(shape)


def solution(mesh):
    split = Mesh(mesh.devices.reshape(4, 2, 2, 4, 2), ROW + COL)
    return jax.shard_map(
        shards,
        mesh=split,
        in_specs=(
            P(None, ROW, COL, None),
            P(None, COL, None, ROW),
            P(COL, None, ROW),
            P(),
            P(None, None, ROW),
        ),
        out_specs=(P(ROW, COL, None), P(ROW, COL, None), P(ROW, COL, None)),
        check_vma=False,
    )
```

```python
import jax
import jax.numpy as jnp
from jax import lax
from jax.experimental import pallas as pl
from jax.experimental.pallas import tpu as pltpu
from jax.sharding import Mesh
from jax.sharding import PartitionSpec as P

HD = 64
RADIUS = 7
SCALE = 0.125
SIDE = 32
RIM = 8
HIDDEN = -1e30
ROW = ("x", "zh")
COL = ("zl", "y", "c")
F32 = jnp.float32
BF16 = jnp.bfloat16
VMEM = 60 << 20


def nt(left, right):
    return lax.dot_general(left, right, (((1,), (1,)), ((), ())), preferred_element_type=F32)


def nn(left, right):
    return lax.dot_general(left, right, (((1,), (0,)), ((), ())), preferred_element_type=F32)


def half(pair, which):
    lane = lax.broadcasted_iota(jnp.int32, pair.shape, 1)
    return jnp.where((lane < HD) == (which == 0), pair, jnp.zeros_like(pair))


def cost(flops, bytes_accessed, exps):
    return pl.CostEstimate(flops=flops, bytes_accessed=bytes_accessed, transcendentals=exps)


def prepare(coarse_qkv, grad_coarse):
    _, tokens, group = coarse_qkv.shape
    heads = group // HD

    def body(qkv_ref, up_ref, kv_out, qu_out):
        for head in range(heads):
            lanes = slice(head * HD, head * HD + HD)
            kv_out[head] = jnp.concatenate([qkv_ref[1, :, lanes], qkv_ref[2, :, lanes]], axis=1)
            qu_out[head] = jnp.concatenate([qkv_ref[0, :, lanes], up_ref[:, lanes]], axis=1)

    return whole_call(
        body,
        [jax.ShapeDtypeStruct((heads, tokens, 2 * HD), BF16)] * 2,
        "prepare",
        1 << 20,
        [],
        coarse_qkv,
        grad_coarse,
    )


def own_block(step, tokens):
    count = lax.axis_size("y")
    owner = (lax.axis_index("y") + count - step) % count
    return pl.ds(pl.multiple_of(owner * tokens, tokens), tokens)


def coarse_stats(key_values, query_ups, key_tile):
    heads, tokens, _ = key_values[0].shape
    blocks = len(query_ups)
    per_block = tokens // key_tile

    def body(*refs):
        kv_refs, qu_refs = refs[:blocks], refs[blocks : 2 * blocks]
        out_ref, held = refs[2 * blocks :]
        for at in range(blocks):

            @pl.when(pl.program_id(1) == at)
            def _():
                held[...] = qu_refs[at][0]

        query = half(held[...], 0) * BF16(SCALE)
        upstream = half(held[...], 1)
        peak = jnp.full((1, tokens), -jnp.inf, F32)
        total = jnp.zeros((1, tokens), F32)
        weighted = jnp.zeros((1, tokens), F32)
        for i in range(blocks * per_block):
            start = (i % per_block) * key_tile
            tile = kv_refs[i // per_block][0, start : start + key_tile, :]
            score = nt(tile, query)
            product = nt(tile, upstream)
            new_peak = jnp.maximum(peak, jnp.max(score, axis=0, keepdims=True))
            decay = jnp.exp(peak - new_peak)
            share = jnp.exp(score - new_peak)
            total = total * decay + jnp.sum(share, axis=0, keepdims=True)
            weighted = weighted * decay + jnp.sum(share * product, axis=0, keepdims=True)
            peak = new_peak
        found = jnp.concatenate([peak + jnp.log(total), weighted / total], axis=0)
        out_ref[0, :, own_block(pl.program_id(1), tokens)] = found

    pairs = heads * (blocks * tokens) ** 2
    return pl.pallas_call(
        body,
        grid=(heads, blocks),
        in_specs=[pl.BlockSpec((1, tokens, 128), lambda h, q: (h, 0, 0))] * (2 * blocks),
        out_specs=pl.BlockSpec((1, 2, blocks * tokens), lambda h, q: (h, 0, 0)),
        out_shape=jax.ShapeDtypeStruct((heads, 2, blocks * tokens), F32),
        scratch_shapes=[pltpu.VMEM((tokens, 128), BF16)],
        name="coarse_stats",
        cost_estimate=cost(4 * pairs * 256, 2 << 20, pairs),
        compiler_params=pltpu.CompilerParams(vmem_limit_bytes=VMEM),
    )(*key_values, *query_ups)


def coarse_grads(key_values, query_ups, stats):
    heads, tokens, _ = key_values[0].shape
    blocks = len(query_ups)
    parts = stats.shape[0]

    def body(*refs):
        kv_refs, qu_refs = refs[:blocks], refs[blocks : 2 * blocks]
        stats_ref, kept_ref, sent_ref = refs[2 * blocks : 2 * blocks + 3]
        q_outs = refs[-blocks - 2 : -2]
        acc, held = refs[-2:]
        for at in range(blocks):

            @pl.when(pl.program_id(1) == at)
            def _():
                held[...] = qu_refs[at][0]

        @pl.when(pl.program_id(1) == 0)
        def _():
            acc[...] = jnp.zeros_like(acc)

        query = half(held[...], 0) * BF16(SCALE)
        upstream = half(held[...], 1)
        found = [stats_ref[i, 0, :, own_block(pl.program_id(1), tokens)] for i in range(parts)]
        peak = found[0][:1]
        for part in found[1:]:
            peak = jnp.maximum(peak, part[:1])
        shares = [jnp.exp(part[:1] - peak) for part in found]
        total = sum(shares)
        log_total = peak + jnp.log(total)
        delta = sum(share * part[1:] for share, part in zip(shares, found)) / total
        found = jnp.zeros((HD, tokens), F32)
        for i in range(blocks):
            tile = kv_refs[i][0]
            share = jnp.exp(nt(tile, query) - log_total)
            grads = (share * (nt(tile, upstream) - delta)).astype(BF16)
            acc[i] += nn(grads, query) + nn(share.astype(BF16), upstream)
            found += nn(tile[:, :HD].T, grads)
        found = (found * SCALE).astype(BF16)
        for at in range(blocks):

            @pl.when(pl.program_id(1) == at)
            def _():
                q_outs[at][...] = found

        @pl.when(pl.program_id(1) == blocks - 1)
        def _():
            for i in range(blocks // 2):
                kept_ref[0, i] = acc[2 * i].astype(BF16)
                sent_ref[0, i] = acc[2 * i + 1].astype(BF16)

    pairs = heads * (blocks * tokens) ** 2
    out_shape = [jax.ShapeDtypeStruct((heads, blocks // 2, tokens, 128), BF16)] * 2
    out_shape += [jax.ShapeDtypeStruct((heads * HD, tokens), BF16)] * blocks
    return pl.pallas_call(
        body,
        grid=(heads, blocks),
        in_specs=[pl.BlockSpec((1, tokens, 128), lambda h, q: (h, 0, 0))] * (2 * blocks)
        + [pl.BlockSpec((parts, 1, 2, blocks * tokens), lambda h, q: (0, h, 0, 0))],
        out_specs=[pl.BlockSpec((1, blocks // 2, tokens, 128), lambda h, q: (h, 0, 0, 0))] * 2
        + [pl.BlockSpec((HD, tokens), lambda h, q: (h, 0))] * blocks,
        out_shape=out_shape,
        scratch_shapes=[
            pltpu.VMEM((blocks, tokens, 128), F32),
            pltpu.VMEM((tokens, 128), BF16),
        ],
        name="coarse_grads",
        cost_estimate=cost(10 * pairs * 256, 4 << 20, pairs),
        compiler_params=pltpu.CompilerParams(vmem_limit_bytes=VMEM),
    )(*key_values, *query_ups, stats)


def whole_call(body, out_shape, name, flops, scratch, *operands):
    return pl.pallas_call(
        body,
        out_shape=out_shape,
        scratch_shapes=scratch,
        name=name,
        cost_estimate=cost(flops, 6 << 20, 1 << 20),
        compiler_params=pltpu.CompilerParams(vmem_limit_bytes=VMEM),
    )(*operands)


def pairs_of(width):
    return [(pair, slice(pair * 128, pair * 128 + 128)) for pair in range(width // 128)]


def window_bias(own, rows, columns, part, transposed):
    count = SIDE * SIDE // 2
    shape = (own, count) if transposed else (count, own)
    ext = lax.broadcasted_iota(jnp.int32, shape, 1 if transposed else 0)
    inner = lax.broadcasted_iota(jnp.int32, shape, 0 if transposed else 1)
    if part == 0:
        ext_row, ext_column = ext >> 4, (ext & 15) + RIM
    else:
        ext_row = (ext & 255) >> 3
        ext_column = (ext & 7) + jnp.where(ext >= 256, SIDE - RIM, 0)
    row_gap = ext_row - (inner >> 4) - RIM
    column_gap = ext_column - (inner & 15) - RIM
    row = ext_row + (lax.axis_index(ROW) * rows - RIM)
    column = ext_column + (lax.axis_index(COL) * columns - RIM)
    seen = (jnp.abs(row_gap) <= RADIUS) & (jnp.abs(column_gap) <= RADIUS)
    seen &= (row >= 0) & (row < lax.axis_size(ROW) * rows)
    seen &= (column >= 0) & (column < lax.axis_size(COL) * columns)
    return jnp.where(seen, 0.0, HIDDEN).astype(F32)


def fill_bias(bias_ref, own, rows, columns):
    count = SIDE * SIDE // 2
    for part in range(2):
        bias_ref[part * count : (part + 1) * count, :] = window_bias(
            own, rows, columns, part, False
        )


def stacked(refs, which, lanes):
    return jnp.concatenate([ref[which, :, lanes] for ref in refs], axis=0)


def window_pieces(columns, rows):
    edge = RIM * columns
    corner = RIM * RIM
    middle = rows * columns
    side = rows * RIM
    base = 2 * edge + middle
    wing = 2 * corner + side
    return [
        ((0, 0), edge, middle),
        ((-1, 0), 0, edge),
        ((1, 0), edge + middle, edge),
        ((0, -1), base + corner, side),
        ((0, 1), base + wing + corner, side),
        ((-1, -1), base, corner),
        ((1, -1), base + corner + side, corner),
        ((-1, 1), base + wing, corner),
        ((1, 1), base + wing + corner + side, corner),
    ]


def fine_grads(own_qkv, ext_kv, own_up, rows, columns):
    _, own, width = own_qkv.shape
    pieces = window_pieces(columns, rows)

    def body(q_ref, mid_ref, low_ref, high_ref, up_ref, q_out, *rest):
        outs, bias_ref = rest[:-1], rest[-1]
        fill_bias(bias_ref, own, rows, columns)
        ext = (mid_ref, low_ref, high_ref)
        for pair, lanes in pairs_of(width):
            key = stacked(ext, 0, lanes)
            key_t = key.T
            value = stacked(ext, 1, lanes)
            parts = []
            key_sum = jnp.zeros((SIDE * SIDE, 128), F32)
            value_sum = jnp.zeros((SIDE * SIDE, 128), F32)
            for side in range(2):
                query = half(q_ref[0, :, lanes], side) * BF16(SCALE)
                up = half(up_ref[:, lanes], side)
                score = nt(key, query) + bias_ref[...]
                product = nt(value, up)
                share = jnp.exp(score - jnp.max(score, axis=0, keepdims=True))
                total = jnp.sum(share, axis=0, keepdims=True)
                delta = jnp.sum(share * product, axis=0, keepdims=True) / total
                share = share * (1.0 / total)
                grads = (share * (product - delta)).astype(BF16)
                key_sum += nn(grads, query)
                value_sum += nn(share.astype(BF16), up)
                parts.append(nn(key_t[side * HD : side * HD + HD], grads))
            q_out[:, lanes] = (jnp.concatenate(parts, axis=0).T * SCALE).astype(BF16)
            right = slice(width + pair * 128, width + pair * 128 + 128)
            for out, (_, place, size) in zip(outs, pieces):
                out[:, lanes] = key_sum[place : place + size].astype(out.dtype)
                out[:, right] = value_sum[place : place + size].astype(out.dtype)

    return whole_call(
        body,
        [jax.ShapeDtypeStruct((own, width), BF16)]
        + [
            jax.ShapeDtypeStruct((size, 2 * width), BF16 if i else F32)
            for i, (_, _, size) in enumerate(pieces)
        ],
        "fine_grads",
        2 << 30,
        [pltpu.VMEM((SIDE * SIDE, own), F32)],
        own_qkv,
        *ext_kv,
        own_up,
    )


def add_arrived(own, arrived, rows, columns):
    cells, wide = own.shape
    width = wide // 2

    def body(own_ref, *rest):
        above, below, left, right, up_left, down_left, up_right, down_right = [
            ref[...].astype(F32) for ref in rest[:-2]
        ]
        k_out, v_out = rest[-2:]
        total = own_ref[...] + jnp.concatenate([above, below], axis=0)

        def halves(first, second, tall):
            first = first.reshape(tall, RIM, wide)
            return jnp.concatenate([first, second.reshape(tall, RIM, wide)], axis=1)

        total += halves(left, right, rows).reshape(cells, wide)
        upper = halves(up_left, up_right, RIM)
        lower = halves(down_left, down_right, RIM)
        total += jnp.concatenate([upper, lower], axis=0).reshape(cells, wide)
        k_out[...] = total[:, :width].astype(BF16)
        v_out[...] = total[:, width:].astype(BF16)

    return whole_call(
        body,
        [jax.ShapeDtypeStruct((cells, width), BF16)] * 2,
        "add_arrived",
        1 << 20,
        [],
        own,
        *arrived,
    )


def project(query_pieces, kept, from_core, arrived, joint, columns, count):
    group, tokens = query_pieces[0].shape
    heads = kept.shape[0]
    rows = tokens // columns
    each = rows // count
    size = each * columns
    wide = joint.shape[2]
    operands = (*query_pieces, kept, from_core, arrived, joint)

    def body(*refs):
        pieces = refs[: len(query_pieces)]
        kept_ref, core_ref, arrived_ref, joint_ref, out, held, weight = refs[len(query_pieces) :]

        @pl.when(pl.program_id(0) == 0)
        def _():
            for head in range(heads):
                total = kept_ref[head, 0].astype(F32) + core_ref[head, 0].astype(F32)
                held[:, head * 128 : head * 128 + 128] = total + arrived_ref[head].astype(F32)
                for part in range(2):
                    at = head * 128 + part * HD
                    weight[at : at + HD, :] = joint_ref[1 + part, head * HD : head * HD + HD, :]
            weight[2 * group :, :] = joint_ref[0]
            total = pieces[0][...].astype(F32)
            for piece in pieces[1:]:
                total += piece[...].astype(F32)
            held[:, 2 * group :] = total.T

        taken = []
        for c in range(columns):
            start = pl.multiple_of(c * rows + pl.program_id(0) * each, each)
            taken.append(held[pl.ds(start, each), :])
        chosen = jnp.concatenate(taken, axis=0).astype(BF16)
        out[0] = nn(chosen, weight[...]).astype(BF16)

    return pl.pallas_call(
        body,
        grid=(count,),
        in_specs=[
            pl.BlockSpec(array.shape, lambda d, rank=array.ndim: (0,) * rank)
            for array in operands
        ],
        out_specs=pl.BlockSpec((1, size, wide), lambda d: (d, 0, 0)),
        out_shape=jax.ShapeDtypeStruct((count, size, wide), BF16),
        scratch_shapes=[
            pltpu.VMEM((tokens, 3 * group), F32),
            pltpu.VMEM((3 * group, wide), BF16),
        ],
        name="project",
        cost_estimate=cost(2 << 30, 6 << 20, 0),
        compiler_params=pltpu.CompilerParams(vmem_limit_bytes=VMEM),
    )(*operands)


def spread(pieces, columns):
    count, tokens, wide = pieces.shape
    width = wide // 4

    def body(in_ref, out):
        total = in_ref[0].astype(F32)
        for at in range(1, count):
            total += in_ref[at].astype(F32)
        total = total.astype(BF16)
        cells = 2 * tokens
        fine = lax.broadcasted_iota(jnp.int32, (cells, tokens), 0)
        token = lax.broadcasted_iota(jnp.int32, (cells, tokens), 1)
        cell = (token & 7) * 2 * columns + (token >> 3) * 2
        for a in range(2):
            grid = jnp.zeros((cells, width), F32)
            for b in range(2):
                place = jnp.where(fine == cell + b, 1.0, 0.0).astype(BF16)
                lanes = slice((2 * a + b) * width, (2 * a + b + 1) * width)
                grid += nn(place, total[:, lanes])
            grid = grid.astype(BF16)
            for row in range(tokens // columns):
                at = (2 * row + a) * 2 * columns
                out[at : at + 2 * columns, :] = grid[row * 2 * columns : (row + 1) * 2 * columns]

    return whole_call(
        body,
        jax.ShapeDtypeStruct((4 * tokens, width), BF16),
        "spread",
        1 << 28,
        [],
        pieces,
    )


def shifted(array, axis, step):
    count = lax.axis_size(axis)
    return lax.ppermute(array, axis, [(i, (i + step) % count) for i in range(count)])


def swapped(array, axis):
    return lax.ppermute(array, axis, [(0, 1), (1, 0)])


def onward(low, high, axis):
    count = lax.axis_size(axis)
    forward = [(i, i + 1) for i in range(count - 1)]
    backward = [(i + 1, i) for i in range(count - 1)]
    return lax.ppermute(low, axis, forward), lax.ppermute(high, axis, backward)


def toward(piece, down, across):
    tall, wide = lax.axis_size(ROW), lax.axis_size(COL)
    pairs = []
    for row in range(tall):
        for column in range(wide):
            if 0 <= row + down < tall and 0 <= column + across < wide:
                here = row * wide + column
                pairs.append((here, here + down * wide + across))
    return lax.ppermute(piece, ROW + COL, pairs)


def edges(block, axis, at):
    size = block.shape[at]
    return onward(
        lax.slice_in_dim(block, size - RIM, None, axis=at),
        lax.slice_in_dim(block, 0, RIM, axis=at),
        axis,
    )


def with_rows(block, dim):
    low, high = edges(block, ROW, dim)
    return jnp.concatenate([low, block, high], axis=dim)


def with_columns(block, dim):
    low, high = edges(block, COL, dim + 1)
    shape = block.shape[:dim] + (-1, block.shape[-1])
    return block.reshape(shape), low.reshape(shape), high.reshape(shape)


def shards(fine_qkv, coarse_qkv, grad_coarse, merge_weight, qkv_weight):
    rows, columns, width = fine_qkv.shape[1:]
    own = rows * columns
    coarse_columns, coarse_rows, group = grad_coarse.shape
    tokens = coarse_columns * coarse_rows

    key_value, query_up = prepare(
        coarse_qkv.reshape(3, tokens, group), grad_coarse.reshape(tokens, group)
    )
    across = swapped(key_value, "zl")
    beside = swapped(key_value, "c")
    queries = [query_up] + [shifted(query_up, "y", step) for step in (1, 2, 3)]
    corner = swapped(across, "c")
    keys = [key_value, beside, across, corner]

    part = coarse_stats(keys, queries, 256)
    stats = lax.all_gather(part, "y", axis=0)
    kept, sent, *query_grads = coarse_grads(keys, queries, stats)

    from_core = swapped(sent, "c")
    query_pieces = [query_grads[0]]
    for step in (1, 2, 3):
        query_pieces.append(shifted(query_grads[step], "y", -step))
    passed = (kept[:, 1].astype(F32) + from_core[:, 1].astype(F32)).astype(BF16)
    arrived = swapped(passed, "zl")
    merge_weight, fine_qkv, _ = lax.optimization_barrier(
        (merge_weight, fine_qkv, passed[0, :1, :1])
    )
    joint = lax.dot_general(
        qkv_weight, merge_weight, (((1,), (1,)), ((), ())), preferred_element_type=F32
    ).astype(BF16)
    own_qkv = fine_qkv.reshape(3, own, width)
    tall = with_rows(fine_qkv[1:], 1)
    count = lax.axis_size(ROW)
    projected = project(
        query_pieces, kept, from_core, arrived, joint, coarse_columns, count
    )
    projected, tall = lax.optimization_barrier((projected, tall))
    ext_kv = with_columns(tall, 1)
    pieces = lax.all_to_all(projected, ROW, 0, 0)
    own_up = spread(pieces, coarse_columns)

    grad_query, middle, *rims = fine_grads(own_qkv, ext_kv, own_up, rows, columns)
    places = window_pieces(columns, rows)[1:]
    arrived = [toward(rim, *place[0]) for rim, place in zip(rims, places)]
    order = [(1, 0), (-1, 0), (0, 1), (0, -1), (1, 1), (-1, 1), (1, -1), (-1, -1)]
    found = {place[0]: piece for place, piece in zip(places, arrived)}
    grad_key, grad_value = add_arrived(middle, [found[at] for at in order], rows, columns)
    shape = (rows, columns, width)
    return grad_query.reshape(shape), grad_key.reshape(shape), grad_value.reshape(shape)


def solution(mesh):
    split = Mesh(mesh.devices.reshape(4, 2, 2, 4, 2), ROW + COL)
    return jax.shard_map(
        shards,
        mesh=split,
        in_specs=(
            P(None, ROW, COL, None),
            P(None, COL, None, ROW),
            P(COL, None, ROW),
            P(),
            P(None, None, ROW),
        ),
        out_specs=(P(ROW, COL, None), P(ROW, COL, None), P(ROW, COL, None)),
        check_vma=False,
    )
```

```python
import jax
import jax.numpy as jnp
from jax import lax
from jax.experimental import pallas as pl
from jax.experimental.pallas import tpu as pltpu
from jax.sharding import Mesh
from jax.sharding import PartitionSpec as P

HD = 64
RADIUS = 7
SCALE = 0.125
SIDE = 32
RIM = 8
HIDDEN = -1e30
ROW = ("x", "zh")
COL = ("zl", "y", "c")
F32 = jnp.float32
BF16 = jnp.bfloat16
VMEM = 60 << 20


def nt(left, right):
    return lax.dot_general(left, right, (((1,), (1,)), ((), ())), preferred_element_type=F32)


def nn(left, right):
    return lax.dot_general(left, right, (((1,), (0,)), ((), ())), preferred_element_type=F32)


def half(pair, which):
    lane = lax.broadcasted_iota(jnp.int32, pair.shape, 1)
    return jnp.where((lane < HD) == (which == 0), pair, jnp.zeros_like(pair))


def cost(flops, bytes_accessed, exps):
    return pl.CostEstimate(flops=flops, bytes_accessed=bytes_accessed, transcendentals=exps)


def prepare(coarse_qkv, grad_coarse):
    _, tokens, group = coarse_qkv.shape
    heads = group // HD

    def body(qkv_ref, up_ref, kv_out, qu_out):
        for head in range(heads):
            lanes = slice(head * HD, head * HD + HD)
            kv_out[head] = jnp.concatenate([qkv_ref[1, :, lanes], qkv_ref[2, :, lanes]], axis=1)
            qu_out[head] = jnp.concatenate([qkv_ref[0, :, lanes], up_ref[:, lanes]], axis=1)

    return whole_call(
        body,
        [jax.ShapeDtypeStruct((heads, tokens, 2 * HD), BF16)] * 2,
        "prepare",
        1 << 20,
        [],
        coarse_qkv,
        grad_coarse,
    )


def own_block(step, tokens):
    count = lax.axis_size("y")
    owner = (lax.axis_index("y") + count - step) % count
    return pl.ds(pl.multiple_of(owner * tokens, tokens), tokens)


def coarse_stats(key_values, query_ups, steps, before, key_tile):
    heads, tokens, _ = key_values[0].shape
    blocks, number = len(key_values), len(query_ups)
    per_block = tokens // key_tile

    def body(*refs):
        kv_refs, qu_refs = refs[:blocks], refs[blocks : blocks + number]
        out_ref, held = refs[-2:]
        if before:

            @pl.when(pl.program_id(1) == 0)
            def _():
                out_ref[...] = refs[blocks + number][...]

        for at in range(number):

            @pl.when(pl.program_id(1) == at)
            def _():
                held[...] = qu_refs[at][0]

        query = half(held[...], 0) * BF16(SCALE)
        upstream = half(held[...], 1)
        peak = jnp.full((1, tokens), -jnp.inf, F32)
        total = jnp.zeros((1, tokens), F32)
        weighted = jnp.zeros((1, tokens), F32)
        for i in range(blocks * per_block):
            start = (i % per_block) * key_tile
            tile = kv_refs[i // per_block][0, start : start + key_tile, :]
            score = nt(tile, query)
            product = nt(tile, upstream)
            new_peak = jnp.maximum(peak, jnp.max(score, axis=0, keepdims=True))
            decay = jnp.exp(peak - new_peak)
            share = jnp.exp(score - new_peak)
            total = total * decay + jnp.sum(share, axis=0, keepdims=True)
            weighted = weighted * decay + jnp.sum(share * product, axis=0, keepdims=True)
            peak = new_peak
        found = jnp.concatenate([peak + jnp.log(total), weighted / total], axis=0)
        for at, step in enumerate(steps):

            @pl.when(pl.program_id(1) == at)
            def _():
                out_ref[0, :, own_block(step, tokens)] = found

    pairs = heads * number * blocks * tokens**2
    return pl.pallas_call(
        body,
        grid=(heads, number),
        in_specs=[pl.BlockSpec((1, tokens, 128), lambda h, q: (h, 0, 0))] * (blocks + number)
        + [pl.BlockSpec((1, 2, blocks * tokens), lambda h, q: (h, 0, 0))] * len(before),
        out_specs=pl.BlockSpec((1, 2, blocks * tokens), lambda h, q: (h, 0, 0)),
        out_shape=jax.ShapeDtypeStruct((heads, 2, blocks * tokens), F32),
        scratch_shapes=[pltpu.VMEM((tokens, 128), BF16)],
        name="coarse_stats",
        cost_estimate=cost(4 * pairs * 256, 2 << 20, pairs),
        compiler_params=pltpu.CompilerParams(vmem_limit_bytes=VMEM),
    )(*key_values, *query_ups, *before)


def coarse_grads(key_values, query_ups, stats):
    heads, tokens, _ = key_values[0].shape
    blocks = len(query_ups)
    parts = stats.shape[0]

    def body(*refs):
        kv_refs, qu_refs = refs[:blocks], refs[blocks : 2 * blocks]
        stats_ref, kept_ref, sent_ref = refs[2 * blocks : 2 * blocks + 3]
        q_outs = refs[-blocks - 2 : -2]
        acc, held = refs[-2:]
        for at in range(blocks):

            @pl.when(pl.program_id(1) == at)
            def _():
                held[...] = qu_refs[at][0]

        @pl.when(pl.program_id(1) == 0)
        def _():
            acc[...] = jnp.zeros_like(acc)

        query = half(held[...], 0) * BF16(SCALE)
        upstream = half(held[...], 1)
        found = [stats_ref[i, 0, :, own_block(pl.program_id(1), tokens)] for i in range(parts)]
        peak = found[0][:1]
        for part in found[1:]:
            peak = jnp.maximum(peak, part[:1])
        shares = [jnp.exp(part[:1] - peak) for part in found]
        total = sum(shares)
        log_total = peak + jnp.log(total)
        delta = sum(share * part[1:] for share, part in zip(shares, found)) / total
        found = jnp.zeros((HD, tokens), F32)
        for i in range(blocks):
            tile = kv_refs[i][0]
            share = jnp.exp(nt(tile, query) - log_total)
            grads = (share * (nt(tile, upstream) - delta)).astype(BF16)
            acc[i] += nn(grads, query) + nn(share.astype(BF16), upstream)
            found += nn(tile[:, :HD].T, grads)
        found = (found * SCALE).astype(BF16)
        for at in range(blocks):

            @pl.when(pl.program_id(1) == at)
            def _():
                q_outs[at][...] = found

        @pl.when(pl.program_id(1) == blocks - 1)
        def _():
            for i in range(blocks // 2):
                kept_ref[0, i] = acc[2 * i].astype(BF16)
                sent_ref[0, i] = acc[2 * i + 1].astype(BF16)

    pairs = heads * (blocks * tokens) ** 2
    out_shape = [jax.ShapeDtypeStruct((heads, blocks // 2, tokens, 128), BF16)] * 2
    out_shape += [jax.ShapeDtypeStruct((heads * HD, tokens), BF16)] * blocks
    return pl.pallas_call(
        body,
        grid=(heads, blocks),
        in_specs=[pl.BlockSpec((1, tokens, 128), lambda h, q: (h, 0, 0))] * (2 * blocks)
        + [pl.BlockSpec((parts, 1, 2, blocks * tokens), lambda h, q: (0, h, 0, 0))],
        out_specs=[pl.BlockSpec((1, blocks // 2, tokens, 128), lambda h, q: (h, 0, 0, 0))] * 2
        + [pl.BlockSpec((HD, tokens), lambda h, q: (h, 0))] * blocks,
        out_shape=out_shape,
        scratch_shapes=[
            pltpu.VMEM((blocks, tokens, 128), F32),
            pltpu.VMEM((tokens, 128), BF16),
        ],
        name="coarse_grads",
        cost_estimate=cost(10 * pairs * 256, 4 << 20, pairs),
        compiler_params=pltpu.CompilerParams(vmem_limit_bytes=VMEM),
    )(*key_values, *query_ups, stats)


def whole_call(body, out_shape, name, flops, scratch, *operands):
    return pl.pallas_call(
        body,
        out_shape=out_shape,
        scratch_shapes=scratch,
        name=name,
        cost_estimate=cost(flops, 6 << 20, 1 << 20),
        compiler_params=pltpu.CompilerParams(vmem_limit_bytes=VMEM),
    )(*operands)


def pairs_of(width):
    return [(pair, slice(pair * 128, pair * 128 + 128)) for pair in range(width // 128)]


def window_bias(own, rows, columns, part, transposed):
    count = SIDE * SIDE // 2
    shape = (own, count) if transposed else (count, own)
    ext = lax.broadcasted_iota(jnp.int32, shape, 1 if transposed else 0)
    inner = lax.broadcasted_iota(jnp.int32, shape, 0 if transposed else 1)
    if part == 0:
        ext_row, ext_column = ext >> 4, (ext & 15) + RIM
    else:
        ext_row = (ext & 255) >> 3
        ext_column = (ext & 7) + jnp.where(ext >= 256, SIDE - RIM, 0)
    row_gap = ext_row - (inner >> 4) - RIM
    column_gap = ext_column - (inner & 15) - RIM
    row = ext_row + (lax.axis_index(ROW) * rows - RIM)
    column = ext_column + (lax.axis_index(COL) * columns - RIM)
    seen = (jnp.abs(row_gap) <= RADIUS) & (jnp.abs(column_gap) <= RADIUS)
    seen &= (row >= 0) & (row < lax.axis_size(ROW) * rows)
    seen &= (column >= 0) & (column < lax.axis_size(COL) * columns)
    return jnp.where(seen, 0.0, HIDDEN).astype(F32)


def fill_bias(bias_ref, own, rows, columns):
    count = SIDE * SIDE // 2
    for part in range(2):
        bias_ref[part * count : (part + 1) * count, :] = window_bias(
            own, rows, columns, part, False
        )


def stacked(refs, which, lanes):
    return jnp.concatenate([ref[which, :, lanes] for ref in refs], axis=0)


def fine_grads(own_qkv, ext_kv, own_up, rows, columns):
    _, own, width = own_qkv.shape
    sizes = [ref.shape[1] for ref in ext_kv]
    places = [sum(sizes[:i]) for i in range(len(sizes))]

    def body(q_ref, mid_ref, low_ref, high_ref, up_ref, q_out, mid_out, *rest):
        inner_out, outer_out, bias_ref = rest
        first = lax.axis_index("c") == 0
        fill_bias(bias_ref, own, rows, columns)
        ext = (mid_ref, low_ref, high_ref)
        for pair, lanes in pairs_of(width):
            key = stacked(ext, 0, lanes)
            key_t = key.T
            value = stacked(ext, 1, lanes)
            parts = []
            key_sum = jnp.zeros((SIDE * SIDE, 128), F32)
            value_sum = jnp.zeros((SIDE * SIDE, 128), F32)
            for side in range(2):
                query = half(q_ref[0, :, lanes], side) * BF16(SCALE)
                up = half(up_ref[:, lanes], side)
                score = nt(key, query) + bias_ref[...]
                product = nt(value, up)
                share = jnp.exp(score - jnp.max(score, axis=0, keepdims=True))
                total = jnp.sum(share, axis=0, keepdims=True)
                delta = jnp.sum(share * product, axis=0, keepdims=True) / total
                share = share * (1.0 / total)
                grads = (share * (product - delta)).astype(BF16)
                key_sum += nn(grads, query)
                value_sum += nn(share.astype(BF16), up)
                parts.append(nn(key_t[side * HD : side * HD + HD], grads))
            q_out[:, lanes] = (jnp.concatenate(parts, axis=0).T * SCALE).astype(BF16)
            right = slice(width + pair * 128, width + pair * 128 + 128)
            for at, total in ((lanes, key_sum), (right, value_sum)):
                mid, low, high = [
                    total[place : place + size] for place, size in zip(places, sizes)
                ]
                mid_out[:, at] = mid
                inner_out[:, at] = jnp.where(first, high, low).astype(BF16)
                outer_out[:, at] = jnp.where(first, low, high).astype(BF16)

    return whole_call(
        body,
        [jax.ShapeDtypeStruct((own, width), BF16)]
        + [
            jax.ShapeDtypeStruct((size, 2 * width), BF16 if i else F32)
            for i, size in enumerate(sizes)
        ],
        "fine_grads",
        2 << 30,
        [pltpu.VMEM((SIDE * SIDE, own), F32)],
        own_qkv,
        *ext_kv,
        own_up,
    )


def add_columns(mid, inner, outer, columns):
    cells, wide = mid.shape
    tall = cells // columns
    edge = RIM * columns

    def body(mid_ref, inner_ref, outer_ref, own_out, inner_out, outer_out):
        first = lax.axis_index("c") == 0
        inner = inner_ref[...].astype(F32).reshape(tall, RIM, wide)
        outer = outer_ref[...].astype(F32).reshape(tall, RIM, wide)
        left, right = jnp.where(first, outer, inner), jnp.where(first, inner, outer)
        both = jnp.concatenate([left, right], axis=1).reshape(cells, wide)
        total = mid_ref[...] + both
        top, bottom = total[:edge], total[cells - edge :]
        upper = lax.axis_index("zh") == 0
        own_out[...] = total[edge : cells - edge]
        inner_out[...] = jnp.where(upper, bottom, top).astype(BF16)
        outer_out[...] = jnp.where(upper, top, bottom).astype(BF16)

    return whole_call(
        body,
        [jax.ShapeDtypeStruct((cells - 2 * edge, wide), F32)]
        + [jax.ShapeDtypeStruct((edge, wide), BF16)] * 2,
        "add_columns",
        1 << 20,
        [],
        mid,
        inner,
        outer,
    )


def add_rows(own, inner, outer):
    cells, wide = own.shape
    width = wide // 2

    def body(own_ref, inner_ref, outer_ref, k_out, v_out):
        upper = lax.axis_index("zh") == 0
        inner = inner_ref[...].astype(F32)
        outer = outer_ref[...].astype(F32)
        above, below = jnp.where(upper, outer, inner), jnp.where(upper, inner, outer)
        total = own_ref[...] + jnp.concatenate([above, below], axis=0)
        k_out[...] = total[:, :width].astype(BF16)
        v_out[...] = total[:, width:].astype(BF16)

    return whole_call(
        body,
        [jax.ShapeDtypeStruct((cells, width), BF16)] * 2,
        "add_rows",
        1 << 20,
        [],
        own,
        inner,
        outer,
    )


def project(query_pieces, kept, from_core, arrived, joint, columns, count):
    group, tokens = query_pieces[0].shape
    heads = kept.shape[0]
    rows = tokens // columns
    each = rows // count
    size = each * columns
    wide = joint.shape[2]
    operands = (*query_pieces, kept, from_core, arrived, joint)

    def body(*refs):
        pieces = refs[: len(query_pieces)]
        kept_ref, core_ref, arrived_ref, joint_ref, out, held, weight = refs[len(query_pieces) :]

        @pl.when(pl.program_id(0) == 0)
        def _():
            for head in range(heads):
                total = kept_ref[head, 0].astype(F32) + core_ref[head, 0].astype(F32)
                held[:, head * 128 : head * 128 + 128] = total + arrived_ref[head].astype(F32)
                for part in range(2):
                    at = head * 128 + part * HD
                    weight[at : at + HD, :] = joint_ref[1 + part, head * HD : head * HD + HD, :]
            weight[2 * group :, :] = joint_ref[0]
            total = pieces[0][...].astype(F32)
            for piece in pieces[1:]:
                total += piece[...].astype(F32)
            held[:, 2 * group :] = total.T

        taken = []
        for c in range(columns):
            start = pl.multiple_of(c * rows + pl.program_id(0) * each, each)
            taken.append(held[pl.ds(start, each), :])
        chosen = jnp.concatenate(taken, axis=0).astype(BF16)
        out[0] = nn(chosen, weight[...]).astype(BF16)

    return pl.pallas_call(
        body,
        grid=(count,),
        in_specs=[
            pl.BlockSpec(array.shape, lambda d, rank=array.ndim: (0,) * rank)
            for array in operands
        ],
        out_specs=pl.BlockSpec((1, size, wide), lambda d: (d, 0, 0)),
        out_shape=jax.ShapeDtypeStruct((count, size, wide), BF16),
        scratch_shapes=[
            pltpu.VMEM((tokens, 3 * group), F32),
            pltpu.VMEM((3 * group, wide), BF16),
        ],
        name="project",
        cost_estimate=cost(2 << 30, 6 << 20, 0),
        compiler_params=pltpu.CompilerParams(vmem_limit_bytes=VMEM),
    )(*operands)


def spread(pieces, columns):
    count, tokens, wide = pieces.shape
    width = wide // 4

    def body(in_ref, out):
        total = in_ref[0].astype(F32)
        for at in range(1, count):
            total += in_ref[at].astype(F32)
        total = total.astype(BF16)
        cells = 2 * tokens
        fine = lax.broadcasted_iota(jnp.int32, (cells, tokens), 0)
        token = lax.broadcasted_iota(jnp.int32, (cells, tokens), 1)
        cell = (token & 7) * 2 * columns + (token >> 3) * 2
        for a in range(2):
            grid = jnp.zeros((cells, width), F32)
            for b in range(2):
                place = jnp.where(fine == cell + b, 1.0, 0.0).astype(BF16)
                lanes = slice((2 * a + b) * width, (2 * a + b + 1) * width)
                grid += nn(place, total[:, lanes])
            grid = grid.astype(BF16)
            for row in range(tokens // columns):
                at = (2 * row + a) * 2 * columns
                out[at : at + 2 * columns, :] = grid[row * 2 * columns : (row + 1) * 2 * columns]

    return whole_call(
        body,
        jax.ShapeDtypeStruct((4 * tokens, width), BF16),
        "spread",
        1 << 28,
        [],
        pieces,
    )


def shifted(array, axis, step):
    count = lax.axis_size(axis)
    return lax.ppermute(array, axis, [(i, (i + step) % count) for i in range(count)])


def swapped(array, axis):
    return lax.ppermute(array, axis, [(0, 1), (1, 0)])


def onward(low, high, axis):
    count = lax.axis_size(axis)
    forward = [(i, i + 1) for i in range(count - 1)]
    backward = [(i + 1, i) for i in range(count - 1)]
    return lax.ppermute(low, axis, forward), lax.ppermute(high, axis, backward)


def exchanged(inner, outer, axis):
    count = lax.axis_size(axis)
    beside = [(i, i ^ 1) for i in range(count)]
    beyond = [(i, ((i + 1) ^ 1) - 1) for i in range(1, count - 1)]
    return lax.ppermute(inner, axis, beside), lax.ppermute(outer, axis, beyond)


def edges(block, axis, at):
    size = block.shape[at]
    return onward(
        lax.slice_in_dim(block, size - RIM, None, axis=at),
        lax.slice_in_dim(block, 0, RIM, axis=at),
        axis,
    )


def with_rows(block, dim):
    low, high = edges(block, ROW, dim)
    return jnp.concatenate([low, block, high], axis=dim)


def with_columns(block, dim):
    low, high = edges(block, COL, dim + 1)
    shape = block.shape[:dim] + (-1, block.shape[-1])
    return block.reshape(shape), low.reshape(shape), high.reshape(shape)


def shards(fine_qkv, coarse_qkv, grad_coarse, merge_weight, qkv_weight):
    rows, columns, width = fine_qkv.shape[1:]
    own = rows * columns
    coarse_columns, coarse_rows, group = grad_coarse.shape
    tokens = coarse_columns * coarse_rows

    key_value, query_up = prepare(
        coarse_qkv.reshape(3, tokens, group), grad_coarse.reshape(tokens, group)
    )
    across = swapped(key_value, "zl")
    beside = swapped(key_value, "c")
    queries = [query_up] + [shifted(query_up, "y", step) for step in (1, 2, 3)]
    across, merge_weight, fine_qkv = lax.optimization_barrier((across, merge_weight, fine_qkv))
    corner = swapped(across, "c")
    joint = lax.dot_general(
        qkv_weight, merge_weight, (((1,), (1,)), ((), ())), preferred_element_type=F32
    ).astype(BF16)
    own_qkv = fine_qkv.reshape(3, own, width)
    tall = with_rows(fine_qkv[1:], 1)
    corner, joint = lax.optimization_barrier((corner, joint))
    keys = [key_value, beside, across, corner]

    near = [0, 1, 3]
    part = coarse_stats(keys, [queries[i] for i in near], near, (), 256)
    part = coarse_stats(keys, [queries[2]], [2], (part,), 256)
    stats = lax.all_gather(part, "y", axis=0)
    kept, sent, *query_grads = coarse_grads(keys, queries, stats)

    from_core = swapped(sent, "c")
    query_pieces = [query_grads[0]]
    for step in (1, 2, 3):
        query_pieces.append(shifted(query_grads[step], "y", -step))
    passed = (kept[:, 1].astype(F32) + from_core[:, 1].astype(F32)).astype(BF16)
    arrived = swapped(passed, "zl")
    count = lax.axis_size(ROW)
    projected = project(
        query_pieces, kept, from_core, arrived, joint, coarse_columns, count
    )
    projected, tall = lax.optimization_barrier((projected, tall))
    ext_kv = with_columns(tall, 1)
    pieces = lax.all_to_all(projected, ROW, 0, 0)
    own_up = spread(pieces, coarse_columns)

    grad_query, mid, inner, outer = fine_grads(own_qkv, ext_kv, own_up, rows, columns)
    inner, outer = exchanged(inner, outer, COL)
    middle, inner, outer = add_columns(mid, inner, outer, columns)
    inner, outer = exchanged(inner, outer, ROW)
    grad_key, grad_value = add_rows(middle, inner, outer)
    shape = (rows, columns, width)
    return grad_query.reshape(shape), grad_key.reshape(shape), grad_value.reshape(shape)


def solution(mesh):
    split = Mesh(mesh.devices.reshape(4, 2, 2, 4, 2), ROW + COL)
    return jax.shard_map(
        shards,
        mesh=split,
        in_specs=(
            P(None, ROW, COL, None),
            P(None, COL, None, ROW),
            P(COL, None, ROW),
            P(),
            P(None, None, ROW),
        ),
        out_specs=(P(ROW, COL, None), P(ROW, COL, None), P(ROW, COL, None)),
        check_vma=False,
    )
```

```python
import jax
import jax.numpy as jnp
from jax import lax
from jax.experimental import pallas as pl
from jax.experimental.pallas import tpu as pltpu
from jax.sharding import Mesh
from jax.sharding import PartitionSpec as P

HD = 64
RADIUS = 7
SCALE = 0.125
SIDE = 32
RIM = 8
HIDDEN = -1e30
ROW = ("x", "zh")
COL = ("zl", "y", "c")
F32 = jnp.float32
BF16 = jnp.bfloat16
VMEM = 60 << 20


def nt(left, right):
    return lax.dot_general(left, right, (((1,), (1,)), ((), ())), preferred_element_type=F32)


def nn(left, right):
    return lax.dot_general(left, right, (((1,), (0,)), ((), ())), preferred_element_type=F32)


def half(pair, which):
    lane = lax.broadcasted_iota(jnp.int32, pair.shape, 1)
    return jnp.where((lane < HD) == (which == 0), pair, jnp.zeros_like(pair))


def cost(flops, bytes_accessed, exps):
    return pl.CostEstimate(flops=flops, bytes_accessed=bytes_accessed, transcendentals=exps)


def prepare(coarse_qkv, grad_coarse):
    _, tokens, group = coarse_qkv.shape
    heads = group // HD

    def body(qkv_ref, up_ref, kv_out, qu_out):
        for head in range(heads):
            lanes = slice(head * HD, head * HD + HD)
            kv_out[head] = jnp.concatenate([qkv_ref[1, :, lanes], qkv_ref[2, :, lanes]], axis=1)
            qu_out[head] = jnp.concatenate([qkv_ref[0, :, lanes], up_ref[:, lanes]], axis=1)

    return whole_call(
        body,
        [jax.ShapeDtypeStruct((heads, tokens, 2 * HD), BF16)] * 2,
        "prepare",
        1 << 20,
        [],
        coarse_qkv,
        grad_coarse,
    )


def own_block(step, tokens):
    owner = lax.axis_index("y") ^ step
    return pl.ds(pl.multiple_of(owner * tokens, tokens), tokens)


def coarse_stats(key_values, query_ups, steps, before, key_tile):
    heads, tokens, _ = key_values[0].shape
    blocks, number = len(key_values), len(query_ups)
    per_block = tokens // key_tile

    def body(*refs):
        kv_refs, qu_refs = refs[:blocks], refs[blocks : blocks + number]
        out_ref, held = refs[-2:]
        if before:

            @pl.when(pl.program_id(1) == 0)
            def _():
                out_ref[...] = refs[blocks + number][...]

        for at in range(number):

            @pl.when(pl.program_id(1) == at)
            def _():
                held[...] = qu_refs[at][0]

        query = half(held[...], 0) * BF16(SCALE)
        upstream = half(held[...], 1)
        peak = jnp.full((1, tokens), -jnp.inf, F32)
        total = jnp.zeros((1, tokens), F32)
        weighted = jnp.zeros((1, tokens), F32)
        for i in range(blocks * per_block):
            start = (i % per_block) * key_tile
            tile = kv_refs[i // per_block][0, start : start + key_tile, :]
            score = nt(tile, query)
            product = nt(tile, upstream)
            new_peak = jnp.maximum(peak, jnp.max(score, axis=0, keepdims=True))
            decay = jnp.exp(peak - new_peak)
            share = jnp.exp(score - new_peak)
            total = total * decay + jnp.sum(share, axis=0, keepdims=True)
            weighted = weighted * decay + jnp.sum(share * product, axis=0, keepdims=True)
            peak = new_peak
        found = jnp.concatenate([peak + jnp.log(total), weighted / total], axis=0)
        for at, step in enumerate(steps):

            @pl.when(pl.program_id(1) == at)
            def _():
                out_ref[0, :, own_block(step, tokens)] = found

    pairs = heads * number * blocks * tokens**2
    return pl.pallas_call(
        body,
        grid=(heads, number),
        in_specs=[pl.BlockSpec((1, tokens, 128), lambda h, q: (h, 0, 0))] * (blocks + number)
        + [pl.BlockSpec((1, 2, blocks * tokens), lambda h, q: (h, 0, 0))] * len(before),
        out_specs=pl.BlockSpec((1, 2, blocks * tokens), lambda h, q: (h, 0, 0)),
        out_shape=jax.ShapeDtypeStruct((heads, 2, blocks * tokens), F32),
        scratch_shapes=[pltpu.VMEM((tokens, 128), BF16)],
        name="coarse_stats",
        cost_estimate=cost(4 * pairs * 256, 2 << 20, pairs),
        compiler_params=pltpu.CompilerParams(vmem_limit_bytes=VMEM),
    )(*key_values, *query_ups, *before)


def coarse_grads(key_values, query_ups, stats):
    heads, tokens, _ = key_values[0].shape
    blocks = len(query_ups)
    parts = len(stats)

    def body(*refs):
        kv_refs, qu_refs = refs[:blocks], refs[blocks : 2 * blocks]
        stats_refs = refs[2 * blocks : 2 * blocks + parts]
        kept_ref, sent_ref = refs[2 * blocks + parts : 2 * blocks + parts + 2]
        q_outs = refs[-blocks - 2 : -2]
        acc, held = refs[-2:]
        step = pl.program_id(1)
        for at in range(blocks):

            @pl.when(pl.program_id(1) == at)
            def _():
                held[...] = qu_refs[at][0]

        @pl.when(pl.program_id(1) == 0)
        def _():
            acc[...] = jnp.zeros_like(acc)

        query = half(held[...], 0) * BF16(SCALE)
        upstream = half(held[...], 1)
        found = [ref[0, :, own_block(step, tokens)] for ref in stats_refs]
        peak = found[0][:1]
        for part in found[1:]:
            peak = jnp.maximum(peak, part[:1])
        shares = [jnp.exp(part[:1] - peak) for part in found]
        total = sum(shares)
        log_total = peak + jnp.log(total)
        delta = sum(share * part[1:] for share, part in zip(shares, found)) / total
        found = jnp.zeros((HD, tokens), F32)
        for i in range(blocks):
            tile = kv_refs[i][0]
            share = jnp.exp(nt(tile, query) - log_total)
            grads = (share * (nt(tile, upstream) - delta)).astype(BF16)
            acc[i] += nn(grads, query) + nn(share.astype(BF16), upstream)
            found += nn(tile[:, :HD].T, grads)
        found = (found * SCALE).astype(BF16)
        for at in range(blocks):

            @pl.when(pl.program_id(1) == at)
            def _():
                q_outs[at][...] = found

        @pl.when(pl.program_id(1) == blocks - 1)
        def _():
            for i in range(blocks // 2):
                kept_ref[i, 0] = acc[2 * i].astype(BF16)
                sent_ref[i, 0] = acc[2 * i + 1].astype(BF16)

    pairs = heads * (blocks * tokens) ** 2
    out_shape = [jax.ShapeDtypeStruct((blocks // 2, heads, tokens, 128), BF16)] * 2
    out_shape += [jax.ShapeDtypeStruct((heads * HD, tokens), BF16)] * blocks
    return pl.pallas_call(
        body,
        grid=(heads, blocks),
        in_specs=[pl.BlockSpec((1, tokens, 128), lambda h, q: (h, 0, 0))] * (2 * blocks)
        + [pl.BlockSpec((1, 2, blocks * tokens), lambda h, q: (h, 0, 0))] * parts,
        out_specs=[pl.BlockSpec((blocks // 2, 1, tokens, 128), lambda h, q: (0, h, 0, 0))] * 2
        + [pl.BlockSpec((HD, tokens), lambda h, q: (h, 0))] * blocks,
        out_shape=out_shape,
        scratch_shapes=[
            pltpu.VMEM((blocks, tokens, 128), F32),
            pltpu.VMEM((tokens, 128), BF16),
        ],
        name="coarse_grads",
        cost_estimate=cost(10 * pairs * 256, 4 << 20, pairs),
        compiler_params=pltpu.CompilerParams(vmem_limit_bytes=VMEM),
    )(*key_values, *query_ups, *stats)


def whole_call(body, out_shape, name, flops, scratch, *operands):
    return pl.pallas_call(
        body,
        out_shape=out_shape,
        scratch_shapes=scratch,
        name=name,
        cost_estimate=cost(flops, 6 << 20, 1 << 20),
        compiler_params=pltpu.CompilerParams(vmem_limit_bytes=VMEM),
    )(*operands)


def pairs_of(width):
    return [(pair, slice(pair * 128, pair * 128 + 128)) for pair in range(width // 128)]


def window_bias(own, rows, columns, part, transposed):
    count = SIDE * SIDE // 2
    shape = (own, count) if transposed else (count, own)
    ext = lax.broadcasted_iota(jnp.int32, shape, 1 if transposed else 0)
    inner = lax.broadcasted_iota(jnp.int32, shape, 0 if transposed else 1)
    if part == 0:
        ext_row, ext_column = ext >> 4, (ext & 15) + RIM
    else:
        ext_row = (ext & 255) >> 3
        ext_column = (ext & 7) + jnp.where(ext >= 256, SIDE - RIM, 0)
    row_gap = ext_row - (inner >> 4) - RIM
    column_gap = ext_column - (inner & 15) - RIM
    row = ext_row + (lax.axis_index(ROW) * rows - RIM)
    column = ext_column + (lax.axis_index(COL) * columns - RIM)
    seen = (jnp.abs(row_gap) <= RADIUS) & (jnp.abs(column_gap) <= RADIUS)
    seen &= (row >= 0) & (row < lax.axis_size(ROW) * rows)
    seen &= (column >= 0) & (column < lax.axis_size(COL) * columns)
    return jnp.where(seen, 0.0, HIDDEN).astype(F32)


def fill_bias(bias_ref, own, rows, columns):
    count = SIDE * SIDE // 2
    for part in range(2):
        bias_ref[part * count : (part + 1) * count, :] = window_bias(
            own, rows, columns, part, False
        )


def stacked(refs, which, lanes):
    return jnp.concatenate([ref[which, :, lanes] for ref in refs], axis=0)


def fine_grads(own_qkv, ext_kv, own_up, rows, columns):
    _, own, width = own_qkv.shape
    sizes = [ref.shape[1] for ref in ext_kv]
    places = [sum(sizes[:i]) for i in range(len(sizes))]

    def body(q_ref, mid_ref, low_ref, high_ref, up_ref, q_out, mid_out, *rest):
        inner_out, outer_out, bias_ref = rest
        first = lax.axis_index("c") == 0
        fill_bias(bias_ref, own, rows, columns)
        ext = (mid_ref, low_ref, high_ref)
        for pair, lanes in pairs_of(width):
            key = stacked(ext, 0, lanes)
            key_t = key.T
            value = stacked(ext, 1, lanes)
            parts = []
            key_sum = jnp.zeros((SIDE * SIDE, 128), F32)
            value_sum = jnp.zeros((SIDE * SIDE, 128), F32)
            for side in range(2):
                query = half(q_ref[0, :, lanes], side) * BF16(SCALE)
                up = half(up_ref[:, lanes], side)
                score = nt(key, query) + bias_ref[...]
                product = nt(value, up)
                share = jnp.exp(score - jnp.max(score, axis=0, keepdims=True))
                total = jnp.sum(share, axis=0, keepdims=True)
                delta = jnp.sum(share * product, axis=0, keepdims=True) / total
                share = share * (1.0 / total)
                grads = (share * (product - delta)).astype(BF16)
                key_sum += nn(grads, query)
                value_sum += nn(share.astype(BF16), up)
                parts.append(nn(key_t[side * HD : side * HD + HD], grads))
            q_out[:, lanes] = (jnp.concatenate(parts, axis=0).T * SCALE).astype(BF16)
            right = slice(width + pair * 128, width + pair * 128 + 128)
            for at, total in ((lanes, key_sum), (right, value_sum)):
                mid, low, high = [
                    total[place : place + size] for place, size in zip(places, sizes)
                ]
                mid_out[:, at] = mid
                inner_out[:, at] = jnp.where(first, high, low).astype(BF16)
                outer_out[:, at] = jnp.where(first, low, high).astype(BF16)

    return whole_call(
        body,
        [jax.ShapeDtypeStruct((own, width), BF16)]
        + [
            jax.ShapeDtypeStruct((size, 2 * width), BF16 if i else F32)
            for i, size in enumerate(sizes)
        ],
        "fine_grads",
        2 << 30,
        [pltpu.VMEM((SIDE * SIDE, own), F32)],
        own_qkv,
        *ext_kv,
        own_up,
    )


def add_columns(mid, inner, outer, columns):
    cells, wide = mid.shape
    tall = cells // columns
    edge = RIM * columns

    def body(mid_ref, inner_ref, outer_ref, own_out, inner_out, outer_out):
        first = lax.axis_index("c") == 0
        inner = inner_ref[...].astype(F32).reshape(tall, RIM, wide)
        outer = outer_ref[...].astype(F32).reshape(tall, RIM, wide)
        left, right = jnp.where(first, outer, inner), jnp.where(first, inner, outer)
        both = jnp.concatenate([left, right], axis=1).reshape(cells, wide)
        total = mid_ref[...] + both
        top, bottom = total[:edge], total[cells - edge :]
        upper = lax.axis_index("zh") == 0
        own_out[...] = total[edge : cells - edge]
        inner_out[...] = jnp.where(upper, bottom, top).astype(BF16)
        outer_out[...] = jnp.where(upper, top, bottom).astype(BF16)

    return whole_call(
        body,
        [jax.ShapeDtypeStruct((cells - 2 * edge, wide), F32)]
        + [jax.ShapeDtypeStruct((edge, wide), BF16)] * 2,
        "add_columns",
        1 << 20,
        [],
        mid,
        inner,
        outer,
    )


def add_rows(own, inner, outer):
    cells, wide = own.shape
    width = wide // 2

    def body(own_ref, inner_ref, outer_ref, k_out, v_out):
        upper = lax.axis_index("zh") == 0
        inner = inner_ref[...].astype(F32)
        outer = outer_ref[...].astype(F32)
        above, below = jnp.where(upper, outer, inner), jnp.where(upper, inner, outer)
        total = own_ref[...] + jnp.concatenate([above, below], axis=0)
        k_out[...] = total[:, :width].astype(BF16)
        v_out[...] = total[:, width:].astype(BF16)

    return whole_call(
        body,
        [jax.ShapeDtypeStruct((cells, width), BF16)] * 2,
        "add_rows",
        1 << 20,
        [],
        own,
        inner,
        outer,
    )


def project(query_pieces, kept, from_core, arrived, joint, columns, count):
    group, tokens = query_pieces[0].shape
    heads = arrived.shape[0]
    rows = tokens // columns
    each = rows // count
    size = each * columns
    wide = joint.shape[1]
    first = count // 2
    operands = (*query_pieces, kept, from_core, arrived, joint)
    params = pltpu.CompilerParams(vmem_limit_bytes=VMEM)

    def whole(array):
        return pl.BlockSpec(array.shape, lambda d: (0,) * array.ndim)

    def pack(*refs):
        pieces = refs[: len(query_pieces)]
        kept_ref, core_ref, arrived_ref, joint_ref = refs[len(query_pieces) :][:4]
        outs, packed, held = refs[len(operands) : -2], refs[-2], refs[-1]

        @pl.when(pl.program_id(0) == 0)
        def _():
            for head in range(heads):
                total = kept_ref[0, head].astype(F32) + core_ref[0, head].astype(F32)
                total += arrived_ref[head].astype(F32)
                for part in range(2):
                    at = (1 + part) * group + head * HD
                    held[:, at : at + HD] = total[:, part * HD : (part + 1) * HD]
            total = pieces[0][...].astype(F32)
            for piece in pieces[1:]:
                total += piece[...].astype(F32)
            held[:, :group] = total.T
            for step in range(count):
                target = lax.axis_index(ROW) ^ (count - 1 - step)
                taken = []
                for c in range(columns):
                    start = pl.multiple_of(c * rows + target * each, each)
                    taken.append(held[pl.ds(start, each), :])
                packed[step] = jnp.concatenate(taken, axis=0).astype(BF16)

        for step, out in enumerate(outs):

            @pl.when(pl.program_id(0) == step)
            def _():
                out[...] = nn(packed[step], joint_ref[...]).astype(BF16)

    def rest(packed, joint_ref, *outs):
        for step, out in enumerate(outs):

            @pl.when(pl.program_id(0) == step)
            def _():
                out[...] = nn(packed[first + step], joint_ref[...]).astype(BF16)

    piece = jax.ShapeDtypeStruct((size, wide), BF16)
    packed = jax.ShapeDtypeStruct((count, size, 3 * group), BF16)
    early = pl.pallas_call(
        pack,
        grid=(first,),
        in_specs=[whole(array) for array in operands],
        out_specs=[whole(piece)] * first + [whole(packed)],
        out_shape=[piece] * first + [packed],
        scratch_shapes=[pltpu.VMEM((tokens, 3 * group), F32)],
        name="project",
        cost_estimate=cost(1 << 30, 6 << 20, 0),
        compiler_params=params,
    )(*operands)
    late = pl.pallas_call(
        rest,
        grid=(count - first,),
        in_specs=[whole(packed), whole(joint)],
        out_specs=[whole(piece)] * (count - first),
        out_shape=[piece] * (count - first),
        name="project_rest",
        cost_estimate=cost(1 << 30, 3 << 20, 0),
        compiler_params=params,
    )(early[-1], joint)
    return [*early[:-1], *late]


def spread(pieces, columns):
    tokens, wide = pieces[0].shape
    width = wide // 4

    def body(*refs):
        out = refs[-1]
        total = refs[0][...].astype(F32)
        for ref in refs[1:-1]:
            total += ref[...].astype(F32)
        total = total.astype(BF16)
        cells = 2 * tokens
        fine = lax.broadcasted_iota(jnp.int32, (cells, tokens), 0)
        token = lax.broadcasted_iota(jnp.int32, (cells, tokens), 1)
        cell = (token & 7) * 2 * columns + (token >> 3) * 2
        for a in range(2):
            grid = jnp.zeros((cells, width), F32)
            for b in range(2):
                place = jnp.where(fine == cell + b, 1.0, 0.0).astype(BF16)
                lanes = slice((2 * a + b) * width, (2 * a + b + 1) * width)
                grid += nn(place, total[:, lanes])
            grid = grid.astype(BF16)
            for row in range(tokens // columns):
                at = (2 * row + a) * 2 * columns
                out[at : at + 2 * columns, :] = grid[row * 2 * columns : (row + 1) * 2 * columns]

    return whole_call(
        body,
        jax.ShapeDtypeStruct((4 * tokens, width), BF16),
        "spread",
        1 << 28,
        [],
        *pieces,
    )


def swapped(array, axis, flip=1):
    return lax.ppermute(array, axis, [(i, i ^ flip) for i in range(lax.axis_size(axis))])


def exchanged(inner, outer, axis):
    count = lax.axis_size(axis)
    beyond = [(i, ((i + 1) ^ 1) - 1) for i in range(1, count - 1)]
    return swapped(inner, axis), lax.ppermute(outer, axis, beyond)


def rims(block, axis, parity, at):
    size = block.shape[at]
    low = lax.slice_in_dim(block, 0, RIM, axis=at)
    high = lax.slice_in_dim(block, size - RIM, None, axis=at)
    first = lax.axis_index(parity) == 0
    inner, outer = exchanged(
        jnp.where(first, high, low), jnp.where(first, low, high), axis
    )
    return jnp.where(first, outer, inner), jnp.where(first, inner, outer)


def with_rows(block, dim):
    low, high = rims(block, ROW, "zh", dim)
    return jnp.concatenate([low, block, high], axis=dim)


def with_columns(block, dim):
    low, high = rims(block, COL, "c", dim + 1)
    shape = block.shape[:dim] + (-1, block.shape[-1])
    return block.reshape(shape), low.reshape(shape), high.reshape(shape)


def shards(fine_qkv, coarse_qkv, grad_coarse, merge_weight, qkv_weight):
    rows, columns, width = fine_qkv.shape[1:]
    own = rows * columns
    coarse_columns, coarse_rows, group = grad_coarse.shape
    tokens = coarse_columns * coarse_rows
    wide = merge_weight.shape[0]

    key_value, query_up = prepare(
        coarse_qkv.reshape(3, tokens, group), grad_coarse.reshape(tokens, group)
    )
    across = swapped(key_value, "zl")
    beside = swapped(key_value, "c")
    queries = [query_up] + [swapped(query_up, "y", step) for step in (1, 2, 3)]
    across, merge_weight, fine_qkv = lax.optimization_barrier((across, merge_weight, fine_qkv))
    corner = swapped(across, "c")
    joint = lax.dot_general(
        qkv_weight, merge_weight, (((1,), (1,)), ((), ())), preferred_element_type=F32
    ).astype(BF16).reshape(3 * group, wide)
    own_qkv = fine_qkv.reshape(3, own, width)
    tall = with_rows(fine_qkv[1:], 1)
    corner, joint, tall = lax.optimization_barrier((corner, joint, tall))
    keys = [key_value, beside, across, corner]

    near = [0, 1, 3]
    part = coarse_stats(keys, [queries[i] for i in near], near, (), 256)
    part = coarse_stats(keys, [queries[2]], [2], (part,), 256)
    stats = [part] + [swapped(part, "y", step) for step in (1, 2, 3)]
    kept, sent, *query_grads = coarse_grads(keys, queries, stats)

    from_core = swapped(sent, "c")
    passed = (kept[1].astype(F32) + from_core[1].astype(F32)).astype(BF16)
    arrived = swapped(passed, "zl")
    query_pieces = [query_grads[0]]
    for step in (1, 2, 3):
        query_pieces.append(swapped(query_grads[step], "y", step))
    count = lax.axis_size(ROW)
    projected = project(
        query_pieces, kept, from_core, arrived, joint, coarse_columns, count
    )
    pieces = [
        swapped(piece, ROW, count - 1 - step) for step, piece in enumerate(projected[:-1])
    ]
    kept_piece, tall = lax.optimization_barrier((projected[-1], tall))
    ext_kv = with_columns(tall, 1)
    own_up = spread([kept_piece, *pieces], coarse_columns)

    grad_query, mid, inner, outer = fine_grads(own_qkv, ext_kv, own_up, rows, columns)
    inner, outer = exchanged(inner, outer, COL)
    middle, inner, outer = add_columns(mid, inner, outer, columns)
    inner, outer = exchanged(inner, outer, ROW)
    grad_key, grad_value = add_rows(middle, inner, outer)
    shape = (rows, columns, width)
    return grad_query.reshape(shape), grad_key.reshape(shape), grad_value.reshape(shape)


def solution(mesh):
    split = Mesh(mesh.devices.reshape(4, 2, 2, 4, 2), ROW + COL)
    return jax.shard_map(
        shards,
        mesh=split,
        in_specs=(
            P(None, ROW, COL, None),
            P(None, COL, None, ROW),
            P(COL, None, ROW),
            P(),
            P(None, None, ROW),
        ),
        out_specs=(P(ROW, COL, None), P(ROW, COL, None), P(ROW, COL, None)),
        check_vma=False,
    )
```

```python
import jax
import jax.numpy as jnp
from jax import lax
from jax.experimental import pallas as pl
from jax.experimental.pallas import tpu as pltpu
from jax.sharding import Mesh
from jax.sharding import PartitionSpec as P

HD = 64
RADIUS = 7
SCALE = 0.125
SIDE = 32
RIM = 8
HIDDEN = -1e30
ROW = ("x", "zh")
COL = ("zl", "y", "c")
F32 = jnp.float32
BF16 = jnp.bfloat16
VMEM = 60 << 20


def nt(left, right):
    return lax.dot_general(left, right, (((1,), (1,)), ((), ())), preferred_element_type=F32)


def nn(left, right):
    return lax.dot_general(left, right, (((1,), (0,)), ((), ())), preferred_element_type=F32)


def half(pair, which):
    lane = lax.broadcasted_iota(jnp.int32, pair.shape, 1)
    return jnp.where((lane < HD) == (which == 0), pair, jnp.zeros_like(pair))


def cost(flops, bytes_accessed, exps):
    return pl.CostEstimate(flops=flops, bytes_accessed=bytes_accessed, transcendentals=exps)


def prepare(coarse_qkv, grad_coarse):
    _, tokens, group = coarse_qkv.shape
    heads = group // HD

    def body(qkv_ref, up_ref, kv_out, qu_out):
        for head in range(heads):
            lanes = slice(head * HD, head * HD + HD)
            kv_out[head] = jnp.concatenate([qkv_ref[1, :, lanes], qkv_ref[2, :, lanes]], axis=1)
            qu_out[head] = jnp.concatenate([qkv_ref[0, :, lanes], up_ref[:, lanes]], axis=1)

    return whole_call(
        body,
        [jax.ShapeDtypeStruct((heads, tokens, 2 * HD), BF16)] * 2,
        "prepare",
        1 << 20,
        [],
        coarse_qkv,
        grad_coarse,
    )


def own_block(step, tokens):
    owner = lax.axis_index("y") ^ step
    return pl.ds(pl.multiple_of(owner * tokens, tokens), tokens)


def coarse_stats(key_values, query_ups, steps, before, key_tile):
    heads, tokens, _ = key_values[0].shape
    blocks, number = len(key_values), len(query_ups)
    per_block = tokens // key_tile

    def body(*refs):
        kv_refs, qu_refs = refs[:blocks], refs[blocks : blocks + number]
        out_ref, held = refs[-2:]
        if before:

            @pl.when(pl.program_id(1) == 0)
            def _():
                out_ref[...] = refs[blocks + number][...]

        for at in range(number):

            @pl.when(pl.program_id(1) == at)
            def _():
                held[...] = qu_refs[at][0]

        query = half(held[...], 0) * BF16(SCALE)
        upstream = half(held[...], 1)
        peak = jnp.full((1, tokens), -jnp.inf, F32)
        total = jnp.zeros((1, tokens), F32)
        weighted = jnp.zeros((1, tokens), F32)
        for i in range(blocks * per_block):
            start = (i % per_block) * key_tile
            tile = kv_refs[i // per_block][0, start : start + key_tile, :]
            score = nt(tile, query)
            product = nt(tile, upstream)
            new_peak = jnp.maximum(peak, jnp.max(score, axis=0, keepdims=True))
            decay = jnp.exp(peak - new_peak)
            share = jnp.exp(score - new_peak)
            total = total * decay + jnp.sum(share, axis=0, keepdims=True)
            weighted = weighted * decay + jnp.sum(share * product, axis=0, keepdims=True)
            peak = new_peak
        found = jnp.concatenate([peak + jnp.log(total), weighted / total], axis=0)
        for at, step in enumerate(steps):

            @pl.when(pl.program_id(1) == at)
            def _():
                out_ref[0, :, own_block(step, tokens)] = found

    pairs = heads * number * blocks * tokens**2
    return pl.pallas_call(
        body,
        grid=(heads, number),
        in_specs=[pl.BlockSpec((1, tokens, 128), lambda h, q: (h, 0, 0))] * (blocks + number)
        + [pl.BlockSpec((1, 2, blocks * tokens), lambda h, q: (h, 0, 0))] * len(before),
        out_specs=pl.BlockSpec((1, 2, blocks * tokens), lambda h, q: (h, 0, 0)),
        out_shape=jax.ShapeDtypeStruct((heads, 2, blocks * tokens), F32),
        scratch_shapes=[pltpu.VMEM((tokens, 128), BF16)],
        name="coarse_stats",
        cost_estimate=cost(4 * pairs * 256, 2 << 20, pairs),
        compiler_params=pltpu.CompilerParams(vmem_limit_bytes=VMEM),
    )(*key_values, *query_ups, *before)


def coarse_grads(key_values, query_ups, stats):
    heads, tokens, _ = key_values[0].shape
    blocks = len(query_ups)
    parts = len(stats)

    def body(*refs):
        kv_refs, qu_refs = refs[:blocks], refs[blocks : 2 * blocks]
        stats_refs = refs[2 * blocks : 2 * blocks + parts]
        kept_ref, sent_ref = refs[2 * blocks + parts : 2 * blocks + parts + 2]
        q_outs = refs[-blocks - 2 : -2]
        acc, held = refs[-2:]
        step = pl.program_id(1)
        for at in range(blocks):

            @pl.when(pl.program_id(1) == at)
            def _():
                held[...] = qu_refs[at][0]

        @pl.when(pl.program_id(1) == 0)
        def _():
            acc[...] = jnp.zeros_like(acc)

        query = half(held[...], 0) * BF16(SCALE)
        upstream = half(held[...], 1)
        found = [ref[0, :, own_block(step, tokens)] for ref in stats_refs]
        peak = found[0][:1]
        for part in found[1:]:
            peak = jnp.maximum(peak, part[:1])
        shares = [jnp.exp(part[:1] - peak) for part in found]
        total = sum(shares)
        log_total = peak + jnp.log(total)
        delta = sum(share * part[1:] for share, part in zip(shares, found)) / total
        found = jnp.zeros((HD, tokens), F32)
        for i in range(blocks):
            tile = kv_refs[i][0]
            share = jnp.exp(nt(tile, query) - log_total)
            grads = (share * (nt(tile, upstream) - delta)).astype(BF16)
            acc[i] += nn(grads, query) + nn(share.astype(BF16), upstream)
            found += nn(tile[:, :HD].T, grads)
        found = (found * SCALE).astype(BF16)
        for at in range(blocks):

            @pl.when(pl.program_id(1) == at)
            def _():
                q_outs[at][...] = found

        @pl.when(pl.program_id(1) == blocks - 1)
        def _():
            for i in range(blocks // 2):
                kept_ref[i, 0] = acc[2 * i].astype(BF16)
                sent_ref[i, 0] = acc[2 * i + 1].astype(BF16)

    pairs = heads * (blocks * tokens) ** 2
    out_shape = [jax.ShapeDtypeStruct((blocks // 2, heads, tokens, 128), BF16)] * 2
    out_shape += [jax.ShapeDtypeStruct((heads * HD, tokens), BF16)] * blocks
    return pl.pallas_call(
        body,
        grid=(heads, blocks),
        in_specs=[pl.BlockSpec((1, tokens, 128), lambda h, q: (h, 0, 0))] * (2 * blocks)
        + [pl.BlockSpec((1, 2, blocks * tokens), lambda h, q: (h, 0, 0))] * parts,
        out_specs=[pl.BlockSpec((blocks // 2, 1, tokens, 128), lambda h, q: (0, h, 0, 0))] * 2
        + [pl.BlockSpec((HD, tokens), lambda h, q: (h, 0))] * blocks,
        out_shape=out_shape,
        scratch_shapes=[
            pltpu.VMEM((blocks, tokens, 128), F32),
            pltpu.VMEM((tokens, 128), BF16),
        ],
        name="coarse_grads",
        cost_estimate=cost(10 * pairs * 256, 4 << 20, pairs),
        compiler_params=pltpu.CompilerParams(vmem_limit_bytes=VMEM),
    )(*key_values, *query_ups, *stats)


def whole_call(body, out_shape, name, flops, scratch, *operands):
    return pl.pallas_call(
        body,
        out_shape=out_shape,
        scratch_shapes=scratch,
        name=name,
        cost_estimate=cost(flops, 6 << 20, 1 << 20),
        compiler_params=pltpu.CompilerParams(vmem_limit_bytes=VMEM),
    )(*operands)


def pairs_of(width):
    return [(pair, slice(pair * 128, pair * 128 + 128)) for pair in range(width // 128)]


def window_bias(own, rows, columns, part, transposed):
    count = SIDE * SIDE // 2
    shape = (own, count) if transposed else (count, own)
    ext = lax.broadcasted_iota(jnp.int32, shape, 1 if transposed else 0)
    inner = lax.broadcasted_iota(jnp.int32, shape, 0 if transposed else 1)
    if part == 0:
        ext_row, ext_column = ext >> 4, (ext & 15) + RIM
    else:
        ext_row = (ext & 255) >> 3
        ext_column = (ext & 7) + jnp.where(ext >= 256, SIDE - RIM, 0)
    row_gap = ext_row - (inner >> 4) - RIM
    column_gap = ext_column - (inner & 15) - RIM
    row = ext_row + (lax.axis_index(ROW) * rows - RIM)
    column = ext_column + (lax.axis_index(COL) * columns - RIM)
    seen = (jnp.abs(row_gap) <= RADIUS) & (jnp.abs(column_gap) <= RADIUS)
    seen &= (row >= 0) & (row < lax.axis_size(ROW) * rows)
    seen &= (column >= 0) & (column < lax.axis_size(COL) * columns)
    return jnp.where(seen, 0.0, HIDDEN).astype(F32)


def fill_bias(bias_ref, own, rows, columns):
    count = SIDE * SIDE // 2
    for part in range(2):
        bias_ref[part * count : (part + 1) * count, :] = window_bias(
            own, rows, columns, part, False
        )


def stacked(refs, which, lanes):
    return jnp.concatenate([ref[which, :, lanes] for ref in refs], axis=0)


def fine_grads(own_qkv, ext_kv, own_up, rows, columns):
    _, own, width = own_qkv.shape
    sizes = [ref.shape[1] for ref in ext_kv]
    places = [sum(sizes[:i]) for i in range(len(sizes))]

    def body(q_ref, mid_ref, low_ref, high_ref, up_ref, q_out, mid_out, *rest):
        inner_out, outer_out, bias_ref = rest
        first = lax.axis_index("c") == 0
        fill_bias(bias_ref, own, rows, columns)
        ext = (mid_ref, low_ref, high_ref)
        for pair, lanes in pairs_of(width):
            key = stacked(ext, 0, lanes)
            key_t = key.T
            value = stacked(ext, 1, lanes)
            parts = []
            key_sum = jnp.zeros((SIDE * SIDE, 128), F32)
            value_sum = jnp.zeros((SIDE * SIDE, 128), F32)
            for side in range(2):
                query = half(q_ref[0, :, lanes], side) * BF16(SCALE)
                up = half(up_ref[:, lanes], side)
                score = nt(key, query) + bias_ref[...]
                product = nt(value, up)
                share = jnp.exp(score - jnp.max(score, axis=0, keepdims=True))
                total = jnp.sum(share, axis=0, keepdims=True)
                delta = jnp.sum(share * product, axis=0, keepdims=True) / total
                share = share * (1.0 / total)
                grads = (share * (product - delta)).astype(BF16)
                key_sum += nn(grads, query)
                value_sum += nn(share.astype(BF16), up)
                parts.append(nn(key_t[side * HD : side * HD + HD], grads))
            q_out[:, lanes] = (jnp.concatenate(parts, axis=0).T * SCALE).astype(BF16)
            right = slice(width + pair * 128, width + pair * 128 + 128)
            for at, total in ((lanes, key_sum), (right, value_sum)):
                mid, low, high = [
                    total[place : place + size] for place, size in zip(places, sizes)
                ]
                mid_out[:, at] = mid
                inner_out[:, at] = jnp.where(first, high, low).astype(BF16)
                outer_out[:, at] = jnp.where(first, low, high).astype(BF16)

    return whole_call(
        body,
        [jax.ShapeDtypeStruct((own, width), BF16)]
        + [
            jax.ShapeDtypeStruct((size, 2 * width), BF16 if i else F32)
            for i, size in enumerate(sizes)
        ],
        "fine_grads",
        2 << 30,
        [pltpu.VMEM((SIDE * SIDE, own), F32)],
        own_qkv,
        *ext_kv,
        own_up,
    )


def add_columns(mid, inner, outer, columns):
    cells, wide = mid.shape
    tall = cells // columns
    edge = RIM * columns

    def body(mid_ref, inner_ref, outer_ref, own_out, inner_out, outer_out):
        first = lax.axis_index("c") == 0
        inner = inner_ref[...].astype(F32).reshape(tall, RIM, wide)
        outer = outer_ref[...].astype(F32).reshape(tall, RIM, wide)
        left, right = jnp.where(first, outer, inner), jnp.where(first, inner, outer)
        both = jnp.concatenate([left, right], axis=1).reshape(cells, wide)
        total = mid_ref[...] + both
        top, bottom = total[:edge], total[cells - edge :]
        upper = lax.axis_index("zh") == 0
        own_out[...] = total[edge : cells - edge]
        inner_out[...] = jnp.where(upper, bottom, top).astype(BF16)
        outer_out[...] = jnp.where(upper, top, bottom).astype(BF16)

    return whole_call(
        body,
        [jax.ShapeDtypeStruct((cells - 2 * edge, wide), F32)]
        + [jax.ShapeDtypeStruct((edge, wide), BF16)] * 2,
        "add_columns",
        1 << 20,
        [],
        mid,
        inner,
        outer,
    )


def add_rows(own, inner, outer):
    cells, wide = own.shape
    width = wide // 2

    def body(own_ref, inner_ref, outer_ref, k_out, v_out):
        upper = lax.axis_index("zh") == 0
        inner = inner_ref[...].astype(F32)
        outer = outer_ref[...].astype(F32)
        above, below = jnp.where(upper, outer, inner), jnp.where(upper, inner, outer)
        total = own_ref[...] + jnp.concatenate([above, below], axis=0)
        k_out[...] = total[:, :width].astype(BF16)
        v_out[...] = total[:, width:].astype(BF16)

    return whole_call(
        body,
        [jax.ShapeDtypeStruct((cells, width), BF16)] * 2,
        "add_rows",
        1 << 20,
        [],
        own,
        inner,
        outer,
    )


def project(query_pieces, kept, from_core, arrived, joint, columns, count):
    group, tokens = query_pieces[0].shape
    heads = arrived.shape[0]
    rows = tokens // columns
    each = rows // count
    size = each * columns
    wide = joint.shape[1]
    chunk = 256
    blocks = len(query_pieces)

    def body(*refs):
        pieces = refs[:blocks]
        kept_ref, core_ref, arrived_ref, joint_ref, out, held, packed = refs[blocks:]

        @pl.when(pl.program_id(0) == 0)
        def _():
            for head in range(heads):
                total = kept_ref[0, head].astype(F32) + core_ref[0, head].astype(F32)
                total += arrived_ref[head].astype(F32)
                for part in range(2):
                    at = (1 + part) * group + head * HD
                    held[:, at : at + HD] = total[:, part * HD : (part + 1) * HD]
            total = pieces[0][...].astype(F32)
            for piece in pieces[1:]:
                total += piece[...].astype(F32)
            held[:, :group] = total.T
            for target in range(count):
                taken = []
                for c in range(columns):
                    start = c * rows + target * each
                    taken.append(held[start : start + each, :])
                chosen = jnp.concatenate(taken, axis=0).astype(BF16)
                packed[target * size : (target + 1) * size, :] = chosen

        out[...] = nn(packed[...], joint_ref[...]).astype(BF16)

    half_spec = pl.BlockSpec((1, heads, tokens, 128), lambda n: (0, 0, 0, 0))
    return pl.pallas_call(
        body,
        grid=(wide // chunk,),
        in_specs=[pl.BlockSpec((group, tokens), lambda n: (0, 0))] * blocks
        + [half_spec] * 2
        + [
            pl.BlockSpec(arrived.shape, lambda n: (0, 0, 0)),
            pl.BlockSpec((3 * group, chunk), lambda n: (0, n)),
        ],
        out_specs=pl.BlockSpec((tokens, chunk), lambda n: (0, n)),
        out_shape=jax.ShapeDtypeStruct((tokens, wide), BF16),
        scratch_shapes=[
            pltpu.VMEM((tokens, 3 * group), F32),
            pltpu.VMEM((tokens, 3 * group), BF16),
        ],
        name="project",
        cost_estimate=cost(2 << 30, 6 << 20, 0),
        compiler_params=pltpu.CompilerParams(vmem_limit_bytes=VMEM),
    )(*query_pieces, kept, from_core, arrived, joint)


def spread(pieces, columns):
    count, tokens, wide = pieces.shape
    width = wide // 4

    def body(in_ref, out):
        total = in_ref[0].astype(F32)
        for at in range(1, count):
            total += in_ref[at].astype(F32)
        total = total.astype(BF16)
        cells = 2 * tokens
        fine = lax.broadcasted_iota(jnp.int32, (cells, tokens), 0)
        token = lax.broadcasted_iota(jnp.int32, (cells, tokens), 1)
        cell = (token & 7) * 2 * columns + (token >> 3) * 2
        for a in range(2):
            grid = jnp.zeros((cells, width), F32)
            for b in range(2):
                place = jnp.where(fine == cell + b, 1.0, 0.0).astype(BF16)
                lanes = slice((2 * a + b) * width, (2 * a + b + 1) * width)
                grid += nn(place, total[:, lanes])
            grid = grid.astype(BF16)
            for row in range(tokens // columns):
                at = (2 * row + a) * 2 * columns
                out[at : at + 2 * columns, :] = grid[row * 2 * columns : (row + 1) * 2 * columns]

    return whole_call(
        body,
        jax.ShapeDtypeStruct((4 * tokens, width), BF16),
        "spread",
        1 << 28,
        [],
        pieces,
    )


def swapped(array, axis, flip=1):
    return lax.ppermute(array, axis, [(i, i ^ flip) for i in range(lax.axis_size(axis))])


def exchanged(inner, outer, axis):
    count = lax.axis_size(axis)
    beyond = [(i, ((i + 1) ^ 1) - 1) for i in range(1, count - 1)]
    return swapped(inner, axis), lax.ppermute(outer, axis, beyond)


def sent_rims(block, axis, parity, at):
    size = block.shape[at]
    low = lax.slice_in_dim(block, 0, RIM, axis=at)
    high = lax.slice_in_dim(block, size - RIM, None, axis=at)
    first = lax.axis_index(parity) == 0
    return exchanged(jnp.where(first, high, low), jnp.where(first, low, high), axis)


def placed_rims(inner, outer, parity):
    first = lax.axis_index(parity) == 0
    return jnp.where(first, outer, inner), jnp.where(first, inner, outer)


def shards(fine_qkv, coarse_qkv, grad_coarse, merge_weight, qkv_weight):
    rows, columns, width = fine_qkv.shape[1:]
    own = rows * columns
    coarse_columns, coarse_rows, group = grad_coarse.shape
    tokens = coarse_columns * coarse_rows
    wide = merge_weight.shape[0]

    key_value, query_up = prepare(
        coarse_qkv.reshape(3, tokens, group), grad_coarse.reshape(tokens, group)
    )
    across = swapped(key_value, "zl")
    near = [query_up, swapped(query_up, "y", 1), swapped(query_up, "y", 3)]
    beside = swapped(key_value, "c")
    beside, merge_weight = lax.optimization_barrier((beside, merge_weight))
    joint = lax.dot_general(
        qkv_weight, merge_weight, (((1,), (1,)), ((), ())), preferred_element_type=F32
    ).astype(BF16).reshape(3 * group, wide)
    corner = swapped(across, "c")
    *near, joint = lax.optimization_barrier((*near, joint))
    far = swapped(near[0], "y", 2)
    keys = [key_value, beside, across, corner]
    queries = [near[0], near[1], far, near[2]]

    part = coarse_stats(keys, near, [0, 1, 3], (), 256)
    part, fine_qkv = lax.optimization_barrier((part, fine_qkv))
    own_qkv = fine_qkv.reshape(3, own, width)
    edges = sent_rims(fine_qkv[1:], ROW, "zh", 1)
    part = coarse_stats(keys, [far], [2], (part,), 256)
    part, *edges = lax.optimization_barrier((part, *edges))
    stats = [part] + [swapped(part, "y", step) for step in (1, 3, 2)]
    kept, sent, *query_grads = coarse_grads(keys, queries, stats)

    from_core = swapped(sent, "c")
    passed = (kept[1].astype(F32) + from_core[1].astype(F32)).astype(BF16)
    arrived = swapped(passed, "zl")
    query_pieces = [query_grads[0]]
    for step in (1, 2, 3):
        query_pieces.append(swapped(query_grads[step], "y", step))
    count = lax.axis_size(ROW)
    projected = project(
        query_pieces, kept, from_core, arrived, joint, coarse_columns, count
    )
    projected, *edges = lax.optimization_barrier((projected, *edges))
    pieces = lax.all_to_all(projected.reshape(count, -1, wide), ROW, 0, 0)
    low, high = placed_rims(*edges, "zh")
    tall = jnp.concatenate([low, fine_qkv[1:], high], axis=1)
    low, high = placed_rims(*sent_rims(tall, COL, "c", 2), "c")
    ext_kv = [array.reshape(2, -1, width) for array in (tall, low, high)]
    own_up = spread(pieces, coarse_columns)

    grad_query, mid, inner, outer = fine_grads(own_qkv, ext_kv, own_up, rows, columns)
    inner, outer = exchanged(inner, outer, COL)
    middle, inner, outer = add_columns(mid, inner, outer, columns)
    inner, outer = exchanged(inner, outer, ROW)
    grad_key, grad_value = add_rows(middle, inner, outer)
    shape = (rows, columns, width)
    return grad_query.reshape(shape), grad_key.reshape(shape), grad_value.reshape(shape)


def solution(mesh):
    split = Mesh(mesh.devices.reshape(4, 2, 2, 4, 2), ROW + COL)
    return jax.shard_map(
        shards,
        mesh=split,
        in_specs=(
            P(None, ROW, COL, None),
            P(None, COL, None, ROW),
            P(COL, None, ROW),
            P(),
            P(None, None, ROW),
        ),
        out_specs=(P(ROW, COL, None), P(ROW, COL, None), P(ROW, COL, None)),
        check_vma=False,
    )
```

```python
import jax
import jax.numpy as jnp
from jax import lax
from jax.experimental import pallas as pl
from jax.experimental.pallas import tpu as pltpu
from jax.sharding import Mesh
from jax.sharding import PartitionSpec as P

HD = 64
RADIUS = 7
SCALE = 0.125
SIDE = 32
RIM = 8
HIDDEN = -1e30
ROW = ("x", "zh")
COL = ("zl", "y", "c")
F32 = jnp.float32
BF16 = jnp.bfloat16
VMEM = 60 << 20


def nt(left, right):
    return lax.dot_general(left, right, (((1,), (1,)), ((), ())), preferred_element_type=F32)


def nn(left, right):
    return lax.dot_general(left, right, (((1,), (0,)), ((), ())), preferred_element_type=F32)


def half(pair, which):
    lane = lax.broadcasted_iota(jnp.int32, pair.shape, 1)
    return jnp.where((lane < HD) == (which == 0), pair, jnp.zeros_like(pair))


def cost(flops, bytes_accessed, exps):
    return pl.CostEstimate(flops=flops, bytes_accessed=bytes_accessed, transcendentals=exps)


def prepare(coarse_qkv, grad_coarse):
    _, tokens, group = coarse_qkv.shape
    heads = group // HD

    def body(qkv_ref, up_ref, kv_out, qu_out):
        for head in range(heads):
            lanes = slice(head * HD, head * HD + HD)
            kv_out[head] = jnp.concatenate([qkv_ref[1, :, lanes], qkv_ref[2, :, lanes]], axis=1)
            qu_out[head] = jnp.concatenate([qkv_ref[0, :, lanes], up_ref[:, lanes]], axis=1)

    return whole_call(
        body,
        [jax.ShapeDtypeStruct((heads, tokens, 2 * HD), BF16)] * 2,
        "prepare",
        1 << 20,
        [],
        coarse_qkv,
        grad_coarse,
    )


def own_block(step, tokens):
    owner = lax.axis_index("y") ^ step
    return pl.ds(pl.multiple_of(owner * tokens, tokens), tokens)


def coarse_stats(key_values, query_ups, steps, before, key_tile):
    heads, tokens, _ = key_values[0].shape
    blocks, number = len(key_values), len(query_ups)
    per_block = tokens // key_tile

    def body(*refs):
        kv_refs, qu_refs = refs[:blocks], refs[blocks : blocks + number]
        out_ref, held = refs[-2:]
        if before:

            @pl.when(pl.program_id(1) == 0)
            def _():
                out_ref[...] = refs[blocks + number][...]

        for at in range(number):

            @pl.when(pl.program_id(1) == at)
            def _():
                held[...] = qu_refs[at][0]

        query = half(held[...], 0) * BF16(SCALE)
        upstream = half(held[...], 1)
        peak = jnp.full((1, tokens), -jnp.inf, F32)
        total = jnp.zeros((1, tokens), F32)
        weighted = jnp.zeros((1, tokens), F32)
        for i in range(blocks * per_block):
            start = (i % per_block) * key_tile
            tile = kv_refs[i // per_block][0, start : start + key_tile, :]
            score = nt(tile, query)
            product = nt(tile, upstream)
            new_peak = jnp.maximum(peak, jnp.max(score, axis=0, keepdims=True))
            decay = jnp.exp(peak - new_peak)
            share = jnp.exp(score - new_peak)
            total = total * decay + jnp.sum(share, axis=0, keepdims=True)
            weighted = weighted * decay + jnp.sum(share * product, axis=0, keepdims=True)
            peak = new_peak
        found = jnp.concatenate([peak + jnp.log(total), weighted / total], axis=0)
        for at, step in enumerate(steps):

            @pl.when(pl.program_id(1) == at)
            def _():
                out_ref[0, :, own_block(step, tokens)] = found

    pairs = heads * number * blocks * tokens**2
    return pl.pallas_call(
        body,
        grid=(heads, number),
        in_specs=[pl.BlockSpec((1, tokens, 128), lambda h, q: (h, 0, 0))] * (blocks + number)
        + [pl.BlockSpec((1, 2, blocks * tokens), lambda h, q: (h, 0, 0))] * len(before),
        out_specs=pl.BlockSpec((1, 2, blocks * tokens), lambda h, q: (h, 0, 0)),
        out_shape=jax.ShapeDtypeStruct((heads, 2, blocks * tokens), F32),
        scratch_shapes=[pltpu.VMEM((tokens, 128), BF16)],
        name="coarse_stats",
        cost_estimate=cost(4 * pairs * 256, 2 << 20, pairs),
        compiler_params=pltpu.CompilerParams(vmem_limit_bytes=VMEM),
    )(*key_values, *query_ups, *before)


def coarse_grads(key_values, query_ups, stats):
    heads, tokens, _ = key_values[0].shape
    blocks = len(query_ups)
    parts = len(stats)

    def body(*refs):
        kv_refs, qu_refs = refs[:blocks], refs[blocks : 2 * blocks]
        stats_refs = refs[2 * blocks : 2 * blocks + parts]
        kept_ref, sent_ref = refs[2 * blocks + parts : 2 * blocks + parts + 2]
        q_outs = refs[-blocks - 2 : -2]
        acc, held = refs[-2:]
        step = pl.program_id(1)
        for at in range(blocks):

            @pl.when(pl.program_id(1) == at)
            def _():
                held[...] = qu_refs[at][0]

        @pl.when(pl.program_id(1) == 0)
        def _():
            acc[...] = jnp.zeros_like(acc)

        query = half(held[...], 0) * BF16(SCALE)
        upstream = half(held[...], 1)
        found = [ref[0, :, own_block(step, tokens)] for ref in stats_refs]
        peak = found[0][:1]
        for part in found[1:]:
            peak = jnp.maximum(peak, part[:1])
        shares = [jnp.exp(part[:1] - peak) for part in found]
        total = sum(shares)
        log_total = peak + jnp.log(total)
        delta = sum(share * part[1:] for share, part in zip(shares, found)) / total
        found = jnp.zeros((HD, tokens), F32)
        for i in range(blocks):
            tile = kv_refs[i][0]
            share = jnp.exp(nt(tile, query) - log_total)
            grads = (share * (nt(tile, upstream) - delta)).astype(BF16)
            acc[i] += nn(grads, query) + nn(share.astype(BF16), upstream)
            found += nn(tile[:, :HD].T, grads)
        found = (found * SCALE).astype(BF16)
        for at in range(blocks):

            @pl.when(pl.program_id(1) == at)
            def _():
                q_outs[at][...] = found

        @pl.when(pl.program_id(1) == blocks - 1)
        def _():
            for i in range(blocks // 2):
                kept_ref[i, 0] = acc[2 * i].astype(BF16)
                sent_ref[i, 0] = acc[2 * i + 1].astype(BF16)

    pairs = heads * (blocks * tokens) ** 2
    out_shape = [jax.ShapeDtypeStruct((blocks // 2, heads, tokens, 128), BF16)] * 2
    out_shape += [jax.ShapeDtypeStruct((heads * HD, tokens), BF16)] * blocks
    return pl.pallas_call(
        body,
        grid=(heads, blocks),
        in_specs=[pl.BlockSpec((1, tokens, 128), lambda h, q: (h, 0, 0))] * (2 * blocks)
        + [pl.BlockSpec((1, 2, blocks * tokens), lambda h, q: (h, 0, 0))] * parts,
        out_specs=[pl.BlockSpec((blocks // 2, 1, tokens, 128), lambda h, q: (0, h, 0, 0))] * 2
        + [pl.BlockSpec((HD, tokens), lambda h, q: (h, 0))] * blocks,
        out_shape=out_shape,
        scratch_shapes=[
            pltpu.VMEM((blocks, tokens, 128), F32),
            pltpu.VMEM((tokens, 128), BF16),
        ],
        name="coarse_grads",
        cost_estimate=cost(10 * pairs * 256, 4 << 20, pairs),
        compiler_params=pltpu.CompilerParams(vmem_limit_bytes=VMEM),
    )(*key_values, *query_ups, *stats)


def whole_call(body, out_shape, name, flops, scratch, *operands):
    return pl.pallas_call(
        body,
        out_shape=out_shape,
        scratch_shapes=scratch,
        name=name,
        cost_estimate=cost(flops, 6 << 20, 1 << 20),
        compiler_params=pltpu.CompilerParams(vmem_limit_bytes=VMEM),
    )(*operands)


def pairs_of(width):
    return [(pair, slice(pair * 128, pair * 128 + 128)) for pair in range(width // 128)]


def window_bias(own, rows, columns, part, transposed):
    count = SIDE * SIDE // 2
    shape = (own, count) if transposed else (count, own)
    ext = lax.broadcasted_iota(jnp.int32, shape, 1 if transposed else 0)
    inner = lax.broadcasted_iota(jnp.int32, shape, 0 if transposed else 1)
    if part == 0:
        ext_row, ext_column = ext >> 4, (ext & 15) + RIM
    else:
        ext_row = (ext & 255) >> 3
        ext_column = (ext & 7) + jnp.where(ext >= 256, SIDE - RIM, 0)
    row_gap = ext_row - (inner >> 4) - RIM
    column_gap = ext_column - (inner & 15) - RIM
    row = ext_row + (lax.axis_index(ROW) * rows - RIM)
    column = ext_column + (lax.axis_index(COL) * columns - RIM)
    seen = (jnp.abs(row_gap) <= RADIUS) & (jnp.abs(column_gap) <= RADIUS)
    seen &= (row >= 0) & (row < lax.axis_size(ROW) * rows)
    seen &= (column >= 0) & (column < lax.axis_size(COL) * columns)
    return jnp.where(seen, 0.0, HIDDEN).astype(F32)


def fill_bias(bias_ref, own, rows, columns):
    count = SIDE * SIDE // 2
    for part in range(2):
        bias_ref[part * count : (part + 1) * count, :] = window_bias(
            own, rows, columns, part, False
        )


def stacked(refs, which, lanes):
    return jnp.concatenate([ref[which, :, lanes] for ref in refs], axis=0)


def fine_shares(own_qkv, ext_kv, rows, columns):
    _, own, width = own_qkv.shape
    heads = width // HD

    def body(q_ref, mid_ref, low_ref, high_ref, out_ref, bias_ref):
        fill_bias(bias_ref, own, rows, columns)
        ext = (mid_ref, low_ref, high_ref)
        for pair, lanes in pairs_of(width):
            key = stacked(ext, 0, lanes)
            for side in range(2):
                query = half(q_ref[0, :, lanes], side) * BF16(SCALE)
                score = nt(key, query) + bias_ref[...]
                share = jnp.exp(score - jnp.max(score, axis=0, keepdims=True))
                total = jnp.sum(share, axis=0, keepdims=True)
                out_ref[2 * pair + side] = (share * (1.0 / total)).astype(BF16)

    return whole_call(
        body,
        jax.ShapeDtypeStruct((heads, SIDE * SIDE, own), BF16),
        "fine_shares",
        1 << 30,
        [pltpu.VMEM((SIDE * SIDE, own), F32)],
        own_qkv,
        *ext_kv,
    )


def fine_grads(own_qkv, ext_kv, own_up, shares, rows, columns):
    _, own, width = own_qkv.shape
    edge, side_size, corner = RIM * columns, RIM * rows, RIM * RIM
    tall = side_size + 2 * corner
    base = 2 * edge + own
    sizes = [edge, edge, side_size, side_size, corner, corner, corner, corner]

    def body(q_ref, mid_ref, low_ref, high_ref, up_ref, share_ref, q_out, own_out, *outs):
        first = lax.axis_index("c") == 0
        upper = lax.axis_index("zh") == 0
        ext = (mid_ref, low_ref, high_ref)
        for pair, lanes in pairs_of(width):
            key_t = stacked(ext, 0, lanes).T
            value = stacked(ext, 1, lanes)
            parts = []
            key_sum = jnp.zeros((SIDE * SIDE, 128), F32)
            value_sum = jnp.zeros((SIDE * SIDE, 128), F32)
            for side in range(2):
                query = half(q_ref[0, :, lanes], side) * BF16(SCALE)
                up = half(up_ref[:, lanes], side)
                rounded = share_ref[2 * pair + side]
                share = rounded.astype(F32)
                product = nt(value, up)
                total = jnp.sum(share, axis=0, keepdims=True)
                delta = jnp.sum(share * product, axis=0, keepdims=True) / total
                grads = (share * (product - delta)).astype(BF16)
                key_sum += nn(grads, query)
                value_sum += nn(rounded, up)
                parts.append(nn(key_t[side * HD : side * HD + HD], grads))
            q_out[:, lanes] = (jnp.concatenate(parts, axis=0).T * SCALE).astype(BF16)
            right = slice(width + pair * 128, width + pair * 128 + 128)
            for at, total in ((lanes, key_sum), (right, value_sum)):
                top, bottom = total[:edge], total[edge + own : base]
                low, high = total[base : base + tall], total[base + tall :]
                own_out[:, at] = total[edge : edge + own]
                wings = [jnp.where(first, high, low), jnp.where(first, low, high)]
                found = [jnp.where(upper, bottom, top), jnp.where(upper, top, bottom)]
                found += [wing[corner : corner + side_size] for wing in wings]
                for wing in wings:
                    above, below = wing[:corner], wing[corner + side_size :]
                    found += [jnp.where(upper, below, above), jnp.where(upper, above, below)]
                for out, piece in zip(outs, found):
                    out[:, at] = piece.astype(BF16)

    return whole_call(
        body,
        [jax.ShapeDtypeStruct((own, width), BF16), jax.ShapeDtypeStruct((own, 2 * width), F32)]
        + [jax.ShapeDtypeStruct((size, 2 * width), BF16) for size in sizes],
        "fine_grads",
        2 << 30,
        [],
        own_qkv,
        *ext_kv,
        own_up,
        shares,
    )


def sent_around(pieces):
    tall, wide = lax.axis_size(ROW), lax.axis_size(COL)

    def partner(index, kind, count):
        if kind == "same":
            return index
        other = index ^ 1 if kind == "inner" else ((index + 1) ^ 1) - 1
        return other if 0 <= other < count else None

    kinds = [("inner", "same"), ("outer", "same"), ("same", "inner"), ("same", "outer")]
    kinds += [(down, across) for across in ("inner", "outer") for down in ("inner", "outer")]
    arrived = []
    for piece, (down, across) in zip(pieces, kinds):
        pairs = []
        for row in range(tall):
            for column in range(wide):
                there = partner(row, down, tall), partner(column, across, wide)
                if None not in there:
                    pairs.append((row * wide + column, there[0] * wide + there[1]))
        arrived.append(lax.ppermute(piece, ROW + COL, pairs))
    return arrived


def add_arrived(own, arrived, rows, columns):
    cells, wide = own.shape
    width = wide // 2

    def body(own_ref, *rest):
        first = lax.axis_index("c") == 0
        upper = lax.axis_index("zh") == 0
        row_in, row_out, side_in, side_out, *corners = [
            ref[...].astype(F32) for ref in rest[:-2]
        ]
        k_out, v_out = rest[-2:]

        def placed(inner, outer):
            above, below = jnp.where(upper, outer, inner), jnp.where(upper, inner, outer)
            return jnp.concatenate([above, below], axis=0)

        total = own_ref[...] + placed(row_in, row_out)
        inner = (side_in + placed(*corners[:2])).reshape(rows, RIM, wide)
        outer = (side_out + placed(*corners[2:])).reshape(rows, RIM, wide)
        left, right = jnp.where(first, outer, inner), jnp.where(first, inner, outer)
        total += jnp.concatenate([left, right], axis=1).reshape(cells, wide)
        k_out[...] = total[:, :width].astype(BF16)
        v_out[...] = total[:, width:].astype(BF16)

    return whole_call(
        body,
        [jax.ShapeDtypeStruct((cells, width), BF16)] * 2,
        "add_arrived",
        1 << 20,
        [],
        own,
        *arrived,
    )


def project(query_pieces, kept, from_core, arrived, joint, columns, count):
    group, tokens = query_pieces[0].shape
    heads = arrived.shape[0]
    rows = tokens // columns
    each = rows // count
    size = each * columns
    wide = joint.shape[1]
    chunk = 256
    blocks = len(query_pieces)

    def body(*refs):
        pieces = refs[:blocks]
        kept_ref, core_ref, arrived_ref, joint_ref, out, held, packed = refs[blocks:]

        @pl.when(pl.program_id(0) == 0)
        def _():
            for head in range(heads):
                total = kept_ref[0, head].astype(F32) + core_ref[0, head].astype(F32)
                total += arrived_ref[head].astype(F32)
                for part in range(2):
                    at = (1 + part) * group + head * HD
                    held[:, at : at + HD] = total[:, part * HD : (part + 1) * HD]
            total = pieces[0][...].astype(F32)
            for piece in pieces[1:]:
                total += piece[...].astype(F32)
            held[:, :group] = total.T
            for target in range(count):
                taken = []
                for c in range(columns):
                    start = c * rows + target * each
                    taken.append(held[start : start + each, :])
                chosen = jnp.concatenate(taken, axis=0).astype(BF16)
                packed[target * size : (target + 1) * size, :] = chosen

        out[...] = nn(packed[...], joint_ref[...]).astype(BF16)

    half_spec = pl.BlockSpec((1, heads, tokens, 128), lambda n: (0, 0, 0, 0))
    return pl.pallas_call(
        body,
        grid=(wide // chunk,),
        in_specs=[pl.BlockSpec((group, tokens), lambda n: (0, 0))] * blocks
        + [half_spec] * 2
        + [
            pl.BlockSpec(arrived.shape, lambda n: (0, 0, 0)),
            pl.BlockSpec((3 * group, chunk), lambda n: (0, n)),
        ],
        out_specs=pl.BlockSpec((tokens, chunk), lambda n: (0, n)),
        out_shape=jax.ShapeDtypeStruct((tokens, wide), BF16),
        scratch_shapes=[
            pltpu.VMEM((tokens, 3 * group), F32),
            pltpu.VMEM((tokens, 3 * group), BF16),
        ],
        name="project",
        cost_estimate=cost(2 << 30, 6 << 20, 0),
        compiler_params=pltpu.CompilerParams(vmem_limit_bytes=VMEM),
    )(*query_pieces, kept, from_core, arrived, joint)


def spread(pieces, columns):
    count, tokens, wide = pieces.shape
    width = wide // 4

    def body(in_ref, out):
        total = in_ref[0].astype(F32)
        for at in range(1, count):
            total += in_ref[at].astype(F32)
        total = total.astype(BF16)
        cells = 2 * tokens
        fine = lax.broadcasted_iota(jnp.int32, (cells, tokens), 0)
        token = lax.broadcasted_iota(jnp.int32, (cells, tokens), 1)
        cell = (token & 7) * 2 * columns + (token >> 3) * 2
        for a in range(2):
            grid = jnp.zeros((cells, width), F32)
            for b in range(2):
                place = jnp.where(fine == cell + b, 1.0, 0.0).astype(BF16)
                lanes = slice((2 * a + b) * width, (2 * a + b + 1) * width)
                grid += nn(place, total[:, lanes])
            grid = grid.astype(BF16)
            for row in range(tokens // columns):
                at = (2 * row + a) * 2 * columns
                out[at : at + 2 * columns, :] = grid[row * 2 * columns : (row + 1) * 2 * columns]

    return whole_call(
        body,
        jax.ShapeDtypeStruct((4 * tokens, width), BF16),
        "spread",
        1 << 28,
        [],
        pieces,
    )


def swapped(array, axis, flip=1):
    return lax.ppermute(array, axis, [(i, i ^ flip) for i in range(lax.axis_size(axis))])


def exchanged(inner, outer, axis):
    count = lax.axis_size(axis)
    beyond = [(i, ((i + 1) ^ 1) - 1) for i in range(1, count - 1)]
    return swapped(inner, axis), lax.ppermute(outer, axis, beyond)


def sent_rims(block, axis, parity, at):
    size = block.shape[at]
    low = lax.slice_in_dim(block, 0, RIM, axis=at)
    high = lax.slice_in_dim(block, size - RIM, None, axis=at)
    first = lax.axis_index(parity) == 0
    return exchanged(jnp.where(first, high, low), jnp.where(first, low, high), axis)


def placed_rims(inner, outer, parity):
    first = lax.axis_index(parity) == 0
    return jnp.where(first, outer, inner), jnp.where(first, inner, outer)


def shards(fine_qkv, coarse_qkv, grad_coarse, merge_weight, qkv_weight):
    rows, columns, width = fine_qkv.shape[1:]
    own = rows * columns
    coarse_columns, coarse_rows, group = grad_coarse.shape
    tokens = coarse_columns * coarse_rows
    wide = merge_weight.shape[0]

    key_value, query_up = prepare(
        coarse_qkv.reshape(3, tokens, group), grad_coarse.reshape(tokens, group)
    )
    across = swapped(key_value, "zl")
    near = [query_up, swapped(query_up, "y", 1), swapped(query_up, "y", 3)]
    beside = swapped(key_value, "c")
    beside, merge_weight = lax.optimization_barrier((beside, merge_weight))
    joint = lax.dot_general(
        qkv_weight, merge_weight, (((1,), (1,)), ((), ())), preferred_element_type=F32
    ).astype(BF16).reshape(3 * group, wide)
    across, joint = lax.optimization_barrier((across, joint))
    corner = swapped(across, "c")
    *near, joint = lax.optimization_barrier((*near, joint))
    far = swapped(near[0], "y", 2)
    keys = [key_value, beside, across, corner]
    queries = [near[0], near[1], far, near[2]]

    part = coarse_stats(keys, near, [0, 1, 3], (), 256)
    part, fine_qkv = lax.optimization_barrier((part, fine_qkv))
    own_qkv = fine_qkv.reshape(3, own, width)
    edges = sent_rims(fine_qkv[1:], ROW, "zh", 1)
    part = coarse_stats(keys, [far], [2], (part,), 256)
    part, *edges = lax.optimization_barrier((part, *edges))
    stats = [part] + [swapped(part, "y", step) for step in (1, 3, 2)]
    kept, sent, *query_grads = coarse_grads(keys, queries, stats)

    from_core = swapped(sent, "c")
    passed = (kept[1].astype(F32) + from_core[1].astype(F32)).astype(BF16)
    arrived = swapped(passed, "zl")
    query_pieces = [query_grads[0]]
    for step in (1, 2, 3):
        query_pieces.append(swapped(query_grads[step], "y", step))
    count = lax.axis_size(ROW)
    projected = project(
        query_pieces, kept, from_core, arrived, joint, coarse_columns, count
    )
    projected, *edges = lax.optimization_barrier((projected, *edges))
    pieces = lax.all_to_all(projected.reshape(count, -1, wide), ROW, 0, 0)
    low, high = placed_rims(*edges, "zh")
    tall = jnp.concatenate([low, fine_qkv[1:], high], axis=1)
    low, high = placed_rims(*sent_rims(tall, COL, "c", 2), "c")
    ext_kv = [array.reshape(2, -1, width) for array in (tall, low, high)]
    shares = fine_shares(own_qkv, ext_kv, rows, columns)
    pieces, shares = lax.optimization_barrier((pieces, shares))
    own_up = spread(pieces, coarse_columns)

    grad_query, middle, *rims = fine_grads(own_qkv, ext_kv, own_up, shares, rows, columns)
    grad_key, grad_value = add_arrived(middle, sent_around(rims), rows, columns)
    shape = (rows, columns, width)
    return grad_query.reshape(shape), grad_key.reshape(shape), grad_value.reshape(shape)


def solution(mesh):
    split = Mesh(mesh.devices.reshape(4, 2, 2, 4, 2), ROW + COL)
    return jax.shard_map(
        shards,
        mesh=split,
        in_specs=(
            P(None, ROW, COL, None),
            P(None, COL, None, ROW),
            P(COL, None, ROW),
            P(),
            P(None, None, ROW),
        ),
        out_specs=(P(ROW, COL, None), P(ROW, COL, None), P(ROW, COL, None)),
        check_vma=False,
    )
```

```python
import jax
import jax.numpy as jnp
from jax import lax
from jax.experimental import pallas as pl
from jax.experimental.pallas import tpu as pltpu
from jax.sharding import Mesh
from jax.sharding import PartitionSpec as P

HD = 64
RADIUS = 7
SCALE = 0.125
SIDE = 32
RIM = 8
HIDDEN = -1e30
ROW = ("x", "zh")
COL = ("zl", "y", "c")
F32 = jnp.float32
BF16 = jnp.bfloat16
VMEM = 60 << 20


def nt(left, right):
    return lax.dot_general(left, right, (((1,), (1,)), ((), ())), preferred_element_type=F32)


def nn(left, right):
    return lax.dot_general(left, right, (((1,), (0,)), ((), ())), preferred_element_type=F32)


def half(pair, which):
    lane = lax.broadcasted_iota(jnp.int32, pair.shape, 1)
    return jnp.where((lane < HD) == (which == 0), pair, jnp.zeros_like(pair))


def cost(flops, bytes_accessed, exps):
    return pl.CostEstimate(flops=flops, bytes_accessed=bytes_accessed, transcendentals=exps)


def prepare(coarse_qkv, grad_coarse):
    _, tokens, group = coarse_qkv.shape
    heads = group // HD

    def body(qkv_ref, up_ref, kv_out, qu_out):
        for head in range(heads):
            lanes = slice(head * HD, head * HD + HD)
            kv_out[head] = jnp.concatenate([qkv_ref[1, :, lanes], qkv_ref[2, :, lanes]], axis=1)
            qu_out[head] = jnp.concatenate([qkv_ref[0, :, lanes], up_ref[:, lanes]], axis=1)

    return whole_call(
        body,
        [jax.ShapeDtypeStruct((heads, tokens, 2 * HD), BF16)] * 2,
        "prepare",
        1 << 20,
        [],
        coarse_qkv,
        grad_coarse,
    )


def own_block(step, tokens):
    owner = lax.axis_index("y") ^ step
    return pl.ds(pl.multiple_of(owner * tokens, tokens), tokens)


def coarse_stats(key_values, query_ups, steps, before, key_tile):
    heads, tokens, _ = key_values[0].shape
    blocks, number = len(key_values), len(query_ups)
    per_block = tokens // key_tile

    def body(*refs):
        kv_refs, qu_refs = refs[:blocks], refs[blocks : blocks + number]
        out_ref, held = refs[-2:]
        if before:

            @pl.when(pl.program_id(1) == 0)
            def _():
                out_ref[...] = refs[blocks + number][...]

        for at in range(number):

            @pl.when(pl.program_id(1) == at)
            def _():
                held[...] = qu_refs[at][0]

        query = half(held[...], 0) * BF16(SCALE)
        upstream = half(held[...], 1)
        peak = jnp.full((1, tokens), -jnp.inf, F32)
        total = jnp.zeros((1, tokens), F32)
        weighted = jnp.zeros((1, tokens), F32)
        for i in range(blocks * per_block):
            start = (i % per_block) * key_tile
            tile = kv_refs[i // per_block][0, start : start + key_tile, :]
            score = nt(tile, query)
            product = nt(tile, upstream)
            new_peak = jnp.maximum(peak, jnp.max(score, axis=0, keepdims=True))
            decay = jnp.exp(peak - new_peak)
            share = jnp.exp(score - new_peak)
            total = total * decay + jnp.sum(share, axis=0, keepdims=True)
            weighted = weighted * decay + jnp.sum(share * product, axis=0, keepdims=True)
            peak = new_peak
        found = jnp.concatenate([peak + jnp.log(total), weighted / total], axis=0)
        for at, step in enumerate(steps):

            @pl.when(pl.program_id(1) == at)
            def _():
                out_ref[0, :, own_block(step, tokens)] = found

    pairs = heads * number * blocks * tokens**2
    return pl.pallas_call(
        body,
        grid=(heads, number),
        in_specs=[pl.BlockSpec((1, tokens, 128), lambda h, q: (h, 0, 0))] * (blocks + number)
        + [pl.BlockSpec((1, 2, blocks * tokens), lambda h, q: (h, 0, 0))] * len(before),
        out_specs=pl.BlockSpec((1, 2, blocks * tokens), lambda h, q: (h, 0, 0)),
        out_shape=jax.ShapeDtypeStruct((heads, 2, blocks * tokens), F32),
        scratch_shapes=[pltpu.VMEM((tokens, 128), BF16)],
        name="coarse_stats",
        cost_estimate=cost(4 * pairs * 256, 2 << 20, pairs),
        compiler_params=pltpu.CompilerParams(vmem_limit_bytes=VMEM),
    )(*key_values, *query_ups, *before)


def coarse_grads(key_values, query_ups, stats):
    heads, tokens, _ = key_values[0].shape
    blocks = len(query_ups)
    parts = len(stats)

    def body(*refs):
        kv_refs, qu_refs = refs[:blocks], refs[blocks : 2 * blocks]
        stats_refs = refs[2 * blocks : 2 * blocks + parts]
        kept_ref, sent_ref = refs[2 * blocks + parts : 2 * blocks + parts + 2]
        q_outs = refs[-blocks - 2 : -2]
        acc, held = refs[-2:]
        step = pl.program_id(1)
        for at in range(blocks):

            @pl.when(pl.program_id(1) == at)
            def _():
                held[...] = qu_refs[at][0]

        @pl.when(pl.program_id(1) == 0)
        def _():
            acc[...] = jnp.zeros_like(acc)

        query = half(held[...], 0) * BF16(SCALE)
        upstream = half(held[...], 1)
        found = [ref[0, :, own_block(step, tokens)] for ref in stats_refs]
        peak = found[0][:1]
        for part in found[1:]:
            peak = jnp.maximum(peak, part[:1])
        shares = [jnp.exp(part[:1] - peak) for part in found]
        total = sum(shares)
        log_total = peak + jnp.log(total)
        delta = sum(share * part[1:] for share, part in zip(shares, found)) / total
        found = jnp.zeros((HD, tokens), F32)
        for i in range(blocks):
            tile = kv_refs[i][0]
            share = jnp.exp(nt(tile, query) - log_total)
            grads = (share * (nt(tile, upstream) - delta)).astype(BF16)
            acc[i] += nn(grads, query) + nn(share.astype(BF16), upstream)
            found += nn(tile[:, :HD].T, grads)
        found = (found * SCALE).astype(BF16)
        for at in range(blocks):

            @pl.when(pl.program_id(1) == at)
            def _():
                q_outs[at][...] = found

        @pl.when(pl.program_id(1) == blocks - 1)
        def _():
            for i in range(blocks // 2):
                kept_ref[i, 0] = acc[2 * i].astype(BF16)
                sent_ref[i, 0] = acc[2 * i + 1].astype(BF16)

    pairs = heads * (blocks * tokens) ** 2
    out_shape = [jax.ShapeDtypeStruct((blocks // 2, heads, tokens, 128), BF16)] * 2
    out_shape += [jax.ShapeDtypeStruct((heads * HD, tokens), BF16)] * blocks
    return pl.pallas_call(
        body,
        grid=(heads, blocks),
        in_specs=[pl.BlockSpec((1, tokens, 128), lambda h, q: (h, 0, 0))] * (2 * blocks)
        + [pl.BlockSpec((1, 2, blocks * tokens), lambda h, q: (h, 0, 0))] * parts,
        out_specs=[pl.BlockSpec((blocks // 2, 1, tokens, 128), lambda h, q: (0, h, 0, 0))] * 2
        + [pl.BlockSpec((HD, tokens), lambda h, q: (h, 0))] * blocks,
        out_shape=out_shape,
        scratch_shapes=[
            pltpu.VMEM((blocks, tokens, 128), F32),
            pltpu.VMEM((tokens, 128), BF16),
        ],
        name="coarse_grads",
        cost_estimate=cost(10 * pairs * 256, 4 << 20, pairs),
        compiler_params=pltpu.CompilerParams(vmem_limit_bytes=VMEM),
    )(*key_values, *query_ups, *stats)


def whole_call(body, out_shape, name, flops, scratch, *operands):
    return pl.pallas_call(
        body,
        out_shape=out_shape,
        scratch_shapes=scratch,
        name=name,
        cost_estimate=cost(flops, 6 << 20, 1 << 20),
        compiler_params=pltpu.CompilerParams(vmem_limit_bytes=VMEM),
    )(*operands)


def pairs_of(width):
    return [(pair, slice(pair * 128, pair * 128 + 128)) for pair in range(width // 128)]


def window_bias(own, rows, columns, part, transposed):
    count = SIDE * SIDE // 2
    shape = (own, count) if transposed else (count, own)
    ext = lax.broadcasted_iota(jnp.int32, shape, 1 if transposed else 0)
    inner = lax.broadcasted_iota(jnp.int32, shape, 0 if transposed else 1)
    if part == 0:
        ext_row, ext_column = ext >> 4, (ext & 15) + RIM
    else:
        ext_row = (ext & 255) >> 3
        ext_column = (ext & 7) + jnp.where(ext >= 256, SIDE - RIM, 0)
    row_gap = ext_row - (inner >> 4) - RIM
    column_gap = ext_column - (inner & 15) - RIM
    row = ext_row + (lax.axis_index(ROW) * rows - RIM)
    column = ext_column + (lax.axis_index(COL) * columns - RIM)
    seen = (jnp.abs(row_gap) <= RADIUS) & (jnp.abs(column_gap) <= RADIUS)
    seen &= (row >= 0) & (row < lax.axis_size(ROW) * rows)
    seen &= (column >= 0) & (column < lax.axis_size(COL) * columns)
    return jnp.where(seen, 0.0, HIDDEN).astype(F32)


def fill_bias(bias_ref, own, rows, columns):
    count = SIDE * SIDE // 2
    for part in range(2):
        bias_ref[part * count : (part + 1) * count, :] = window_bias(
            own, rows, columns, part, False
        )


def stacked(refs, which, lanes):
    return jnp.concatenate([ref[which, :, lanes] for ref in refs], axis=0)


def fine_shares(own_qkv, ext_kv, rows, columns):
    _, own, width = own_qkv.shape
    heads = width // HD

    def body(q_ref, mid_ref, low_ref, high_ref, out_ref, bias_ref):
        fill_bias(bias_ref, own, rows, columns)
        ext = (mid_ref, low_ref, high_ref)
        for pair, lanes in pairs_of(width):
            key = stacked(ext, 0, lanes)
            for side in range(2):
                query = half(q_ref[0, :, lanes], side) * BF16(SCALE)
                score = nt(key, query) + bias_ref[...]
                share = jnp.exp(score - jnp.max(score, axis=0, keepdims=True))
                total = jnp.sum(share, axis=0, keepdims=True)
                out_ref[2 * pair + side] = (share * (1.0 / total)).astype(BF16)

    return whole_call(
        body,
        jax.ShapeDtypeStruct((heads, SIDE * SIDE, own), BF16),
        "fine_shares",
        1 << 30,
        [pltpu.VMEM((SIDE * SIDE, own), F32)],
        own_qkv,
        *ext_kv,
    )


def pair_call(body, out_shape, name, flops, *operands):
    width = 384
    pairs = width // 128

    def spec(array):
        shape = tuple(array.shape)
        rank = len(shape)
        if shape[0] == 2 * pairs:
            return pl.BlockSpec((2,) + shape[1:], lambda p: (p,) + (0,) * (rank - 1))
        return pl.BlockSpec(
            shape[:-1] + (shape[-1] // pairs,), lambda p: (0,) * (rank - 1) + (p,)
        )

    return pl.pallas_call(
        body,
        grid=(pairs,),
        in_specs=[spec(array) for array in operands],
        out_specs=[spec(shape) for shape in out_shape],
        out_shape=out_shape,
        name=name,
        cost_estimate=cost(flops, 6 << 20, 0),
        compiler_params=pltpu.CompilerParams(vmem_limit_bytes=VMEM),
    )(*operands)


def fine_grads(own_qkv, ext_kv, own_up, shares, rows, columns):
    _, own, width = own_qkv.shape
    mid_size, side_size = ext_kv[0].shape[1], ext_kv[1].shape[1]

    def body(q_ref, mid_ref, low_ref, high_ref, up_ref, share_ref, q_out, mid_out, *outs):
        first = lax.axis_index("c") == 0
        ext = (mid_ref, low_ref, high_ref)
        key_t = jnp.concatenate([ref[0] for ref in ext], axis=0).T
        value = jnp.concatenate([ref[1] for ref in ext], axis=0)
        parts = []
        key_sum = jnp.zeros((SIDE * SIDE, 128), F32)
        value_sum = jnp.zeros((SIDE * SIDE, 128), F32)
        for side in range(2):
            query = half(q_ref[0], side) * BF16(SCALE)
            up = half(up_ref[...], side)
            rounded = share_ref[side]
            share = rounded.astype(F32)
            product = nt(value, up)
            total = jnp.sum(share, axis=0, keepdims=True)
            delta = jnp.sum(share * product, axis=0, keepdims=True) / total
            grads = (share * (product - delta)).astype(BF16)
            key_sum += nn(grads, query)
            value_sum += nn(rounded, up)
            parts.append(nn(key_t[side * HD : side * HD + HD], grads))
        q_out[...] = (jnp.concatenate(parts, axis=0).T * SCALE).astype(BF16)
        for at, total in ((slice(0, 128), key_sum), (slice(128, 256), value_sum)):
            mid_out[:, at] = total[:mid_size]
            low = total[mid_size : mid_size + side_size].astype(BF16)
            high = total[mid_size + side_size :].astype(BF16)
            outs[0][:, at] = jnp.where(first, high, low)
            outs[1][:, at] = jnp.where(first, low, high)

    return pair_call(
        body,
        [
            jax.ShapeDtypeStruct((own, width), BF16),
            jax.ShapeDtypeStruct((mid_size, 2 * width), F32),
            jax.ShapeDtypeStruct((side_size, 2 * width), BF16),
            jax.ShapeDtypeStruct((side_size, 2 * width), BF16),
        ],
        "fine_grads",
        2 << 30,
        own_qkv,
        *ext_kv,
        own_up,
        shares,
    )


def add_columns(mid, inner, outer, columns):
    cells, wide = mid.shape
    tall = cells // columns
    edge = RIM * columns

    def body(mid_ref, inner_ref, outer_ref, own_out, inner_out, outer_out):
        first = lax.axis_index("c") == 0
        inner = inner_ref[...].astype(F32).reshape(tall, RIM, -1)
        outer = outer_ref[...].astype(F32).reshape(tall, RIM, -1)
        left, right = jnp.where(first, outer, inner), jnp.where(first, inner, outer)
        both = jnp.concatenate([left, right], axis=1).reshape(mid_ref.shape)
        total = mid_ref[...] + both
        top, bottom = total[:edge], total[cells - edge :]
        upper = lax.axis_index("zh") == 0
        own_out[...] = total[edge : cells - edge]
        inner_out[...] = jnp.where(upper, bottom, top).astype(BF16)
        outer_out[...] = jnp.where(upper, top, bottom).astype(BF16)

    return pair_call(
        body,
        [jax.ShapeDtypeStruct((cells - 2 * edge, wide), F32)]
        + [jax.ShapeDtypeStruct((edge, wide), BF16)] * 2,
        "add_columns",
        1 << 20,
        mid,
        inner,
        outer,
    )


def add_rows(own, inner, outer):
    cells, wide = own.shape

    def body(own_ref, inner_ref, outer_ref, k_out, v_out):
        upper = lax.axis_index("zh") == 0
        inner = inner_ref[...].astype(F32)
        outer = outer_ref[...].astype(F32)
        above, below = jnp.where(upper, outer, inner), jnp.where(upper, inner, outer)
        total = own_ref[...] + jnp.concatenate([above, below], axis=0)
        k_out[...] = total[:, :128].astype(BF16)
        v_out[...] = total[:, 128:].astype(BF16)

    return pair_call(
        body,
        [jax.ShapeDtypeStruct((cells, wide // 2), BF16)] * 2,
        "add_rows",
        1 << 20,
        own,
        inner,
        outer,
    )


def project(query_pieces, kept, from_core, arrived, joint, columns, count):
    group, tokens = query_pieces[0].shape
    heads = arrived.shape[0]
    rows = tokens // columns
    each = rows // count
    size = each * columns
    wide = joint.shape[1]
    chunk = 256
    blocks = len(query_pieces)

    def body(*refs):
        pieces = refs[:blocks]
        kept_ref, core_ref, arrived_ref, joint_ref, out, held, packed = refs[blocks:]

        @pl.when(pl.program_id(0) == 0)
        def _():
            for head in range(heads):
                total = kept_ref[0, head].astype(F32) + core_ref[0, head].astype(F32)
                total += arrived_ref[head].astype(F32)
                for part in range(2):
                    at = (1 + part) * group + head * HD
                    held[:, at : at + HD] = total[:, part * HD : (part + 1) * HD]
            total = pieces[0][...].astype(F32)
            for piece in pieces[1:]:
                total += piece[...].astype(F32)
            held[:, :group] = total.T
            for target in range(count):
                taken = []
                for c in range(columns):
                    start = c * rows + target * each
                    taken.append(held[start : start + each, :])
                chosen = jnp.concatenate(taken, axis=0).astype(BF16)
                packed[target * size : (target + 1) * size, :] = chosen

        out[...] = nn(packed[...], joint_ref[...]).astype(BF16)

    half_spec = pl.BlockSpec((1, heads, tokens, 128), lambda n: (0, 0, 0, 0))
    return pl.pallas_call(
        body,
        grid=(wide // chunk,),
        in_specs=[pl.BlockSpec((group, tokens), lambda n: (0, 0))] * blocks
        + [half_spec] * 2
        + [
            pl.BlockSpec(arrived.shape, lambda n: (0, 0, 0)),
            pl.BlockSpec((3 * group, chunk), lambda n: (0, n)),
        ],
        out_specs=pl.BlockSpec((tokens, chunk), lambda n: (0, n)),
        out_shape=jax.ShapeDtypeStruct((tokens, wide), BF16),
        scratch_shapes=[
            pltpu.VMEM((tokens, 3 * group), F32),
            pltpu.VMEM((tokens, 3 * group), BF16),
        ],
        name="project",
        cost_estimate=cost(2 << 30, 6 << 20, 0),
        compiler_params=pltpu.CompilerParams(vmem_limit_bytes=VMEM),
    )(*query_pieces, kept, from_core, arrived, joint)


def spread(pieces, columns):
    count, tokens, wide = pieces.shape
    width = wide // 4

    def body(in_ref, out):
        total = in_ref[0].astype(F32)
        for at in range(1, count):
            total += in_ref[at].astype(F32)
        total = total.astype(BF16)
        cells = 2 * tokens
        fine = lax.broadcasted_iota(jnp.int32, (cells, tokens), 0)
        token = lax.broadcasted_iota(jnp.int32, (cells, tokens), 1)
        cell = (token & 7) * 2 * columns + (token >> 3) * 2
        for a in range(2):
            grid = jnp.zeros((cells, width), F32)
            for b in range(2):
                place = jnp.where(fine == cell + b, 1.0, 0.0).astype(BF16)
                lanes = slice((2 * a + b) * width, (2 * a + b + 1) * width)
                grid += nn(place, total[:, lanes])
            grid = grid.astype(BF16)
            for row in range(tokens // columns):
                at = (2 * row + a) * 2 * columns
                out[at : at + 2 * columns, :] = grid[row * 2 * columns : (row + 1) * 2 * columns]

    return whole_call(
        body,
        jax.ShapeDtypeStruct((4 * tokens, width), BF16),
        "spread",
        1 << 28,
        [],
        pieces,
    )


def swapped(array, axis, flip=1):
    return lax.ppermute(array, axis, [(i, i ^ flip) for i in range(lax.axis_size(axis))])


def exchanged(inner, outer, axis):
    count = lax.axis_size(axis)
    beyond = [(i, ((i + 1) ^ 1) - 1) for i in range(1, count - 1)]
    return swapped(inner, axis), lax.ppermute(outer, axis, beyond)


def sent_rims(block, axis, parity, at):
    size = block.shape[at]
    low = lax.slice_in_dim(block, 0, RIM, axis=at)
    high = lax.slice_in_dim(block, size - RIM, None, axis=at)
    first = lax.axis_index(parity) == 0
    return exchanged(jnp.where(first, high, low), jnp.where(first, low, high), axis)


def placed_rims(inner, outer, parity):
    first = lax.axis_index(parity) == 0
    return jnp.where(first, outer, inner), jnp.where(first, inner, outer)


def shards(fine_qkv, coarse_qkv, grad_coarse, merge_weight, qkv_weight):
    rows, columns, width = fine_qkv.shape[1:]
    own = rows * columns
    coarse_columns, coarse_rows, group = grad_coarse.shape
    tokens = coarse_columns * coarse_rows
    wide = merge_weight.shape[0]

    key_value, query_up = prepare(
        coarse_qkv.reshape(3, tokens, group), grad_coarse.reshape(tokens, group)
    )
    across = swapped(key_value, "zl")
    near = [query_up, swapped(query_up, "y", 1), swapped(query_up, "y", 3)]
    beside = swapped(key_value, "c")
    beside, merge_weight = lax.optimization_barrier((beside, merge_weight))
    joint = lax.dot_general(
        qkv_weight, merge_weight, (((1,), (1,)), ((), ())), preferred_element_type=F32
    ).astype(BF16).reshape(3 * group, wide)
    across, joint = lax.optimization_barrier((across, joint))
    corner = swapped(across, "c")
    *near, joint, fine_qkv = lax.optimization_barrier((*near, joint, fine_qkv))
    far = swapped(near[0], "y", 2)
    keys = [key_value, beside, across, corner]
    queries = [near[0], near[1], far, near[2]]
    own_qkv = fine_qkv.reshape(3, own, width)
    edges = sent_rims(fine_qkv[1:], ROW, "zh", 1)

    part = coarse_stats(keys, near, [0, 1, 3], (), 256)
    part, *edges = lax.optimization_barrier((part, *edges))
    low, high = placed_rims(*edges, "zh")
    tall = jnp.concatenate([low, fine_qkv[1:], high], axis=1)
    edges = sent_rims(tall, COL, "c", 2)
    part = coarse_stats(keys, [far], [2], (part,), 256)
    part, *edges = lax.optimization_barrier((part, *edges))
    stats = [part] + [swapped(part, "y", step) for step in (1, 3, 2)]
    kept, sent, *query_grads = coarse_grads(keys, queries, stats)

    from_core = swapped(sent, "c")
    passed = (kept[1].astype(F32) + from_core[1].astype(F32)).astype(BF16)
    arrived = swapped(passed, "zl")
    query_pieces = [query_grads[0]]
    for step in (1, 2, 3):
        query_pieces.append(swapped(query_grads[step], "y", step))
    count = lax.axis_size(ROW)
    low, high = placed_rims(*edges, "c")
    ext_kv = [array.reshape(2, -1, width) for array in (tall, low, high)]
    shares = fine_shares(own_qkv, ext_kv, rows, columns)
    arrived, shares = lax.optimization_barrier((arrived, shares))
    projected = project(
        query_pieces, kept, from_core, arrived, joint, coarse_columns, count
    )
    pieces = lax.all_to_all(projected.reshape(count, -1, wide), ROW, 0, 0)
    own_up = spread(pieces, coarse_columns)

    grad_query, mid, inner, outer = fine_grads(
        own_qkv, ext_kv, own_up, shares, rows, columns
    )
    inner, outer = exchanged(inner, outer, COL)
    middle, inner, outer = add_columns(mid, inner, outer, columns)
    inner, outer = exchanged(inner, outer, ROW)
    grad_key, grad_value = add_rows(middle, inner, outer)
    shape = (rows, columns, width)
    return grad_query.reshape(shape), grad_key.reshape(shape), grad_value.reshape(shape)


def solution(mesh):
    split = Mesh(mesh.devices.reshape(4, 2, 2, 4, 2), ROW + COL)
    return jax.shard_map(
        shards,
        mesh=split,
        in_specs=(
            P(None, ROW, COL, None),
            P(None, COL, None, ROW),
            P(COL, None, ROW),
            P(),
            P(None, None, ROW),
        ),
        out_specs=(P(ROW, COL, None), P(ROW, COL, None), P(ROW, COL, None)),
        check_vma=False,
    )
```

```python
import jax
import jax.numpy as jnp
from jax import lax
from jax.experimental import pallas as pl
from jax.experimental.pallas import tpu as pltpu
from jax.sharding import Mesh
from jax.sharding import PartitionSpec as P

HD = 64
RADIUS = 7
SCALE = 0.125
SIDE = 32
RIM = 8
HIDDEN = -1e30
ROW = ("x", "zh")
COL = ("zl", "y", "c")
F32 = jnp.float32
BF16 = jnp.bfloat16
VMEM = 60 << 20


def nt(left, right):
    return lax.dot_general(left, right, (((1,), (1,)), ((), ())), preferred_element_type=F32)


def nn(left, right):
    return lax.dot_general(left, right, (((1,), (0,)), ((), ())), preferred_element_type=F32)


def half(pair, which):
    lane = lax.broadcasted_iota(jnp.int32, pair.shape, 1)
    return jnp.where((lane < HD) == (which == 0), pair, jnp.zeros_like(pair))


def cost(flops, bytes_accessed, exps):
    return pl.CostEstimate(flops=flops, bytes_accessed=bytes_accessed, transcendentals=exps)


def prepare(coarse_qkv, grad_coarse):
    _, tokens, group = coarse_qkv.shape
    heads = group // HD

    def body(qkv_ref, up_ref, kv_out, qu_out):
        for head in range(heads):
            lanes = slice(head * HD, head * HD + HD)
            kv_out[head] = jnp.concatenate([qkv_ref[1, :, lanes], qkv_ref[2, :, lanes]], axis=1)
            qu_out[head] = jnp.concatenate([qkv_ref[0, :, lanes], up_ref[:, lanes]], axis=1)

    return whole_call(
        body,
        [jax.ShapeDtypeStruct((heads, tokens, 2 * HD), BF16)] * 2,
        "prepare",
        1 << 20,
        [],
        coarse_qkv,
        grad_coarse,
    )


def own_block(step, tokens):
    owner = lax.axis_index("y") ^ step
    return pl.ds(pl.multiple_of(owner * tokens, tokens), tokens)


def coarse_stats(key_values, query_ups, steps, before, key_tile):
    heads, tokens, _ = key_values[0].shape
    blocks, number = len(key_values), len(query_ups)
    per_block = tokens // key_tile

    def body(*refs):
        kv_refs, qu_refs = refs[:blocks], refs[blocks : blocks + number]
        out_ref, held = refs[-2:]
        if before:

            @pl.when(pl.program_id(1) == 0)
            def _():
                out_ref[...] = refs[blocks + number][...]

        for at in range(number):

            @pl.when(pl.program_id(1) == at)
            def _():
                held[...] = qu_refs[at][0]

        query = half(held[...], 0) * BF16(SCALE)
        upstream = half(held[...], 1)
        peak = jnp.full((1, tokens), -jnp.inf, F32)
        total = jnp.zeros((1, tokens), F32)
        weighted = jnp.zeros((1, tokens), F32)
        for i in range(blocks * per_block):
            start = (i % per_block) * key_tile
            tile = kv_refs[i // per_block][0, start : start + key_tile, :]
            score = nt(tile, query)
            product = nt(tile, upstream)
            new_peak = jnp.maximum(peak, jnp.max(score, axis=0, keepdims=True))
            decay = jnp.exp(peak - new_peak)
            share = jnp.exp(score - new_peak)
            total = total * decay + jnp.sum(share, axis=0, keepdims=True)
            weighted = weighted * decay + jnp.sum(share * product, axis=0, keepdims=True)
            peak = new_peak
        found = jnp.concatenate([peak + jnp.log(total), weighted / total], axis=0)
        for at, step in enumerate(steps):

            @pl.when(pl.program_id(1) == at)
            def _():
                out_ref[0, :, own_block(step, tokens)] = found

    pairs = heads * number * blocks * tokens**2
    return pl.pallas_call(
        body,
        grid=(heads, number),
        in_specs=[pl.BlockSpec((1, tokens, 128), lambda h, q: (h, 0, 0))] * (blocks + number)
        + [pl.BlockSpec((1, 2, blocks * tokens), lambda h, q: (h, 0, 0))] * len(before),
        out_specs=pl.BlockSpec((1, 2, blocks * tokens), lambda h, q: (h, 0, 0)),
        out_shape=jax.ShapeDtypeStruct((heads, 2, blocks * tokens), F32),
        scratch_shapes=[pltpu.VMEM((tokens, 128), BF16)],
        name="coarse_stats",
        cost_estimate=cost(4 * pairs * 256, 2 << 20, pairs),
        compiler_params=pltpu.CompilerParams(vmem_limit_bytes=VMEM),
    )(*key_values, *query_ups, *before)


def coarse_grads(key_values, query_ups, stats):
    heads, tokens, _ = key_values[0].shape
    blocks = len(query_ups)
    parts = len(stats)

    def body(*refs):
        kv_refs, qu_refs = refs[:blocks], refs[blocks : 2 * blocks]
        stats_refs = refs[2 * blocks : 2 * blocks + parts]
        kept_ref, sent_ref = refs[2 * blocks + parts : 2 * blocks + parts + 2]
        q_outs = refs[-blocks - 2 : -2]
        acc, held = refs[-2:]
        step = pl.program_id(1)
        for at in range(blocks):

            @pl.when(pl.program_id(1) == at)
            def _():
                held[...] = qu_refs[at][0]

        @pl.when(pl.program_id(1) == 0)
        def _():
            acc[...] = jnp.zeros_like(acc)

        query = half(held[...], 0) * BF16(SCALE)
        upstream = half(held[...], 1)
        found = [ref[0, :, own_block(step, tokens)] for ref in stats_refs]
        peak = found[0][:1]
        for part in found[1:]:
            peak = jnp.maximum(peak, part[:1])
        shares = [jnp.exp(part[:1] - peak) for part in found]
        total = sum(shares)
        log_total = peak + jnp.log(total)
        delta = sum(share * part[1:] for share, part in zip(shares, found)) / total
        found = jnp.zeros((HD, tokens), F32)
        for i in range(blocks):
            tile = kv_refs[i][0]
            share = jnp.exp(nt(tile, query) - log_total)
            grads = (share * (nt(tile, upstream) - delta)).astype(BF16)
            acc[i] += nn(grads, query) + nn(share.astype(BF16), upstream)
            found += nn(tile[:, :HD].T, grads)
        found = (found * SCALE).astype(BF16)
        for at in range(blocks):

            @pl.when(pl.program_id(1) == at)
            def _():
                q_outs[at][...] = found

        @pl.when(pl.program_id(1) == blocks - 1)
        def _():
            for i in range(blocks // 2):
                kept_ref[i, 0] = acc[2 * i].astype(BF16)
                sent_ref[i, 0] = acc[2 * i + 1].astype(BF16)

    pairs = heads * (blocks * tokens) ** 2
    out_shape = [jax.ShapeDtypeStruct((blocks // 2, heads, tokens, 128), BF16)] * 2
    out_shape += [jax.ShapeDtypeStruct((heads * HD, tokens), BF16)] * blocks
    return pl.pallas_call(
        body,
        grid=(heads, blocks),
        in_specs=[pl.BlockSpec((1, tokens, 128), lambda h, q: (h, 0, 0))] * (2 * blocks)
        + [pl.BlockSpec((1, 2, blocks * tokens), lambda h, q: (h, 0, 0))] * parts,
        out_specs=[pl.BlockSpec((blocks // 2, 1, tokens, 128), lambda h, q: (0, h, 0, 0))] * 2
        + [pl.BlockSpec((HD, tokens), lambda h, q: (h, 0))] * blocks,
        out_shape=out_shape,
        scratch_shapes=[
            pltpu.VMEM((blocks, tokens, 128), F32),
            pltpu.VMEM((tokens, 128), BF16),
        ],
        name="coarse_grads",
        cost_estimate=cost(10 * pairs * 256, 4 << 20, pairs),
        compiler_params=pltpu.CompilerParams(vmem_limit_bytes=VMEM),
    )(*key_values, *query_ups, *stats)


def whole_call(body, out_shape, name, flops, scratch, *operands):
    return pl.pallas_call(
        body,
        out_shape=out_shape,
        scratch_shapes=scratch,
        name=name,
        cost_estimate=cost(flops, 6 << 20, 1 << 20),
        compiler_params=pltpu.CompilerParams(vmem_limit_bytes=VMEM),
    )(*operands)


def pairs_of(width):
    return [(pair, slice(pair * 128, pair * 128 + 128)) for pair in range(width // 128)]


def window_bias(own, rows, columns, part, transposed):
    count = SIDE * SIDE // 2
    shape = (own, count) if transposed else (count, own)
    ext = lax.broadcasted_iota(jnp.int32, shape, 1 if transposed else 0)
    inner = lax.broadcasted_iota(jnp.int32, shape, 0 if transposed else 1)
    if part == 0:
        ext_row, ext_column = ext >> 4, (ext & 15) + RIM
    else:
        ext_row = (ext & 255) >> 3
        ext_column = (ext & 7) + jnp.where(ext >= 256, SIDE - RIM, 0)
    row_gap = ext_row - (inner >> 4) - RIM
    column_gap = ext_column - (inner & 15) - RIM
    row = ext_row + (lax.axis_index(ROW) * rows - RIM)
    column = ext_column + (lax.axis_index(COL) * columns - RIM)
    seen = (jnp.abs(row_gap) <= RADIUS) & (jnp.abs(column_gap) <= RADIUS)
    seen &= (row >= 0) & (row < lax.axis_size(ROW) * rows)
    seen &= (column >= 0) & (column < lax.axis_size(COL) * columns)
    return jnp.where(seen, 0.0, HIDDEN).astype(F32)


def fill_bias(bias_ref, own, rows, columns):
    count = SIDE * SIDE // 2
    for part in range(2):
        bias_ref[part * count : (part + 1) * count, :] = window_bias(
            own, rows, columns, part, False
        )


def stacked(refs, which, lanes):
    return jnp.concatenate([ref[which, :, lanes] for ref in refs], axis=0)


def fine_shares(own_qkv, ext_kv, rows, columns):
    _, own, width = own_qkv.shape
    heads = width // HD
    count = SIDE * SIDE // 2

    def body(q_ref, mid_ref, low_ref, high_ref, mid_out, side_out, o_ref, bias_ref):
        fill_bias(bias_ref, own, rows, columns)
        ext = (mid_ref, low_ref, high_ref)
        for pair, lanes in pairs_of(width):
            key = stacked(ext, 0, lanes)
            value_t = stacked(ext, 1, lanes).T
            parts = []
            for side in range(2):
                query = half(q_ref[0, :, lanes], side) * BF16(SCALE)
                score = nt(key, query) + bias_ref[...]
                share = jnp.exp(score - jnp.max(score, axis=0, keepdims=True))
                total = jnp.sum(share, axis=0, keepdims=True)
                rounded = (share * (1.0 / total)).astype(BF16)
                mid_out[2 * pair + side] = rounded[:count]
                side_out[2 * pair + side] = rounded[count:]
                total = jnp.sum(rounded.astype(F32), axis=0, keepdims=True)
                parts.append(nn(value_t[side * HD : side * HD + HD], rounded) / total)
            o_ref[:, lanes] = jnp.concatenate(parts, axis=0).T

    return whole_call(
        body,
        [jax.ShapeDtypeStruct((heads, count, own), BF16)] * 2
        + [jax.ShapeDtypeStruct((own, width), F32)],
        "fine_shares",
        1 << 30,
        [pltpu.VMEM((SIDE * SIDE, own), F32)],
        own_qkv,
        *ext_kv,
    )


def pair_call(body, out_shape, name, flops, *operands):
    width = 384
    pairs = width // 128

    def spec(array):
        shape = tuple(array.shape)
        rank = len(shape)
        if shape[0] == 2 * pairs:
            return pl.BlockSpec((2,) + shape[1:], lambda p: (p,) + (0,) * (rank - 1))
        return pl.BlockSpec(
            shape[:-1] + (shape[-1] // pairs,), lambda p: (0,) * (rank - 1) + (p,)
        )

    return pl.pallas_call(
        body,
        grid=(pairs,),
        in_specs=[spec(array) for array in operands],
        out_specs=[spec(shape) for shape in out_shape],
        out_shape=out_shape,
        name=name,
        cost_estimate=cost(flops, 6 << 20, 0),
        compiler_params=pltpu.CompilerParams(vmem_limit_bytes=VMEM),
    )(*operands)


def head_sums(up, out):
    head = lax.broadcasted_iota(jnp.int32, (8, up.shape[1]), 0)
    lane = lax.broadcasted_iota(jnp.int32, (8, up.shape[1]), 1)
    pick = jnp.where((lane >> 6) == head, 1.0, 0.0).astype(F32)
    return lax.dot_general(
        pick,
        up * out,
        (((1,), (1,)), ((), ())),
        preferred_element_type=F32,
        precision=lax.Precision.HIGHEST,
    )


def pair_grads(q_ref, ext, up_ref, o_ref, share_ref):
    delta = head_sums(up_ref[...].astype(F32), o_ref[...])
    key = jnp.concatenate([ref[0] for ref in ext], axis=0)
    key_t = key.T
    value = jnp.concatenate([ref[1] for ref in ext], axis=0)
    parts = []
    key_sum = jnp.zeros(key.shape, F32)
    value_sum = jnp.zeros(key.shape, F32)
    for side in range(2):
        query = half(q_ref[0], side) * BF16(SCALE)
        up = half(up_ref[...], side)
        rounded = share_ref[side]
        product = nt(value, up) - delta[side : side + 1]
        grads = (rounded.astype(F32) * product).astype(BF16)
        key_sum += nn(grads, query)
        value_sum += nn(rounded, up)
        parts.append(nn(key_t[side * HD : side * HD + HD], grads))
    return jnp.concatenate(parts, axis=0).T, key_sum, value_sum


def fine_sides(own_qkv, sides, own_up, out, shares):
    _, own, width = own_qkv.shape
    size = sides[0].shape[1]

    def body(q_ref, low_ref, high_ref, up_ref, o_ref, share_ref, q_out, inner_out, outer_out):
        first = lax.axis_index("c") == 0
        q_out[...], *sums = pair_grads(q_ref, (low_ref, high_ref), up_ref, o_ref, share_ref)
        for at, total in zip((slice(0, 128), slice(128, 256)), sums):
            low, high = total[:size].astype(BF16), total[size:].astype(BF16)
            inner_out[:, at] = jnp.where(first, high, low)
            outer_out[:, at] = jnp.where(first, low, high)

    return pair_call(
        body,
        [jax.ShapeDtypeStruct((own, width), F32)]
        + [jax.ShapeDtypeStruct((size, 2 * width), BF16)] * 2,
        "fine_sides",
        1 << 30,
        own_qkv,
        *sides,
        own_up,
        out,
        shares,
    )


def fine_middle(own_qkv, middle, own_up, out, shares, query_part):
    _, own, width = own_qkv.shape
    size = middle.shape[1]
    edge = (size - own) // 2

    def body(q_ref, mid_ref, up_ref, o_ref, share_ref, part_ref, q_out, top, inside, bottom):
        found, *sums = pair_grads(q_ref, (mid_ref,), up_ref, o_ref, share_ref)
        q_out[...] = ((found + part_ref[...]) * SCALE).astype(BF16)
        for at, total in zip((slice(0, 128), slice(128, 256)), sums):
            top[:, at] = total[:edge]
            inside[:, at] = total[edge : edge + own]
            bottom[:, at] = total[edge + own :]

    return pair_call(
        body,
        [jax.ShapeDtypeStruct((own, width), BF16)]
        + [jax.ShapeDtypeStruct((count, 2 * width), F32) for count in (edge, own, edge)],
        "fine_middle",
        1 << 30,
        own_qkv,
        middle,
        own_up,
        out,
        shares,
        query_part,
    )


def beside_each_other(inner, outer):
    first = lax.axis_index("c") == 0
    cells, wide = inner.shape
    inner = inner.astype(F32).reshape(cells // RIM, RIM, wide)
    outer = outer.astype(F32).reshape(cells // RIM, RIM, wide)
    left, right = jnp.where(first, outer, inner), jnp.where(first, inner, outer)
    return jnp.concatenate([left, right], axis=1).reshape(2 * cells, wide)


def add_strips(top, bottom, inner, outer):
    edge, wide = top.shape
    corner = edge // 2

    def body(top_ref, bottom_ref, inner_ref, outer_ref, inner_out, outer_out):
        upper = lax.axis_index("zh") == 0
        cells = inner_ref.shape[0]
        above = top_ref[...] + beside_each_other(inner_ref[:corner], outer_ref[:corner])
        below = bottom_ref[...] + beside_each_other(
            inner_ref[cells - corner :], outer_ref[cells - corner :]
        )
        inner_out[...] = jnp.where(upper, below, above).astype(BF16)
        outer_out[...] = jnp.where(upper, above, below).astype(BF16)

    return whole_call(
        body,
        [jax.ShapeDtypeStruct((edge, wide), BF16)] * 2,
        "add_strips",
        1 << 20,
        [],
        top,
        bottom,
        inner,
        outer,
    )


def add_all(own, side_inner, side_outer, row_inner, row_outer):
    cells, wide = own.shape
    width = wide // 2
    half_cells = cells // 2

    def body(own_ref, side_in, side_out, row_in, row_out, k_out, v_out):
        upper = lax.axis_index("zh") == 0
        corner = (side_in.shape[0] - half_cells) // 2
        middle = slice(corner, corner + half_cells)
        inner, outer = row_in[...].astype(F32), row_out[...].astype(F32)
        above, below = jnp.where(upper, outer, inner), jnp.where(upper, inner, outer)
        total = own_ref[...] + jnp.concatenate([above, below], axis=0)
        total += beside_each_other(side_in[middle], side_out[middle])
        for pair, lanes in pairs_of(width):
            k_out[:, lanes] = total[:, pair * 256 : pair * 256 + 128].astype(BF16)
            v_out[:, lanes] = total[:, pair * 256 + 128 : pair * 256 + 256].astype(BF16)

    return whole_call(
        body,
        [jax.ShapeDtypeStruct((cells, width), BF16)] * 2,
        "add_all",
        1 << 20,
        [],
        own,
        side_inner,
        side_outer,
        row_inner,
        row_outer,
    )


def project(query_pieces, kept, from_core, arrived, joint, columns, count):
    group, tokens = query_pieces[0].shape
    heads = arrived.shape[0]
    rows = tokens // columns
    each = rows // count
    size = each * columns
    wide = joint.shape[1]
    chunk = 256
    blocks = len(query_pieces)

    def body(*refs):
        pieces = refs[:blocks]
        kept_ref, core_ref, arrived_ref, joint_ref, out, held, packed = refs[blocks:]

        @pl.when(pl.program_id(0) == 0)
        def _():
            for head in range(heads):
                total = kept_ref[0, head].astype(F32) + core_ref[0, head].astype(F32)
                total += arrived_ref[head].astype(F32)
                for part in range(2):
                    at = (1 + part) * group + head * HD
                    held[:, at : at + HD] = total[:, part * HD : (part + 1) * HD]
            total = pieces[0][...].astype(F32)
            for piece in pieces[1:]:
                total += piece[...].astype(F32)
            held[:, :group] = total.T
            for target in range(count):
                taken = []
                for c in range(columns):
                    start = c * rows + target * each
                    taken.append(held[start : start + each, :])
                chosen = jnp.concatenate(taken, axis=0).astype(BF16)
                packed[target * size : (target + 1) * size, :] = chosen

        out[...] = nn(packed[...], joint_ref[...]).astype(BF16)

    half_spec = pl.BlockSpec((1, heads, tokens, 128), lambda n: (0, 0, 0, 0))
    return pl.pallas_call(
        body,
        grid=(wide // chunk,),
        in_specs=[pl.BlockSpec((group, tokens), lambda n: (0, 0))] * blocks
        + [half_spec] * 2
        + [
            pl.BlockSpec(arrived.shape, lambda n: (0, 0, 0)),
            pl.BlockSpec((3 * group, chunk), lambda n: (0, n)),
        ],
        out_specs=pl.BlockSpec((tokens, chunk), lambda n: (0, n)),
        out_shape=jax.ShapeDtypeStruct((tokens, wide), BF16),
        scratch_shapes=[
            pltpu.VMEM((tokens, 3 * group), F32),
            pltpu.VMEM((tokens, 3 * group), BF16),
        ],
        name="project",
        cost_estimate=cost(2 << 30, 6 << 20, 0),
        compiler_params=pltpu.CompilerParams(vmem_limit_bytes=VMEM),
    )(*query_pieces, kept, from_core, arrived, joint)


def spread(pieces, columns):
    count, tokens, wide = pieces.shape
    width = wide // 4

    def body(in_ref, out):
        total = in_ref[0].astype(F32)
        for at in range(1, count):
            total += in_ref[at].astype(F32)
        total = total.astype(BF16)
        cells = 2 * tokens
        fine = lax.broadcasted_iota(jnp.int32, (cells, tokens), 0)
        token = lax.broadcasted_iota(jnp.int32, (cells, tokens), 1)
        cell = (token & 7) * 2 * columns + (token >> 3) * 2
        for a in range(2):
            grid = jnp.zeros((cells, width), F32)
            for b in range(2):
                place = jnp.where(fine == cell + b, 1.0, 0.0).astype(BF16)
                lanes = slice((2 * a + b) * width, (2 * a + b + 1) * width)
                grid += nn(place, total[:, lanes])
            grid = grid.astype(BF16)
            for row in range(tokens // columns):
                at = (2 * row + a) * 2 * columns
                out[at : at + 2 * columns, :] = grid[row * 2 * columns : (row + 1) * 2 * columns]

    return whole_call(
        body,
        jax.ShapeDtypeStruct((4 * tokens, width), BF16),
        "spread",
        1 << 28,
        [],
        pieces,
    )


def swapped(array, axis, flip=1):
    return lax.ppermute(array, axis, [(i, i ^ flip) for i in range(lax.axis_size(axis))])


def exchanged(inner, outer, axis):
    count = lax.axis_size(axis)
    beyond = [(i, ((i + 1) ^ 1) - 1) for i in range(1, count - 1)]
    return swapped(inner, axis), lax.ppermute(outer, axis, beyond)


def sent_rims(block, axis, parity, at):
    size = block.shape[at]
    low = lax.slice_in_dim(block, 0, RIM, axis=at)
    high = lax.slice_in_dim(block, size - RIM, None, axis=at)
    first = lax.axis_index(parity) == 0
    return exchanged(jnp.where(first, high, low), jnp.where(first, low, high), axis)


def placed_rims(inner, outer, parity):
    first = lax.axis_index(parity) == 0
    return jnp.where(first, outer, inner), jnp.where(first, inner, outer)


def shards(fine_qkv, coarse_qkv, grad_coarse, merge_weight, qkv_weight):
    rows, columns, width = fine_qkv.shape[1:]
    own = rows * columns
    coarse_columns, coarse_rows, group = grad_coarse.shape
    tokens = coarse_columns * coarse_rows
    wide = merge_weight.shape[0]

    key_value, query_up = prepare(
        coarse_qkv.reshape(3, tokens, group), grad_coarse.reshape(tokens, group)
    )
    across = swapped(key_value, "zl")
    beside = swapped(key_value, "c")
    beside, query_up, merge_weight, fine_qkv = lax.optimization_barrier(
        (beside, query_up, merge_weight, fine_qkv)
    )
    near = [query_up, swapped(query_up, "y", 1), swapped(query_up, "y", 3)]
    own_qkv = fine_qkv.reshape(3, own, width)
    edges = sent_rims(fine_qkv[1:], ROW, "zh", 1)
    joint = lax.dot_general(
        qkv_weight, merge_weight, (((1,), (1,)), ((), ())), preferred_element_type=F32
    ).astype(BF16).reshape(3 * group, wide)
    across, joint, *edges = lax.optimization_barrier((across, joint, *edges))
    corner = swapped(across, "c")
    *near, joint = lax.optimization_barrier((*near, joint))
    far = swapped(near[0], "y", 2)
    keys = [key_value, beside, across, corner]
    queries = [near[0], near[1], far, near[2]]

    part = coarse_stats(keys, near, [0, 1, 3], (), 256)
    part, *edges = lax.optimization_barrier((part, *edges))
    low, high = placed_rims(*edges, "zh")
    tall = jnp.concatenate([low, fine_qkv[1:], high], axis=1)
    edges = sent_rims(tall, COL, "c", 2)
    part = coarse_stats(keys, [far], [2], (part,), 256)
    part, *edges = lax.optimization_barrier((part, *edges))
    stats = [part] + [swapped(part, "y", step) for step in (1, 3, 2)]
    kept, sent, *query_grads = coarse_grads(keys, queries, stats)

    from_core = swapped(sent, "c")
    passed = (kept[1].astype(F32) + from_core[1].astype(F32)).astype(BF16)
    arrived = swapped(passed, "zl")
    query_pieces = [query_grads[0]]
    for step in (1, 2, 3):
        query_pieces.append(swapped(query_grads[step], "y", step))
    count = lax.axis_size(ROW)
    low, high = placed_rims(*edges, "c")
    ext_kv = [array.reshape(2, -1, width) for array in (tall, low, high)]
    mid_shares, side_shares, out = fine_shares(own_qkv, ext_kv, rows, columns)
    arrived, out = lax.optimization_barrier((arrived, out))
    projected = project(
        query_pieces, kept, from_core, arrived, joint, coarse_columns, count
    )
    pieces = lax.all_to_all(projected.reshape(count, -1, wide), ROW, 0, 0)
    own_up = spread(pieces, coarse_columns)

    query_part, inner, outer = fine_sides(own_qkv, ext_kv[1:], own_up, out, side_shares)
    side_inner, side_outer = exchanged(inner, outer, COL)
    grad_query, top, middle, bottom = fine_middle(
        own_qkv, ext_kv[0], own_up, out, mid_shares, query_part
    )
    strips = add_strips(top, bottom, side_inner, side_outer)
    row_inner, row_outer = exchanged(*strips, ROW)
    grad_key, grad_value = add_all(middle, side_inner, side_outer, row_inner, row_outer)
    shape = (rows, columns, width)
    return grad_query.reshape(shape), grad_key.reshape(shape), grad_value.reshape(shape)


def solution(mesh):
    split = Mesh(mesh.devices.reshape(4, 2, 2, 4, 2), ROW + COL)
    return jax.shard_map(
        shards,
        mesh=split,
        in_specs=(
            P(None, ROW, COL, None),
            P(None, COL, None, ROW),
            P(COL, None, ROW),
            P(),
            P(None, None, ROW),
        ),
        out_specs=(P(ROW, COL, None), P(ROW, COL, None), P(ROW, COL, None)),
        check_vma=False,
    )
```

```python
import jax
import jax.numpy as jnp
from jax import lax
from jax.experimental import pallas as pl
from jax.experimental.pallas import tpu as pltpu
from jax.sharding import Mesh
from jax.sharding import PartitionSpec as P

HD = 64
RADIUS = 7
SCALE = 0.125
SIDE = 32
RIM = 8
HIDDEN = -1e30
ROW = ("x", "zh")
COL = ("zl", "y", "c")
F32 = jnp.float32
BF16 = jnp.bfloat16
VMEM = 24 << 20


def nt(left, right):
    return lax.dot_general(left, right, (((1,), (1,)), ((), ())), preferred_element_type=F32)


def nn(left, right):
    return lax.dot_general(left, right, (((1,), (0,)), ((), ())), preferred_element_type=F32)


def half(pair, which):
    lane = lax.broadcasted_iota(jnp.int32, pair.shape, 1)
    return jnp.where((lane < HD) == (which == 0), pair, jnp.zeros_like(pair))


def cost(flops, bytes_accessed, exps):
    return pl.CostEstimate(flops=flops, bytes_accessed=bytes_accessed, transcendentals=exps)


def prepare(coarse_qkv, grad_coarse):
    _, tokens, group = coarse_qkv.shape
    heads = group // HD

    def body(qkv_ref, up_ref, kv_out, qu_out):
        for head in range(heads):
            lanes = slice(head * HD, head * HD + HD)
            kv_out[head] = jnp.concatenate([qkv_ref[1, :, lanes], qkv_ref[2, :, lanes]], axis=1)
            qu_out[head] = jnp.concatenate([qkv_ref[0, :, lanes], up_ref[:, lanes]], axis=1)

    return whole_call(
        body,
        [jax.ShapeDtypeStruct((heads, tokens, 2 * HD), BF16)] * 2,
        "prepare",
        1 << 20,
        [],
        coarse_qkv,
        grad_coarse,
    )


def own_block(step, tokens):
    owner = lax.axis_index("y") ^ step
    return pl.ds(pl.multiple_of(owner * tokens, tokens), tokens)


def coarse_stats(key_values, query_ups, steps, before, key_tile):
    heads, tokens, _ = key_values[0].shape
    blocks, number = len(key_values), len(query_ups)
    per_block = tokens // key_tile

    def body(*refs):
        kv_refs, qu_refs = refs[:blocks], refs[blocks : blocks + number]
        out_ref, held = refs[-2:]
        if before:

            @pl.when(pl.program_id(1) == 0)
            def _():
                out_ref[...] = refs[blocks + number][...]

        for at in range(number):

            @pl.when(pl.program_id(1) == at)
            def _():
                held[...] = qu_refs[at][0]

        query = half(held[...], 0) * BF16(SCALE)
        upstream = half(held[...], 1)
        peak = jnp.full((1, tokens), -jnp.inf, F32)
        total = jnp.zeros((1, tokens), F32)
        weighted = jnp.zeros((1, tokens), F32)
        for i in range(blocks * per_block):
            start = (i % per_block) * key_tile
            tile = kv_refs[i // per_block][0, start : start + key_tile, :]
            score = nt(tile, query)
            product = nt(tile, upstream)
            new_peak = jnp.maximum(peak, jnp.max(score, axis=0, keepdims=True))
            decay = jnp.exp(peak - new_peak)
            share = jnp.exp(score - new_peak)
            total = total * decay + jnp.sum(share, axis=0, keepdims=True)
            weighted = weighted * decay + jnp.sum(share * product, axis=0, keepdims=True)
            peak = new_peak
        found = jnp.concatenate([peak + jnp.log(total), weighted / total], axis=0)
        for at, step in enumerate(steps):

            @pl.when(pl.program_id(1) == at)
            def _():
                out_ref[0, :, own_block(step, tokens)] = found

    pairs = heads * number * blocks * tokens**2
    return pl.pallas_call(
        body,
        grid=(heads, number),
        in_specs=[pl.BlockSpec((1, tokens, 128), lambda h, q: (h, 0, 0))] * (blocks + number)
        + [pl.BlockSpec((1, 2, blocks * tokens), lambda h, q: (h, 0, 0))] * len(before),
        out_specs=pl.BlockSpec((1, 2, blocks * tokens), lambda h, q: (h, 0, 0)),
        out_shape=jax.ShapeDtypeStruct((heads, 2, blocks * tokens), F32),
        scratch_shapes=[pltpu.VMEM((tokens, 128), BF16)],
        name="coarse_stats",
        cost_estimate=cost(4 * pairs * 256, 2 << 20, pairs),
        compiler_params=pltpu.CompilerParams(vmem_limit_bytes=VMEM),
    )(*key_values, *query_ups, *before)


def coarse_grads(key_values, query_ups, stats):
    heads, tokens, _ = key_values[0].shape
    blocks = len(query_ups)
    parts = len(stats)

    def body(*refs):
        kv_refs, qu_refs = refs[:blocks], refs[blocks : 2 * blocks]
        stats_refs = refs[2 * blocks : 2 * blocks + parts]
        kept_ref, sent_ref = refs[2 * blocks + parts : 2 * blocks + parts + 2]
        q_outs = refs[-blocks - 2 : -2]
        acc, held = refs[-2:]
        step = pl.program_id(1)
        for at in range(blocks):

            @pl.when(pl.program_id(1) == at)
            def _():
                held[...] = qu_refs[at][0]

        @pl.when(pl.program_id(1) == 0)
        def _():
            acc[...] = jnp.zeros_like(acc)

        query = half(held[...], 0) * BF16(SCALE)
        upstream = half(held[...], 1)
        found = [ref[0, :, own_block(step, tokens)] for ref in stats_refs]
        peak = found[0][:1]
        for part in found[1:]:
            peak = jnp.maximum(peak, part[:1])
        shares = [jnp.exp(part[:1] - peak) for part in found]
        total = sum(shares)
        log_total = peak + jnp.log(total)
        delta = sum(share * part[1:] for share, part in zip(shares, found)) / total
        found = jnp.zeros((HD, tokens), F32)
        for i in range(blocks):
            tile = kv_refs[i][0]
            share = jnp.exp(nt(tile, query) - log_total)
            grads = (share * (nt(tile, upstream) - delta)).astype(BF16)
            acc[i] += nn(grads, query) + nn(share.astype(BF16), upstream)
            found += nn(tile[:, :HD].T, grads)
        found = (found * SCALE).astype(BF16)
        for at in range(blocks):

            @pl.when(pl.program_id(1) == at)
            def _():
                q_outs[at][...] = found

        @pl.when(pl.program_id(1) == blocks - 1)
        def _():
            for i in range(blocks // 2):
                kept_ref[i, 0] = acc[2 * i].astype(BF16)
                sent_ref[i, 0] = acc[2 * i + 1].astype(BF16)

    pairs = heads * (blocks * tokens) ** 2
    out_shape = [jax.ShapeDtypeStruct((blocks // 2, heads, tokens, 128), BF16)] * 2
    out_shape += [jax.ShapeDtypeStruct((heads * HD, tokens), BF16)] * blocks
    return pl.pallas_call(
        body,
        grid=(heads, blocks),
        in_specs=[pl.BlockSpec((1, tokens, 128), lambda h, q: (h, 0, 0))] * (2 * blocks)
        + [pl.BlockSpec((1, 2, blocks * tokens), lambda h, q: (h, 0, 0))] * parts,
        out_specs=[pl.BlockSpec((blocks // 2, 1, tokens, 128), lambda h, q: (0, h, 0, 0))] * 2
        + [pl.BlockSpec((HD, tokens), lambda h, q: (h, 0))] * blocks,
        out_shape=out_shape,
        scratch_shapes=[
            pltpu.VMEM((blocks, tokens, 128), F32),
            pltpu.VMEM((tokens, 128), BF16),
        ],
        name="coarse_grads",
        cost_estimate=cost(10 * pairs * 256, 4 << 20, pairs),
        compiler_params=pltpu.CompilerParams(vmem_limit_bytes=VMEM),
    )(*key_values, *query_ups, *stats)


def whole_call(body, out_shape, name, flops, scratch, *operands):
    return pl.pallas_call(
        body,
        out_shape=out_shape,
        scratch_shapes=scratch,
        name=name,
        cost_estimate=cost(flops, 6 << 20, 1 << 20),
        compiler_params=pltpu.CompilerParams(vmem_limit_bytes=VMEM),
    )(*operands)


def pairs_of(width):
    return [(pair, slice(pair * 128, pair * 128 + 128)) for pair in range(width // 128)]


def window_bias(own, rows, columns, part, transposed):
    count = SIDE * SIDE // 2
    shape = (own, count) if transposed else (count, own)
    ext = lax.broadcasted_iota(jnp.int32, shape, 1 if transposed else 0)
    inner = lax.broadcasted_iota(jnp.int32, shape, 0 if transposed else 1)
    if part == 0:
        ext_row, ext_column = ext >> 4, (ext & 15) + RIM
    else:
        ext_row = (ext & 255) >> 3
        ext_column = (ext & 7) + jnp.where(ext >= 256, SIDE - RIM, 0)
    row_gap = ext_row - (inner >> 4) - RIM
    column_gap = ext_column - (inner & 15) - RIM
    row = ext_row + (lax.axis_index(ROW) * rows - RIM)
    column = ext_column + (lax.axis_index(COL) * columns - RIM)
    seen = (jnp.abs(row_gap) <= RADIUS) & (jnp.abs(column_gap) <= RADIUS)
    seen &= (row >= 0) & (row < lax.axis_size(ROW) * rows)
    seen &= (column >= 0) & (column < lax.axis_size(COL) * columns)
    return jnp.where(seen, 0.0, HIDDEN).astype(F32)


def fill_bias(bias_ref, own, rows, columns):
    count = SIDE * SIDE // 2
    for part in range(2):
        bias_ref[part * count : (part + 1) * count, :] = window_bias(
            own, rows, columns, part, False
        )


def stacked(refs, which, lanes):
    return jnp.concatenate([ref[which, :, lanes] for ref in refs], axis=0)


def fine_shares(own_qkv, ext_kv, rows, columns):
    _, own, width = own_qkv.shape
    heads = width // HD
    count = SIDE * SIDE // 2

    def body(q_ref, mid_ref, low_ref, high_ref, mid_out, side_out, o_ref, bias_ref):
        fill_bias(bias_ref, own, rows, columns)
        ext = (mid_ref, low_ref, high_ref)
        for pair, lanes in pairs_of(width):
            key = stacked(ext, 0, lanes)
            value_t = stacked(ext, 1, lanes).T
            parts = []
            for side in range(2):
                query = half(q_ref[0, :, lanes], side) * BF16(SCALE)
                score = nt(key, query) + bias_ref[...]
                share = jnp.exp(score - jnp.max(score, axis=0, keepdims=True))
                total = jnp.sum(share, axis=0, keepdims=True)
                rounded = (share * (1.0 / total)).astype(BF16)
                mid_out[2 * pair + side] = rounded[:count]
                side_out[2 * pair + side] = rounded[count:]
                total = jnp.sum(rounded.astype(F32), axis=0, keepdims=True)
                parts.append(nn(value_t[side * HD : side * HD + HD], rounded) / total)
            o_ref[:, lanes] = jnp.concatenate(parts, axis=0).T

    return whole_call(
        body,
        [jax.ShapeDtypeStruct((heads, count, own), BF16)] * 2
        + [jax.ShapeDtypeStruct((own, width), F32)],
        "fine_shares",
        1 << 30,
        [pltpu.VMEM((SIDE * SIDE, own), F32)],
        own_qkv,
        *ext_kv,
    )


def pair_call(body, out_shape, name, flops, *operands):
    width = 384
    pairs = width // 128

    def spec(array):
        shape = tuple(array.shape)
        rank = len(shape)
        if shape[0] == 2 * pairs:
            return pl.BlockSpec((2,) + shape[1:], lambda p: (p,) + (0,) * (rank - 1))
        return pl.BlockSpec(
            shape[:-1] + (shape[-1] // pairs,), lambda p: (0,) * (rank - 1) + (p,)
        )

    return pl.pallas_call(
        body,
        grid=(pairs,),
        in_specs=[spec(array) for array in operands],
        out_specs=[spec(shape) for shape in out_shape],
        out_shape=out_shape,
        name=name,
        cost_estimate=cost(flops, 6 << 20, 0),
        compiler_params=pltpu.CompilerParams(vmem_limit_bytes=VMEM),
    )(*operands)


def head_sums(up, out):
    head = lax.broadcasted_iota(jnp.int32, (8, up.shape[1]), 0)
    lane = lax.broadcasted_iota(jnp.int32, (8, up.shape[1]), 1)
    pick = jnp.where((lane >> 6) == head, 1.0, 0.0).astype(F32)
    return lax.dot_general(
        pick,
        up * out,
        (((1,), (1,)), ((), ())),
        preferred_element_type=F32,
        precision=lax.Precision.HIGHEST,
    )


def pair_grads(q_ref, ext, up_ref, o_ref, share_ref):
    delta = head_sums(up_ref[...].astype(F32), o_ref[...])
    key = jnp.concatenate([ref[0] for ref in ext], axis=0)
    key_t = key.T
    value = jnp.concatenate([ref[1] for ref in ext], axis=0)
    parts = []
    key_sum = jnp.zeros(key.shape, F32)
    value_sum = jnp.zeros(key.shape, F32)
    for side in range(2):
        query = half(q_ref[0], side) * BF16(SCALE)
        up = half(up_ref[...], side)
        rounded = share_ref[side]
        product = nt(value, up) - delta[side : side + 1]
        grads = (rounded.astype(F32) * product).astype(BF16)
        key_sum += nn(grads, query)
        value_sum += nn(rounded, up)
        parts.append(nn(key_t[side * HD : side * HD + HD], grads))
    return jnp.concatenate(parts, axis=0).T, key_sum, value_sum


def fine_sides(own_qkv, sides, own_up, out, shares):
    _, own, width = own_qkv.shape
    size = sides[0].shape[1]

    def body(q_ref, low_ref, high_ref, up_ref, o_ref, share_ref, q_out, inner_out, outer_out):
        first = lax.axis_index("c") == 0
        q_out[...], *sums = pair_grads(q_ref, (low_ref, high_ref), up_ref, o_ref, share_ref)
        for at, total in zip((slice(0, 128), slice(128, 256)), sums):
            low, high = total[:size].astype(BF16), total[size:].astype(BF16)
            inner_out[:, at] = jnp.where(first, high, low)
            outer_out[:, at] = jnp.where(first, low, high)

    return pair_call(
        body,
        [jax.ShapeDtypeStruct((own, width), F32)]
        + [jax.ShapeDtypeStruct((size, 2 * width), BF16)] * 2,
        "fine_sides",
        1 << 30,
        own_qkv,
        *sides,
        own_up,
        out,
        shares,
    )


def fine_middle(own_qkv, middle, own_up, out, shares, query_part):
    _, own, width = own_qkv.shape
    size = middle.shape[1]
    edge = (size - own) // 2

    def body(q_ref, mid_ref, up_ref, o_ref, share_ref, part_ref, q_out, top, inside, bottom):
        found, *sums = pair_grads(q_ref, (mid_ref,), up_ref, o_ref, share_ref)
        q_out[...] = ((found + part_ref[...]) * SCALE).astype(BF16)
        for at, total in zip((slice(0, 128), slice(128, 256)), sums):
            top[:, at] = total[:edge]
            inside[:, at] = total[edge : edge + own]
            bottom[:, at] = total[edge + own :]

    return pair_call(
        body,
        [jax.ShapeDtypeStruct((own, width), BF16)]
        + [jax.ShapeDtypeStruct((count, 2 * width), F32) for count in (edge, own, edge)],
        "fine_middle",
        1 << 30,
        own_qkv,
        middle,
        own_up,
        out,
        shares,
        query_part,
    )


def beside_each_other(inner, outer):
    first = lax.axis_index("c") == 0
    cells, wide = inner.shape
    inner = inner.astype(F32).reshape(cells // RIM, RIM, wide)
    outer = outer.astype(F32).reshape(cells // RIM, RIM, wide)
    left, right = jnp.where(first, outer, inner), jnp.where(first, inner, outer)
    return jnp.concatenate([left, right], axis=1).reshape(2 * cells, wide)


def add_strips(top, bottom, inner, outer):
    edge, wide = top.shape
    corner = edge // 2
    sent = edge // RIM * RADIUS

    def body(top_ref, bottom_ref, inner_ref, outer_ref, inner_out, outer_out):
        upper = lax.axis_index("zh") == 0
        cells = inner_ref.shape[0]
        above = top_ref[...] + beside_each_other(inner_ref[:corner], outer_ref[:corner])
        below = bottom_ref[...] + beside_each_other(
            inner_ref[cells - corner :], outer_ref[cells - corner :]
        )
        above, below = above[edge - sent :], below[:sent]
        inner_out[...] = jnp.where(upper, below, above).astype(BF16)
        outer_out[...] = jnp.where(upper, above, below).astype(BF16)

    return whole_call(
        body,
        [jax.ShapeDtypeStruct((sent, wide), BF16)] * 2,
        "add_strips",
        1 << 20,
        [],
        top,
        bottom,
        inner,
        outer,
    )


def add_all(own, side_inner, side_outer, row_inner, row_outer):
    cells, wide = own.shape
    width = wide // 2
    half_cells = cells // 2

    def body(own_ref, side_in, side_out, row_in, row_out, k_out, v_out):
        upper = lax.axis_index("zh") == 0
        corner = (side_in.shape[0] - half_cells) // 2
        middle = slice(corner, corner + half_cells)
        inner, outer = row_in[...].astype(F32), row_out[...].astype(F32)
        above, below = jnp.where(upper, outer, inner), jnp.where(upper, inner, outer)
        skipped = jnp.zeros((cells - 2 * above.shape[0], wide), F32)
        total = own_ref[...] + jnp.concatenate([above, skipped, below], axis=0)
        total += beside_each_other(side_in[middle], side_out[middle])
        for pair, lanes in pairs_of(width):
            k_out[:, lanes] = total[:, pair * 256 : pair * 256 + 128].astype(BF16)
            v_out[:, lanes] = total[:, pair * 256 + 128 : pair * 256 + 256].astype(BF16)

    return whole_call(
        body,
        [jax.ShapeDtypeStruct((cells, width), BF16)] * 2,
        "add_all",
        1 << 20,
        [],
        own,
        side_inner,
        side_outer,
        row_inner,
        row_outer,
    )


def project(query_pieces, kept, from_core, arrived, joint, columns, count):
    group, tokens = query_pieces[0].shape
    heads = arrived.shape[0]
    rows = tokens // columns
    each = rows // count
    size = each * columns
    wide = joint.shape[1]
    chunk = 512
    blocks = len(query_pieces)

    def body(*refs):
        pieces = refs[:blocks]
        kept_ref, core_ref, arrived_ref, joint_ref, out, held, packed = refs[blocks:]

        @pl.when(pl.program_id(0) == 0)
        def _():
            for head in range(heads):
                total = kept_ref[0, head].astype(F32) + core_ref[0, head].astype(F32)
                total += arrived_ref[head].astype(F32)
                for part in range(2):
                    at = (1 + part) * group + head * HD
                    held[:, at : at + HD] = total[:, part * HD : (part + 1) * HD]
            total = pieces[0][...].astype(F32)
            for piece in pieces[1:]:
                total += piece[...].astype(F32)
            held[:, :group] = total.T
            for target in range(count):
                taken = []
                for c in range(columns):
                    start = c * rows + target * each
                    taken.append(held[start : start + each, :])
                chosen = jnp.concatenate(taken, axis=0).astype(BF16)
                packed[target * size : (target + 1) * size, :] = chosen

        out[...] = nn(packed[...], joint_ref[...]).astype(BF16)

    half_spec = pl.BlockSpec((1, heads, tokens, 128), lambda n: (0, 0, 0, 0))
    return pl.pallas_call(
        body,
        grid=(wide // chunk,),
        in_specs=[pl.BlockSpec((group, tokens), lambda n: (0, 0))] * blocks
        + [half_spec] * 2
        + [
            pl.BlockSpec(arrived.shape, lambda n: (0, 0, 0)),
            pl.BlockSpec((3 * group, chunk), lambda n: (0, n)),
        ],
        out_specs=pl.BlockSpec((tokens, chunk), lambda n: (0, n)),
        out_shape=jax.ShapeDtypeStruct((tokens, wide), BF16),
        scratch_shapes=[
            pltpu.VMEM((tokens, 3 * group), F32),
            pltpu.VMEM((tokens, 3 * group), BF16),
        ],
        name="project",
        cost_estimate=cost(2 << 30, 6 << 20, 0),
        compiler_params=pltpu.CompilerParams(vmem_limit_bytes=VMEM),
    )(*query_pieces, kept, from_core, arrived, joint)


def spread(pieces, columns):
    count, tokens, wide = pieces.shape
    width = wide // 4

    def body(in_ref, out):
        total = in_ref[0].astype(F32)
        for at in range(1, count):
            total += in_ref[at].astype(F32)
        total = total.astype(BF16)
        cells = 2 * tokens
        fine = lax.broadcasted_iota(jnp.int32, (cells, tokens), 0)
        token = lax.broadcasted_iota(jnp.int32, (cells, tokens), 1)
        cell = (token & 7) * 2 * columns + (token >> 3) * 2
        for a in range(2):
            grid = jnp.zeros((cells, width), F32)
            for b in range(2):
                place = jnp.where(fine == cell + b, 1.0, 0.0).astype(BF16)
                lanes = slice((2 * a + b) * width, (2 * a + b + 1) * width)
                grid += nn(place, total[:, lanes])
            grid = grid.astype(BF16)
            for row in range(tokens // columns):
                at = (2 * row + a) * 2 * columns
                out[at : at + 2 * columns, :] = grid[row * 2 * columns : (row + 1) * 2 * columns]

    return whole_call(
        body,
        jax.ShapeDtypeStruct((4 * tokens, width), BF16),
        "spread",
        1 << 28,
        [],
        pieces,
    )


def swapped(array, axis, flip=1):
    return lax.ppermute(array, axis, [(i, i ^ flip) for i in range(lax.axis_size(axis))])


def exchanged(inner, outer, axis):
    count = lax.axis_size(axis)
    beyond = [(i, ((i + 1) ^ 1) - 1) for i in range(1, count - 1)]
    return swapped(inner, axis), lax.ppermute(outer, axis, beyond)


def sent_rims(block, axis, parity, at):
    size = block.shape[at]
    low = lax.slice_in_dim(block, 0, RIM, axis=at)
    high = lax.slice_in_dim(block, size - RIM, None, axis=at)
    first = lax.axis_index(parity) == 0
    return exchanged(jnp.where(first, high, low), jnp.where(first, low, high), axis)


def placed_rims(inner, outer, parity):
    first = lax.axis_index(parity) == 0
    return jnp.where(first, outer, inner), jnp.where(first, inner, outer)


def shards(fine_qkv, coarse_qkv, grad_coarse, merge_weight, qkv_weight):
    rows, columns, width = fine_qkv.shape[1:]
    own = rows * columns
    coarse_columns, coarse_rows, group = grad_coarse.shape
    tokens = coarse_columns * coarse_rows
    wide = merge_weight.shape[0]

    key_value, query_up = prepare(
        coarse_qkv.reshape(3, tokens, group), grad_coarse.reshape(tokens, group)
    )
    across = swapped(key_value, "zl")
    beside = swapped(key_value, "c")
    beside, query_up, merge_weight, fine_qkv = lax.optimization_barrier(
        (beside, query_up, merge_weight, fine_qkv)
    )
    near = [query_up, swapped(query_up, "y", 1), swapped(query_up, "y", 3)]
    own_qkv = fine_qkv.reshape(3, own, width)
    edges = sent_rims(fine_qkv[1:], ROW, "zh", 1)
    joint = lax.dot_general(
        qkv_weight, merge_weight, (((1,), (1,)), ((), ())), preferred_element_type=F32
    ).astype(BF16).reshape(3 * group, wide)
    across, joint, *edges = lax.optimization_barrier((across, joint, *edges))
    corner = swapped(across, "c")
    *near, joint = lax.optimization_barrier((*near, joint))
    far = swapped(near[0], "y", 2)
    keys = [key_value, beside, across, corner]
    queries = [near[0], near[1], far, near[2]]

    part = coarse_stats(keys, near, [0, 1, 3], (), 256)
    part, *edges = lax.optimization_barrier((part, *edges))
    low, high = placed_rims(*edges, "zh")
    tall = jnp.concatenate([low, fine_qkv[1:], high], axis=1)
    edges = sent_rims(tall, COL, "c", 2)
    part = coarse_stats(keys, [far], [2], (part,), 256)
    part, *edges = lax.optimization_barrier((part, *edges))
    stats = [part] + [swapped(part, "y", step) for step in (1, 3, 2)]
    kept, sent, *query_grads = coarse_grads(keys, queries, stats)

    from_core = swapped(sent, "c")
    passed = (kept[1].astype(F32) + from_core[1].astype(F32)).astype(BF16)
    arrived = swapped(passed, "zl")
    query_pieces = [query_grads[0]]
    for step in (1, 2, 3):
        query_pieces.append(swapped(query_grads[step], "y", step))
    count = lax.axis_size(ROW)
    low, high = placed_rims(*edges, "c")
    ext_kv = [array.reshape(2, -1, width) for array in (tall, low, high)]
    mid_shares, side_shares, out = fine_shares(own_qkv, ext_kv, rows, columns)
    arrived, out = lax.optimization_barrier((arrived, out))
    projected = project(
        query_pieces, kept, from_core, arrived, joint, coarse_columns, count
    )
    pieces = lax.all_to_all(projected.reshape(count, -1, wide), ROW, 0, 0)
    own_up = spread(pieces, coarse_columns)

    query_part, inner, outer = fine_sides(own_qkv, ext_kv[1:], own_up, out, side_shares)
    side_inner, side_outer = exchanged(inner, outer, COL)
    grad_query, top, middle, bottom = fine_middle(
        own_qkv, ext_kv[0], own_up, out, mid_shares, query_part
    )
    strips = add_strips(top, bottom, side_inner, side_outer)
    row_inner, row_outer = exchanged(*strips, ROW)
    grad_key, grad_value = add_all(middle, side_inner, side_outer, row_inner, row_outer)
    shape = (rows, columns, width)
    return grad_query.reshape(shape), grad_key.reshape(shape), grad_value.reshape(shape)


def solution(mesh):
    split = Mesh(mesh.devices.reshape(4, 2, 2, 4, 2), ROW + COL)
    return jax.shard_map(
        shards,
        mesh=split,
        in_specs=(
            P(None, ROW, COL, None),
            P(None, COL, None, ROW),
            P(COL, None, ROW),
            P(),
            P(None, None, ROW),
        ),
        out_specs=(P(ROW, COL, None), P(ROW, COL, None), P(ROW, COL, None)),
        check_vma=False,
    )
```

```python
import jax
import jax.numpy as jnp
from jax import lax
from jax.experimental import pallas as pl
from jax.experimental.pallas import tpu as pltpu
from jax.sharding import Mesh
from jax.sharding import PartitionSpec as P

HD = 64
RADIUS = 7
SCALE = 0.125
SIDE = 32
RIM = 8
HIDDEN = -1e30
ROW = ("x", "zh")
COL = ("zl", "y", "c")
F32 = jnp.float32
BF16 = jnp.bfloat16
VMEM = 24 << 20


def nt(left, right):
    return lax.dot_general(left, right, (((1,), (1,)), ((), ())), preferred_element_type=F32)


def nn(left, right):
    return lax.dot_general(left, right, (((1,), (0,)), ((), ())), preferred_element_type=F32)


def half(pair, which):
    lane = lax.broadcasted_iota(jnp.int32, pair.shape, 1)
    return jnp.where((lane < HD) == (which == 0), pair, jnp.zeros_like(pair))


def cost(flops, bytes_accessed, exps):
    return pl.CostEstimate(flops=flops, bytes_accessed=bytes_accessed, transcendentals=exps)


def prepare(coarse_qkv, grad_coarse):
    _, tokens, group = coarse_qkv.shape
    heads = group // HD

    def body(qkv_ref, up_ref, kv_out, qu_out):
        for head in range(heads):
            lanes = slice(head * HD, head * HD + HD)
            kv_out[head] = jnp.concatenate([qkv_ref[1, :, lanes], qkv_ref[2, :, lanes]], axis=1)
            qu_out[head] = jnp.concatenate([qkv_ref[0, :, lanes], up_ref[:, lanes]], axis=1)

    return whole_call(
        body,
        [jax.ShapeDtypeStruct((heads, tokens, 2 * HD), BF16)] * 2,
        "prepare",
        1 << 20,
        [],
        coarse_qkv,
        grad_coarse,
    )


def own_block(step, tokens):
    owner = lax.axis_index("y") ^ step
    return pl.ds(pl.multiple_of(owner * tokens, tokens), tokens)


def coarse_stats(key_values, query_ups, steps, before, key_tile):
    heads, tokens, _ = key_values[0].shape
    blocks, number = len(key_values), len(query_ups)
    per_block = tokens // key_tile

    def body(*refs):
        kv_refs, qu_refs = refs[:blocks], refs[blocks : blocks + number]
        out_ref, held = refs[-2:]
        if before:

            @pl.when(pl.program_id(1) == 0)
            def _():
                out_ref[...] = refs[blocks + number][...]

        for at in range(number):

            @pl.when(pl.program_id(1) == at)
            def _():
                held[...] = qu_refs[at][0]

        query = half(held[...], 0) * BF16(SCALE)
        upstream = half(held[...], 1)
        peak = jnp.full((1, tokens), -jnp.inf, F32)
        total = jnp.zeros((1, tokens), F32)
        weighted = jnp.zeros((1, tokens), F32)
        for i in range(blocks * per_block):
            start = (i % per_block) * key_tile
            tile = kv_refs[i // per_block][0, start : start + key_tile, :]
            score = nt(tile, query)
            product = nt(tile, upstream)
            new_peak = jnp.maximum(peak, jnp.max(score, axis=0, keepdims=True))
            decay = jnp.exp(peak - new_peak)
            share = jnp.exp(score - new_peak)
            total = total * decay + jnp.sum(share, axis=0, keepdims=True)
            weighted = weighted * decay + jnp.sum(share * product, axis=0, keepdims=True)
            peak = new_peak
        found = jnp.concatenate([peak + jnp.log(total), weighted / total], axis=0)
        for at, step in enumerate(steps):

            @pl.when(pl.program_id(1) == at)
            def _():
                out_ref[0, :, own_block(step, tokens)] = found

    pairs = heads * number * blocks * tokens**2
    return pl.pallas_call(
        body,
        grid=(heads, number),
        in_specs=[pl.BlockSpec((1, tokens, 128), lambda h, q: (h, 0, 0))] * (blocks + number)
        + [pl.BlockSpec((1, 2, blocks * tokens), lambda h, q: (h, 0, 0))] * len(before),
        out_specs=pl.BlockSpec((1, 2, blocks * tokens), lambda h, q: (h, 0, 0)),
        out_shape=jax.ShapeDtypeStruct((heads, 2, blocks * tokens), F32),
        scratch_shapes=[pltpu.VMEM((tokens, 128), BF16)],
        name="coarse_stats",
        cost_estimate=cost(4 * pairs * 256, 2 << 20, pairs),
        compiler_params=pltpu.CompilerParams(vmem_limit_bytes=VMEM),
    )(*key_values, *query_ups, *before)


def coarse_grads(key_values, query_ups, stats):
    heads, tokens, _ = key_values[0].shape
    blocks = len(query_ups)
    parts = len(stats)

    def body(*refs):
        kv_refs, qu_refs = refs[:blocks], refs[blocks : 2 * blocks]
        stats_refs = refs[2 * blocks : 2 * blocks + parts]
        kept_ref, sent_ref = refs[2 * blocks + parts : 2 * blocks + parts + 2]
        q_outs = refs[-blocks - 2 : -2]
        acc, held = refs[-2:]
        step = pl.program_id(1)
        for at in range(blocks):

            @pl.when(step == at // 2)
            def _():
                held[at % 2 * tokens : (at % 2 + 1) * tokens] = qu_refs[at][0]

        @pl.when(pl.program_id(1) == 0)
        def _():
            acc[...] = jnp.zeros_like(acc)

        query = half(held[...], 0) * BF16(SCALE)
        upstream = half(held[...], 1)
        found = [
            jnp.concatenate(
                [ref[0, :, own_block(2 * step + i, tokens)] for i in range(2)], axis=1
            )
            for ref in stats_refs
        ]
        peak = found[0][:1]
        for part in found[1:]:
            peak = jnp.maximum(peak, part[:1])
        shares = [jnp.exp(part[:1] - peak) for part in found]
        total = sum(shares)
        log_total = peak + jnp.log(total)
        delta = sum(share * part[1:] for share, part in zip(shares, found)) / total
        found = jnp.zeros((HD, 2 * tokens), F32)
        both = jnp.concatenate([query, upstream], axis=0)
        for i in range(blocks):
            tile = kv_refs[i][0]
            share = jnp.exp(nt(tile, query) - log_total)
            grads = (share * (nt(tile, upstream) - delta)).astype(BF16)
            acc[i] += nn(jnp.concatenate([grads, share.astype(BF16)], axis=1), both)
            found += nn(tile[:, :HD].T, grads)
        found = (found * SCALE).astype(BF16)
        for at in range(blocks):

            @pl.when(step == at // 2)
            def _():
                q_outs[at][...] = found[:, at % 2 * tokens : (at % 2 + 1) * tokens]

        @pl.when(step == blocks // 2 - 1)
        def _():
            for i in range(blocks // 2):
                kept_ref[i, 0] = acc[2 * i].astype(BF16)
                sent_ref[i, 0] = acc[2 * i + 1].astype(BF16)

    pairs = heads * (blocks * tokens) ** 2
    out_shape = [jax.ShapeDtypeStruct((blocks // 2, heads, tokens, 128), BF16)] * 2
    out_shape += [jax.ShapeDtypeStruct((heads * HD, tokens), BF16)] * blocks
    return pl.pallas_call(
        body,
        grid=(heads, blocks // 2),
        in_specs=[pl.BlockSpec((1, tokens, 128), lambda h, q: (h, 0, 0))] * (2 * blocks)
        + [pl.BlockSpec((1, 2, blocks * tokens), lambda h, q: (h, 0, 0))] * parts,
        out_specs=[pl.BlockSpec((blocks // 2, 1, tokens, 128), lambda h, q: (0, h, 0, 0))] * 2
        + [pl.BlockSpec((HD, tokens), lambda h, q: (h, 0))] * blocks,
        out_shape=out_shape,
        scratch_shapes=[
            pltpu.VMEM((blocks, tokens, 128), F32),
            pltpu.VMEM((2 * tokens, 128), BF16),
        ],
        name="coarse_grads",
        cost_estimate=cost(10 * pairs * 256, 4 << 20, pairs),
        compiler_params=pltpu.CompilerParams(vmem_limit_bytes=VMEM),
    )(*key_values, *query_ups, *stats)


def whole_call(body, out_shape, name, flops, scratch, *operands):
    return pl.pallas_call(
        body,
        out_shape=out_shape,
        scratch_shapes=scratch,
        name=name,
        cost_estimate=cost(flops, 6 << 20, 1 << 20),
        compiler_params=pltpu.CompilerParams(vmem_limit_bytes=VMEM),
    )(*operands)


def pairs_of(width):
    return [(pair, slice(pair * 128, pair * 128 + 128)) for pair in range(width // 128)]


def window_bias(own, rows, columns, part, transposed):
    count = SIDE * SIDE // 2
    shape = (own, count) if transposed else (count, own)
    ext = lax.broadcasted_iota(jnp.int32, shape, 1 if transposed else 0)
    inner = lax.broadcasted_iota(jnp.int32, shape, 0 if transposed else 1)
    if part == 0:
        ext_row, ext_column = ext >> 4, (ext & 15) + RIM
    else:
        ext_row = (ext & 255) >> 3
        ext_column = (ext & 7) + jnp.where(ext >= 256, SIDE - RIM, 0)
    row_gap = ext_row - (inner >> 4) - RIM
    column_gap = ext_column - (inner & 15) - RIM
    row = ext_row + (lax.axis_index(ROW) * rows - RIM)
    column = ext_column + (lax.axis_index(COL) * columns - RIM)
    seen = (jnp.abs(row_gap) <= RADIUS) & (jnp.abs(column_gap) <= RADIUS)
    seen &= (row >= 0) & (row < lax.axis_size(ROW) * rows)
    seen &= (column >= 0) & (column < lax.axis_size(COL) * columns)
    return jnp.where(seen, 0.0, HIDDEN).astype(F32)


def fill_bias(bias_ref, own, rows, columns):
    count = SIDE * SIDE // 2
    for part in range(2):
        bias_ref[part * count : (part + 1) * count, :] = window_bias(
            own, rows, columns, part, False
        )


def stacked(refs, which, lanes):
    return jnp.concatenate([ref[which, :, lanes] for ref in refs], axis=0)


def fine_shares(own_qkv, ext_kv, rows, columns):
    _, own, width = own_qkv.shape
    heads = width // HD
    count = SIDE * SIDE // 2

    def body(q_ref, mid_ref, low_ref, high_ref, mid_out, side_out, o_ref, bias_ref):
        fill_bias(bias_ref, own, rows, columns)
        ext = (mid_ref, low_ref, high_ref)
        for pair, lanes in pairs_of(width):
            key = stacked(ext, 0, lanes)
            value_t = stacked(ext, 1, lanes).T
            parts = []
            for side in range(2):
                query = half(q_ref[0, :, lanes], side) * BF16(SCALE)
                score = nt(key, query) + bias_ref[...]
                share = jnp.exp(score - jnp.max(score, axis=0, keepdims=True))
                total = jnp.sum(share, axis=0, keepdims=True)
                rounded = (share * (1.0 / total)).astype(BF16)
                mid_out[2 * pair + side] = rounded[:count]
                side_out[2 * pair + side] = rounded[count:]
                total = jnp.sum(rounded.astype(F32), axis=0, keepdims=True)
                parts.append(nn(value_t[side * HD : side * HD + HD], rounded) / total)
            o_ref[:, lanes] = jnp.concatenate(parts, axis=0).T

    return whole_call(
        body,
        [jax.ShapeDtypeStruct((heads, count, own), BF16)] * 2
        + [jax.ShapeDtypeStruct((own, width), F32)],
        "fine_shares",
        1 << 30,
        [pltpu.VMEM((SIDE * SIDE, own), F32)],
        own_qkv,
        *ext_kv,
    )


def pair_call(body, out_shape, name, flops, *operands):
    width = 384
    pairs = width // 128

    def spec(array):
        shape = tuple(array.shape)
        rank = len(shape)
        if shape[0] == 2 * pairs:
            return pl.BlockSpec((2,) + shape[1:], lambda p: (p,) + (0,) * (rank - 1))
        return pl.BlockSpec(
            shape[:-1] + (shape[-1] // pairs,), lambda p: (0,) * (rank - 1) + (p,)
        )

    return pl.pallas_call(
        body,
        grid=(pairs,),
        in_specs=[spec(array) for array in operands],
        out_specs=[spec(shape) for shape in out_shape],
        out_shape=out_shape,
        name=name,
        cost_estimate=cost(flops, 6 << 20, 0),
        compiler_params=pltpu.CompilerParams(vmem_limit_bytes=VMEM),
    )(*operands)


def head_sums(up, out):
    head = lax.broadcasted_iota(jnp.int32, (8, up.shape[1]), 0)
    lane = lax.broadcasted_iota(jnp.int32, (8, up.shape[1]), 1)
    pick = jnp.where((lane >> 6) == head, 1.0, 0.0).astype(F32)
    return lax.dot_general(
        pick,
        up * out,
        (((1,), (1,)), ((), ())),
        preferred_element_type=F32,
        precision=lax.Precision.HIGHEST,
    )


def pair_grads(q_ref, ext, up_ref, o_ref, share_ref):
    delta = head_sums(up_ref[...].astype(F32), o_ref[...])
    key = jnp.concatenate([ref[0] for ref in ext], axis=0)
    key_t = key.T
    value = jnp.concatenate([ref[1] for ref in ext], axis=0)
    parts = []
    key_sum = jnp.zeros(key.shape, F32)
    value_sum = jnp.zeros(key.shape, F32)
    for side in range(2):
        query = half(q_ref[0], side) * BF16(SCALE)
        up = half(up_ref[...], side)
        rounded = share_ref[side]
        product = nt(value, up) - delta[side : side + 1]
        grads = (rounded.astype(F32) * product).astype(BF16)
        key_sum += nn(grads, query)
        value_sum += nn(rounded, up)
        parts.append(nn(key_t[side * HD : side * HD + HD], grads))
    return jnp.concatenate(parts, axis=0).T, key_sum, value_sum


def fine_sides(own_qkv, sides, own_up, out, shares):
    _, own, width = own_qkv.shape
    size = sides[0].shape[1]

    def body(q_ref, low_ref, high_ref, up_ref, o_ref, share_ref, q_out, inner_out, outer_out):
        first = lax.axis_index("c") == 0
        q_out[...], *sums = pair_grads(q_ref, (low_ref, high_ref), up_ref, o_ref, share_ref)
        for at, total in zip((slice(0, 128), slice(128, 256)), sums):
            low, high = total[:size].astype(BF16), total[size:].astype(BF16)
            inner_out[:, at] = jnp.where(first, high, low)
            outer_out[:, at] = jnp.where(first, low, high)

    return pair_call(
        body,
        [jax.ShapeDtypeStruct((own, width), F32)]
        + [jax.ShapeDtypeStruct((size, 2 * width), BF16)] * 2,
        "fine_sides",
        1 << 30,
        own_qkv,
        *sides,
        own_up,
        out,
        shares,
    )


def fine_middle(own_qkv, middle, own_up, out, shares, query_part):
    _, own, width = own_qkv.shape
    size = middle.shape[1]
    edge = (size - own) // 2

    def body(q_ref, mid_ref, up_ref, o_ref, share_ref, part_ref, q_out, top, inside, bottom):
        found, *sums = pair_grads(q_ref, (mid_ref,), up_ref, o_ref, share_ref)
        q_out[...] = ((found + part_ref[...]) * SCALE).astype(BF16)
        for at, total in zip((slice(0, 128), slice(128, 256)), sums):
            top[:, at] = total[:edge]
            inside[:, at] = total[edge : edge + own]
            bottom[:, at] = total[edge + own :]

    return pair_call(
        body,
        [jax.ShapeDtypeStruct((own, width), BF16)]
        + [jax.ShapeDtypeStruct((count, 2 * width), F32) for count in (edge, own, edge)],
        "fine_middle",
        1 << 30,
        own_qkv,
        middle,
        own_up,
        out,
        shares,
        query_part,
    )


def beside_each_other(inner, outer):
    first = lax.axis_index("c") == 0
    cells, wide = inner.shape
    inner = inner.astype(F32).reshape(cells // RIM, RIM, wide)
    outer = outer.astype(F32).reshape(cells // RIM, RIM, wide)
    left, right = jnp.where(first, outer, inner), jnp.where(first, inner, outer)
    return jnp.concatenate([left, right], axis=1).reshape(2 * cells, wide)


def add_strips(top, bottom, inner, outer):
    edge, wide = top.shape
    corner = edge // 2
    sent = edge // RIM * RADIUS

    def body(top_ref, bottom_ref, inner_ref, outer_ref, inner_out, outer_out):
        upper = lax.axis_index("zh") == 0
        cells = inner_ref.shape[0]
        above = top_ref[...] + beside_each_other(inner_ref[:corner], outer_ref[:corner])
        below = bottom_ref[...] + beside_each_other(
            inner_ref[cells - corner :], outer_ref[cells - corner :]
        )
        above, below = above[edge - sent :], below[:sent]
        inner_out[...] = jnp.where(upper, below, above).astype(BF16)
        outer_out[...] = jnp.where(upper, above, below).astype(BF16)

    return whole_call(
        body,
        [jax.ShapeDtypeStruct((sent, wide), BF16)] * 2,
        "add_strips",
        1 << 20,
        [],
        top,
        bottom,
        inner,
        outer,
    )


def add_all(own, side_inner, side_outer, row_inner, row_outer):
    cells, wide = own.shape
    width = wide // 2
    half_cells = cells // 2

    def body(own_ref, side_in, side_out, row_in, row_out, k_out, v_out):
        upper = lax.axis_index("zh") == 0
        corner = (side_in.shape[0] - half_cells) // 2
        middle = slice(corner, corner + half_cells)
        inner, outer = row_in[...].astype(F32), row_out[...].astype(F32)
        above, below = jnp.where(upper, outer, inner), jnp.where(upper, inner, outer)
        skipped = jnp.zeros((cells - 2 * above.shape[0], wide), F32)
        total = own_ref[...] + jnp.concatenate([above, skipped, below], axis=0)
        total += beside_each_other(side_in[middle], side_out[middle])
        for pair, lanes in pairs_of(width):
            k_out[:, lanes] = total[:, pair * 256 : pair * 256 + 128].astype(BF16)
            v_out[:, lanes] = total[:, pair * 256 + 128 : pair * 256 + 256].astype(BF16)

    return whole_call(
        body,
        [jax.ShapeDtypeStruct((cells, width), BF16)] * 2,
        "add_all",
        1 << 20,
        [],
        own,
        side_inner,
        side_outer,
        row_inner,
        row_outer,
    )


def project(query_pieces, kept, from_core, arrived, joint, columns, count):
    group, tokens = query_pieces[0].shape
    heads = arrived.shape[0]
    rows = tokens // columns
    each = rows // count
    size = each * columns
    wide = joint.shape[1]
    chunk = 512
    blocks = len(query_pieces)

    def body(*refs):
        pieces = refs[:blocks]
        kept_ref, core_ref, arrived_ref, joint_ref, out, held, packed = refs[blocks:]

        @pl.when(pl.program_id(0) == 0)
        def _():
            for head in range(heads):
                total = kept_ref[0, head].astype(F32) + core_ref[0, head].astype(F32)
                total += arrived_ref[head].astype(F32)
                for part in range(2):
                    at = (1 + part) * group + head * HD
                    held[:, at : at + HD] = total[:, part * HD : (part + 1) * HD]
            total = pieces[0][...].astype(F32)
            for piece in pieces[1:]:
                total += piece[...].astype(F32)
            held[:, :group] = total.T
            for target in range(count):
                taken = []
                for c in range(columns):
                    start = c * rows + target * each
                    taken.append(held[start : start + each, :])
                chosen = jnp.concatenate(taken, axis=0).astype(BF16)
                packed[target * size : (target + 1) * size, :] = chosen

        out[...] = nn(packed[...], joint_ref[...]).astype(BF16)

    half_spec = pl.BlockSpec((1, heads, tokens, 128), lambda n: (0, 0, 0, 0))
    return pl.pallas_call(
        body,
        grid=(wide // chunk,),
        in_specs=[pl.BlockSpec((group, tokens), lambda n: (0, 0))] * blocks
        + [half_spec] * 2
        + [
            pl.BlockSpec(arrived.shape, lambda n: (0, 0, 0)),
            pl.BlockSpec((3 * group, chunk), lambda n: (0, n)),
        ],
        out_specs=pl.BlockSpec((tokens, chunk), lambda n: (0, n)),
        out_shape=jax.ShapeDtypeStruct((tokens, wide), BF16),
        scratch_shapes=[
            pltpu.VMEM((tokens, 3 * group), F32),
            pltpu.VMEM((tokens, 3 * group), BF16),
        ],
        name="project",
        cost_estimate=cost(2 << 30, 6 << 20, 0),
        compiler_params=pltpu.CompilerParams(vmem_limit_bytes=VMEM),
    )(*query_pieces, kept, from_core, arrived, joint)


def spread(pieces, columns):
    count, tokens, wide = pieces.shape
    width = wide // 4

    def body(in_ref, out):
        total = in_ref[0].astype(F32)
        for at in range(1, count):
            total += in_ref[at].astype(F32)
        total = total.astype(BF16)
        cells = 2 * tokens
        fine = lax.broadcasted_iota(jnp.int32, (cells, tokens), 0)
        token = lax.broadcasted_iota(jnp.int32, (cells, tokens), 1)
        cell = (token & 7) * 2 * columns + (token >> 3) * 2
        for a in range(2):
            grid = jnp.zeros((cells, width), F32)
            for b in range(2):
                place = jnp.where(fine == cell + b, 1.0, 0.0).astype(BF16)
                lanes = slice((2 * a + b) * width, (2 * a + b + 1) * width)
                grid += nn(place, total[:, lanes])
            grid = grid.astype(BF16)
            for row in range(tokens // columns):
                at = (2 * row + a) * 2 * columns
                out[at : at + 2 * columns, :] = grid[row * 2 * columns : (row + 1) * 2 * columns]

    return whole_call(
        body,
        jax.ShapeDtypeStruct((4 * tokens, width), BF16),
        "spread",
        1 << 28,
        [],
        pieces,
    )


def swapped(array, axis, flip=1):
    return lax.ppermute(array, axis, [(i, i ^ flip) for i in range(lax.axis_size(axis))])


def exchanged(inner, outer, axis):
    count = lax.axis_size(axis)
    beyond = [(i, ((i + 1) ^ 1) - 1) for i in range(1, count - 1)]
    return swapped(inner, axis), lax.ppermute(outer, axis, beyond)


def sent_rims(block, axis, parity, at):
    size = block.shape[at]
    low = lax.slice_in_dim(block, 0, RIM, axis=at)
    high = lax.slice_in_dim(block, size - RIM, None, axis=at)
    first = lax.axis_index(parity) == 0
    return exchanged(jnp.where(first, high, low), jnp.where(first, low, high), axis)


def placed_rims(inner, outer, parity):
    first = lax.axis_index(parity) == 0
    return jnp.where(first, outer, inner), jnp.where(first, inner, outer)


def shards(fine_qkv, coarse_qkv, grad_coarse, merge_weight, qkv_weight):
    rows, columns, width = fine_qkv.shape[1:]
    own = rows * columns
    coarse_columns, coarse_rows, group = grad_coarse.shape
    tokens = coarse_columns * coarse_rows
    wide = merge_weight.shape[0]

    key_value, query_up = prepare(
        coarse_qkv.reshape(3, tokens, group), grad_coarse.reshape(tokens, group)
    )
    across = swapped(key_value, "zl")
    beside = swapped(key_value, "c")
    beside, query_up, merge_weight, fine_qkv = lax.optimization_barrier(
        (beside, query_up, merge_weight, fine_qkv)
    )
    near = [query_up, swapped(query_up, "y", 1), swapped(query_up, "y", 3)]
    own_qkv = fine_qkv.reshape(3, own, width)
    edges = sent_rims(fine_qkv[1:], ROW, "zh", 1)
    joint = lax.dot_general(
        qkv_weight, merge_weight, (((1,), (1,)), ((), ())), preferred_element_type=F32
    ).astype(BF16).reshape(3 * group, wide)
    across, joint, *edges = lax.optimization_barrier((across, joint, *edges))
    corner = swapped(across, "c")
    *near, joint = lax.optimization_barrier((*near, joint))
    far = swapped(near[0], "y", 2)
    keys = [key_value, beside, across, corner]
    queries = [near[0], near[1], far, near[2]]

    part = coarse_stats(keys, near, [0, 1, 3], (), 256)
    part, *edges = lax.optimization_barrier((part, *edges))
    low, high = placed_rims(*edges, "zh")
    tall = jnp.concatenate([low, fine_qkv[1:], high], axis=1)
    edges = sent_rims(tall, COL, "c", 2)
    part = coarse_stats(keys, [far], [2], (part,), 256)
    part, *edges = lax.optimization_barrier((part, *edges))
    stats = [part] + [swapped(part, "y", step) for step in (1, 3, 2)]
    kept, sent, *query_grads = coarse_grads(keys, queries, stats)

    from_core = swapped(sent, "c")
    passed = (kept[1].astype(F32) + from_core[1].astype(F32)).astype(BF16)
    arrived = swapped(passed, "zl")
    query_pieces = [query_grads[0]]
    for step in (1, 2, 3):
        query_pieces.append(swapped(query_grads[step], "y", step))
    count = lax.axis_size(ROW)
    low, high = placed_rims(*edges, "c")
    ext_kv = [array.reshape(2, -1, width) for array in (tall, low, high)]
    mid_shares, side_shares, out = fine_shares(own_qkv, ext_kv, rows, columns)
    arrived, out = lax.optimization_barrier((arrived, out))
    projected = project(
        query_pieces, kept, from_core, arrived, joint, coarse_columns, count
    )
    pieces = lax.all_to_all(projected.reshape(count, -1, wide), ROW, 0, 0)
    own_up = spread(pieces, coarse_columns)

    query_part, inner, outer = fine_sides(own_qkv, ext_kv[1:], own_up, out, side_shares)
    side_inner, side_outer = exchanged(inner, outer, COL)
    grad_query, top, middle, bottom = fine_middle(
        own_qkv, ext_kv[0], own_up, out, mid_shares, query_part
    )
    strips = add_strips(top, bottom, side_inner, side_outer)
    row_inner, row_outer = exchanged(*strips, ROW)
    grad_key, grad_value = add_all(middle, side_inner, side_outer, row_inner, row_outer)
    shape = (rows, columns, width)
    return grad_query.reshape(shape), grad_key.reshape(shape), grad_value.reshape(shape)


def solution(mesh):
    split = Mesh(mesh.devices.reshape(4, 2, 2, 4, 2), ROW + COL)
    return jax.shard_map(
        shards,
        mesh=split,
        in_specs=(
            P(None, ROW, COL, None),
            P(None, COL, None, ROW),
            P(COL, None, ROW),
            P(),
            P(None, None, ROW),
        ),
        out_specs=(P(ROW, COL, None), P(ROW, COL, None), P(ROW, COL, None)),
        check_vma=False,
    )
```

```python
import jax
import jax.numpy as jnp
from jax import lax
from jax.experimental import pallas as pl
from jax.experimental.pallas import tpu as pltpu
from jax.sharding import Mesh
from jax.sharding import PartitionSpec as P

HD = 64
RADIUS = 7
SCALE = 0.125
SIDE = 32
RIM = 8
HIDDEN = -1e30
ROW = ("x", "zh")
COL = ("zl", "y", "c")
F32 = jnp.float32
BF16 = jnp.bfloat16
VMEM = 24 << 20


def nt(left, right):
    return lax.dot_general(left, right, (((1,), (1,)), ((), ())), preferred_element_type=F32)


def nn(left, right):
    return lax.dot_general(left, right, (((1,), (0,)), ((), ())), preferred_element_type=F32)


def half(pair, which):
    lane = lax.broadcasted_iota(jnp.int32, pair.shape, 1)
    return jnp.where((lane < HD) == (which == 0), pair, jnp.zeros_like(pair))


def cost(flops, bytes_accessed, exps):
    return pl.CostEstimate(flops=flops, bytes_accessed=bytes_accessed, transcendentals=exps)


def prepare(coarse_qkv, grad_coarse):
    _, tokens, group = coarse_qkv.shape
    heads = group // HD

    def body(qkv_ref, up_ref, kv_out, qu_out):
        for head in range(heads):
            lanes = slice(head * HD, head * HD + HD)
            kv_out[head] = jnp.concatenate([qkv_ref[1, :, lanes], qkv_ref[2, :, lanes]], axis=1)
            qu_out[head] = jnp.concatenate([qkv_ref[0, :, lanes], up_ref[:, lanes]], axis=1)

    return whole_call(
        body,
        [jax.ShapeDtypeStruct((heads, tokens, 2 * HD), BF16)] * 2,
        "prepare",
        1 << 20,
        [],
        coarse_qkv,
        grad_coarse,
    )


def own_block(step, tokens):
    owner = lax.axis_index("y") ^ step
    return pl.ds(pl.multiple_of(owner * tokens, tokens), tokens)


def coarse_stats(key_values, query_ups, steps, before, key_tile):
    heads, tokens, _ = key_values[0].shape
    blocks, number = len(key_values), len(query_ups)
    per_block = tokens // key_tile

    def body(*refs):
        kv_refs, qu_refs = refs[:blocks], refs[blocks : blocks + number]
        out_ref, held = refs[-2:]
        if before:

            @pl.when(pl.program_id(1) == 0)
            def _():
                out_ref[...] = refs[blocks + number][...]

        for at in range(number):

            @pl.when(pl.program_id(1) == at)
            def _():
                held[...] = qu_refs[at][0]

        query = half(held[...], 0) * BF16(SCALE)
        upstream = half(held[...], 1)
        peak = jnp.full((1, tokens), -jnp.inf, F32)
        total = jnp.zeros((1, tokens), F32)
        weighted = jnp.zeros((1, tokens), F32)
        for i in range(blocks * per_block):
            start = (i % per_block) * key_tile
            tile = kv_refs[i // per_block][0, start : start + key_tile, :]
            score = nt(tile, query)
            product = nt(tile, upstream)
            new_peak = jnp.maximum(peak, jnp.max(score, axis=0, keepdims=True))
            decay = jnp.exp(peak - new_peak)
            share = jnp.exp(score - new_peak)
            total = total * decay + jnp.sum(share, axis=0, keepdims=True)
            weighted = weighted * decay + jnp.sum(share * product, axis=0, keepdims=True)
            peak = new_peak
        found = jnp.concatenate([peak + jnp.log(total), weighted / total], axis=0)
        for at, step in enumerate(steps):

            @pl.when(pl.program_id(1) == at)
            def _():
                out_ref[0, :, own_block(step, tokens)] = found

    pairs = heads * number * blocks * tokens**2
    return pl.pallas_call(
        body,
        grid=(heads, number),
        in_specs=[pl.BlockSpec((1, tokens, 128), lambda h, q: (h, 0, 0))] * (blocks + number)
        + [pl.BlockSpec((1, 2, blocks * tokens), lambda h, q: (h, 0, 0))] * len(before),
        out_specs=pl.BlockSpec((1, 2, blocks * tokens), lambda h, q: (h, 0, 0)),
        out_shape=jax.ShapeDtypeStruct((heads, 2, blocks * tokens), F32),
        scratch_shapes=[pltpu.VMEM((tokens, 128), BF16)],
        name="coarse_stats",
        cost_estimate=cost(4 * pairs * 256, 2 << 20, pairs),
        compiler_params=pltpu.CompilerParams(vmem_limit_bytes=VMEM),
    )(*key_values, *query_ups, *before)


def coarse_grads(key_values, query_ups, stats):
    heads, tokens, _ = key_values[0].shape
    blocks = len(query_ups)
    parts = len(stats)

    def body(*refs):
        kv_refs, qu_refs = refs[:blocks], refs[blocks : 2 * blocks]
        stats_refs = refs[2 * blocks : 2 * blocks + parts]
        kept_ref, sent_ref = refs[2 * blocks + parts : 2 * blocks + parts + 2]
        q_outs = refs[-blocks - 2 : -2]
        acc, held = refs[-2:]
        step = pl.program_id(1)
        for at in range(blocks):

            @pl.when(step == at // 2)
            def _():
                held[at % 2 * tokens : (at % 2 + 1) * tokens] = qu_refs[at][0]

        @pl.when(pl.program_id(1) == 0)
        def _():
            acc[...] = jnp.zeros_like(acc)

        query = half(held[...], 0) * BF16(SCALE)
        upstream = half(held[...], 1)
        found = [
            jnp.concatenate(
                [ref[0, :, own_block(2 * step + i, tokens)] for i in range(2)], axis=1
            )
            for ref in stats_refs
        ]
        peak = found[0][:1]
        for part in found[1:]:
            peak = jnp.maximum(peak, part[:1])
        shares = [jnp.exp(part[:1] - peak) for part in found]
        total = sum(shares)
        log_total = peak + jnp.log(total)
        delta = sum(share * part[1:] for share, part in zip(shares, found)) / total
        found = jnp.zeros((HD, 2 * tokens), F32)
        both = jnp.concatenate([query, upstream], axis=0)
        for i in range(blocks):
            tile = kv_refs[i][0]
            share = jnp.exp(nt(tile, query) - log_total)
            grads = (share * (nt(tile, upstream) - delta)).astype(BF16)
            acc[i] += nn(jnp.concatenate([grads, share.astype(BF16)], axis=1), both)
            found += nn(tile[:, :HD].T, grads)
        found = (found * SCALE).astype(BF16)
        for at in range(blocks):

            @pl.when(step == at // 2)
            def _():
                q_outs[at][...] = found[:, at % 2 * tokens : (at % 2 + 1) * tokens]

        @pl.when(step == blocks // 2 - 1)
        def _():
            for i in range(blocks // 2):
                kept_ref[i, 0] = acc[2 * i].astype(BF16)
                sent_ref[i, 0] = acc[2 * i + 1].astype(BF16)

    pairs = heads * (blocks * tokens) ** 2
    out_shape = [jax.ShapeDtypeStruct((blocks // 2, heads, tokens, 128), BF16)] * 2
    out_shape += [jax.ShapeDtypeStruct((heads * HD, tokens), BF16)] * blocks
    return pl.pallas_call(
        body,
        grid=(heads, blocks // 2),
        in_specs=[pl.BlockSpec((1, tokens, 128), lambda h, q: (h, 0, 0))] * (2 * blocks)
        + [pl.BlockSpec((1, 2, blocks * tokens), lambda h, q: (h, 0, 0))] * parts,
        out_specs=[pl.BlockSpec((blocks // 2, 1, tokens, 128), lambda h, q: (0, h, 0, 0))] * 2
        + [pl.BlockSpec((HD, tokens), lambda h, q: (h, 0))] * blocks,
        out_shape=out_shape,
        scratch_shapes=[
            pltpu.VMEM((blocks, tokens, 128), F32),
            pltpu.VMEM((2 * tokens, 128), BF16),
        ],
        name="coarse_grads",
        cost_estimate=cost(10 * pairs * 256, 4 << 20, pairs),
        compiler_params=pltpu.CompilerParams(vmem_limit_bytes=VMEM),
    )(*key_values, *query_ups, *stats)


def whole_call(body, out_shape, name, flops, scratch, *operands):
    return pl.pallas_call(
        body,
        out_shape=out_shape,
        scratch_shapes=scratch,
        name=name,
        cost_estimate=cost(flops, 6 << 20, 1 << 20),
        compiler_params=pltpu.CompilerParams(vmem_limit_bytes=VMEM),
    )(*operands)


def pairs_of(width):
    return [(pair, slice(pair * 128, pair * 128 + 128)) for pair in range(width // 128)]


def window_bias(own, rows, columns, part, transposed):
    count = SIDE * SIDE // 2
    shape = (own, count) if transposed else (count, own)
    ext = lax.broadcasted_iota(jnp.int32, shape, 1 if transposed else 0)
    inner = lax.broadcasted_iota(jnp.int32, shape, 0 if transposed else 1)
    if part == 0:
        ext_row, ext_column = ext >> 4, (ext & 15) + RIM
    else:
        ext_row = (ext & 255) >> 3
        ext_column = (ext & 7) + jnp.where(ext >= 256, SIDE - RIM, 0)
    row_gap = ext_row - (inner >> 4) - RIM
    column_gap = ext_column - (inner & 15) - RIM
    row = ext_row + (lax.axis_index(ROW) * rows - RIM)
    column = ext_column + (lax.axis_index(COL) * columns - RIM)
    seen = (jnp.abs(row_gap) <= RADIUS) & (jnp.abs(column_gap) <= RADIUS)
    seen &= (row >= 0) & (row < lax.axis_size(ROW) * rows)
    seen &= (column >= 0) & (column < lax.axis_size(COL) * columns)
    return jnp.where(seen, 0.0, HIDDEN).astype(F32)


def fill_bias(bias_ref, own, rows, columns):
    count = SIDE * SIDE // 2
    for part in range(2):
        bias_ref[part * count : (part + 1) * count, :] = window_bias(
            own, rows, columns, part, False
        )


def stacked(refs, which, lanes):
    return jnp.concatenate([ref[which, :, lanes] for ref in refs], axis=0)


def fine_shares(own_qkv, ext_kv, rows, columns):
    _, own, width = own_qkv.shape
    heads = width // HD
    count = SIDE * SIDE // 2

    def body(q_ref, mid_ref, low_ref, high_ref, mid_out, side_out, o_ref, bias_ref):
        fill_bias(bias_ref, own, rows, columns)
        ext = (mid_ref, low_ref, high_ref)
        for pair, lanes in pairs_of(width):
            key = stacked(ext, 0, lanes)
            value_t = stacked(ext, 1, lanes).T
            parts = []
            for side in range(2):
                query = half(q_ref[0, :, lanes], side) * BF16(SCALE)
                score = nt(key, query) + bias_ref[...]
                share = jnp.exp(score - jnp.max(score, axis=0, keepdims=True))
                total = jnp.sum(share, axis=0, keepdims=True)
                rounded = (share * (1.0 / total)).astype(BF16)
                mid_out[2 * pair + side] = rounded[:count]
                side_out[2 * pair + side] = rounded[count:]
                total = jnp.sum(rounded.astype(F32), axis=0, keepdims=True)
                parts.append(nn(value_t[side * HD : side * HD + HD], rounded) / total)
            o_ref[:, lanes] = jnp.concatenate(parts, axis=0).T

    return whole_call(
        body,
        [jax.ShapeDtypeStruct((heads, count, own), BF16)] * 2
        + [jax.ShapeDtypeStruct((own, width), F32)],
        "fine_shares",
        1 << 30,
        [pltpu.VMEM((SIDE * SIDE, own), F32)],
        own_qkv,
        *ext_kv,
    )


def pair_call(body, out_shape, name, flops, *operands):
    width = 384
    pairs = width // 128

    def spec(array):
        shape = tuple(array.shape)
        rank = len(shape)
        if shape[0] == 2 * pairs:
            return pl.BlockSpec((2,) + shape[1:], lambda p: (p,) + (0,) * (rank - 1))
        return pl.BlockSpec(
            shape[:-1] + (shape[-1] // pairs,), lambda p: (0,) * (rank - 1) + (p,)
        )

    return pl.pallas_call(
        body,
        grid=(pairs,),
        in_specs=[spec(array) for array in operands],
        out_specs=[spec(shape) for shape in out_shape],
        out_shape=out_shape,
        name=name,
        cost_estimate=cost(flops, 6 << 20, 0),
        compiler_params=pltpu.CompilerParams(vmem_limit_bytes=VMEM),
    )(*operands)


def head_sums(up, out):
    head = lax.broadcasted_iota(jnp.int32, (8, up.shape[1]), 0)
    lane = lax.broadcasted_iota(jnp.int32, (8, up.shape[1]), 1)
    pick = jnp.where((lane >> 6) == head, 1.0, 0.0).astype(F32)
    return lax.dot_general(
        pick,
        up * out,
        (((1,), (1,)), ((), ())),
        preferred_element_type=F32,
        precision=lax.Precision.HIGHEST,
    )


def pair_grads(q_ref, ext, up_ref, o_ref, share_ref):
    delta = head_sums(up_ref[...].astype(F32), o_ref[...])
    key = jnp.concatenate([ref[0] for ref in ext], axis=0)
    key_t = key.T
    value = jnp.concatenate([ref[1] for ref in ext], axis=0)
    parts = []
    key_sum = jnp.zeros(key.shape, F32)
    value_sum = jnp.zeros(key.shape, F32)
    for side in range(2):
        query = half(q_ref[0], side) * BF16(SCALE)
        up = half(up_ref[...], side)
        rounded = share_ref[side]
        product = nt(value, up) - delta[side : side + 1]
        grads = (rounded.astype(F32) * product).astype(BF16)
        key_sum += nn(grads, query)
        value_sum += nn(rounded, up)
        parts.append(nn(key_t[side * HD : side * HD + HD], grads))
    return jnp.concatenate(parts, axis=0).T, key_sum, value_sum


def fine_sides(own_qkv, sides, own_up, out, shares):
    _, own, width = own_qkv.shape
    size = sides[0].shape[1]

    def body(q_ref, low_ref, high_ref, up_ref, o_ref, share_ref, q_out, inner_out, outer_out):
        first = lax.axis_index("c") == 0
        q_out[...], *sums = pair_grads(q_ref, (low_ref, high_ref), up_ref, o_ref, share_ref)
        for at, total in zip((slice(0, 128), slice(128, 256)), sums):
            low, high = total[:size].astype(BF16), total[size:].astype(BF16)
            inner_out[:, at] = jnp.where(first, high, low)
            outer_out[:, at] = jnp.where(first, low, high)

    return pair_call(
        body,
        [jax.ShapeDtypeStruct((own, width), F32)]
        + [jax.ShapeDtypeStruct((size, 2 * width), BF16)] * 2,
        "fine_sides",
        1 << 30,
        own_qkv,
        *sides,
        own_up,
        out,
        shares,
    )


def fine_middle(own_qkv, middle, own_up, out, shares, query_part):
    _, own, width = own_qkv.shape
    size = middle.shape[1]
    edge = (size - own) // 2

    def body(q_ref, mid_ref, up_ref, o_ref, share_ref, part_ref, q_out, top, inside, bottom):
        found, *sums = pair_grads(q_ref, (mid_ref,), up_ref, o_ref, share_ref)
        q_out[...] = ((found + part_ref[...]) * SCALE).astype(BF16)
        for at, total in zip((slice(0, 128), slice(128, 256)), sums):
            top[:, at] = total[:edge]
            inside[:, at] = total[edge : edge + own]
            bottom[:, at] = total[edge + own :]

    return pair_call(
        body,
        [jax.ShapeDtypeStruct((own, width), BF16)]
        + [jax.ShapeDtypeStruct((count, 2 * width), F32) for count in (edge, own, edge)],
        "fine_middle",
        1 << 30,
        own_qkv,
        middle,
        own_up,
        out,
        shares,
        query_part,
    )


def beside_each_other(inner, outer):
    first = lax.axis_index("c") == 0
    cells, wide = inner.shape
    inner = inner.astype(F32).reshape(cells // RIM, RIM, wide)
    outer = outer.astype(F32).reshape(cells // RIM, RIM, wide)
    left, right = jnp.where(first, outer, inner), jnp.where(first, inner, outer)
    return jnp.concatenate([left, right], axis=1).reshape(2 * cells, wide)


def add_strips(top, bottom, inner, outer):
    edge, wide = top.shape
    corner = edge // 2
    sent = edge // RIM * RADIUS

    def body(top_ref, bottom_ref, inner_ref, outer_ref, inner_out, outer_out):
        upper = lax.axis_index("zh") == 0
        cells = inner_ref.shape[0]
        above = top_ref[...] + beside_each_other(inner_ref[:corner], outer_ref[:corner])
        below = bottom_ref[...] + beside_each_other(
            inner_ref[cells - corner :], outer_ref[cells - corner :]
        )
        above, below = above[edge - sent :], below[:sent]
        inner_out[...] = jnp.where(upper, below, above).astype(BF16)
        outer_out[...] = jnp.where(upper, above, below).astype(BF16)

    return whole_call(
        body,
        [jax.ShapeDtypeStruct((sent, wide), BF16)] * 2,
        "add_strips",
        1 << 20,
        [],
        top,
        bottom,
        inner,
        outer,
    )


def add_all(own, side_inner, side_outer, row_inner, row_outer):
    cells, wide = own.shape
    width = wide // 2
    half_cells = cells // 2

    def body(own_ref, side_in, side_out, row_in, row_out, k_out, v_out):
        upper = lax.axis_index("zh") == 0
        corner = (side_in.shape[0] - half_cells) // 2
        middle = slice(corner, corner + half_cells)
        inner, outer = row_in[...].astype(F32), row_out[...].astype(F32)
        above, below = jnp.where(upper, outer, inner), jnp.where(upper, inner, outer)
        skipped = jnp.zeros((cells - 2 * above.shape[0], wide), F32)
        total = own_ref[...] + jnp.concatenate([above, skipped, below], axis=0)
        total += beside_each_other(side_in[middle], side_out[middle])
        for pair, lanes in pairs_of(width):
            k_out[:, lanes] = total[:, pair * 256 : pair * 256 + 128].astype(BF16)
            v_out[:, lanes] = total[:, pair * 256 + 128 : pair * 256 + 256].astype(BF16)

    return whole_call(
        body,
        [jax.ShapeDtypeStruct((cells, width), BF16)] * 2,
        "add_all",
        1 << 20,
        [],
        own,
        side_inner,
        side_outer,
        row_inner,
        row_outer,
    )


def project(query_pieces, kept, from_core, arrived, joint, columns, count):
    group, tokens = query_pieces[0].shape
    heads = arrived.shape[0]
    rows = tokens // columns
    each = rows // count
    size = each * columns
    wide = joint.shape[1]
    chunk = 512
    blocks = len(query_pieces)

    def body(*refs):
        pieces = refs[:blocks]
        kept_ref, core_ref, arrived_ref, joint_ref, out, held, packed = refs[blocks:]

        @pl.when(pl.program_id(0) == 0)
        def _():
            for head in range(heads):
                total = kept_ref[0, head].astype(F32) + core_ref[0, head].astype(F32)
                total += arrived_ref[head].astype(F32)
                for part in range(2):
                    at = (1 + part) * group + head * HD
                    held[:, at : at + HD] = total[:, part * HD : (part + 1) * HD]
            total = pieces[0][...].astype(F32)
            for piece in pieces[1:]:
                total += piece[...].astype(F32)
            held[:, :group] = total.T
            for target in range(count):
                taken = []
                for c in range(columns):
                    start = c * rows + target * each
                    taken.append(held[start : start + each, :])
                chosen = jnp.concatenate(taken, axis=0).astype(BF16)
                packed[target * size : (target + 1) * size, :] = chosen

        out[...] = nn(packed[...], joint_ref[...]).astype(BF16)

    half_spec = pl.BlockSpec((1, heads, tokens, 128), lambda n: (0, 0, 0, 0))
    return pl.pallas_call(
        body,
        grid=(wide // chunk,),
        in_specs=[pl.BlockSpec((group, tokens), lambda n: (0, 0))] * blocks
        + [half_spec] * 2
        + [
            pl.BlockSpec(arrived.shape, lambda n: (0, 0, 0)),
            pl.BlockSpec((3 * group, chunk), lambda n: (0, n)),
        ],
        out_specs=pl.BlockSpec((tokens, chunk), lambda n: (0, n)),
        out_shape=jax.ShapeDtypeStruct((tokens, wide), BF16),
        scratch_shapes=[
            pltpu.VMEM((tokens, 3 * group), F32),
            pltpu.VMEM((tokens, 3 * group), BF16),
        ],
        name="project",
        cost_estimate=cost(2 << 30, 6 << 20, 0),
        compiler_params=pltpu.CompilerParams(vmem_limit_bytes=VMEM),
    )(*query_pieces, kept, from_core, arrived, joint)


def spread(pieces, columns):
    count, tokens, wide = pieces.shape
    width = wide // 4

    def body(in_ref, out):
        total = in_ref[0].astype(F32)
        for at in range(1, count):
            total += in_ref[at].astype(F32)
        total = total.astype(BF16)
        cells = 2 * tokens
        fine = lax.broadcasted_iota(jnp.int32, (cells, tokens), 0)
        token = lax.broadcasted_iota(jnp.int32, (cells, tokens), 1)
        cell = (token & 7) * 2 * columns + (token >> 3) * 2
        for a in range(2):
            grid = jnp.zeros((cells, width), F32)
            for b in range(2):
                place = jnp.where(fine == cell + b, 1.0, 0.0).astype(BF16)
                lanes = slice((2 * a + b) * width, (2 * a + b + 1) * width)
                grid += nn(place, total[:, lanes])
            grid = grid.astype(BF16)
            for row in range(tokens // columns):
                at = (2 * row + a) * 2 * columns
                out[at : at + 2 * columns, :] = grid[row * 2 * columns : (row + 1) * 2 * columns]

    return whole_call(
        body,
        jax.ShapeDtypeStruct((4 * tokens, width), BF16),
        "spread",
        1 << 28,
        [],
        pieces,
    )


def swapped(array, axis, flip=1):
    return lax.ppermute(array, axis, [(i, i ^ flip) for i in range(lax.axis_size(axis))])


def exchanged(inner, outer, axis):
    count = lax.axis_size(axis)
    beyond = [(i, ((i + 1) ^ 1) - 1) for i in range(1, count - 1)]
    return swapped(inner, axis), lax.ppermute(outer, axis, beyond)


def sent_rims(block, axis, parity, at):
    size = block.shape[at]
    low = lax.slice_in_dim(block, 0, RIM, axis=at)
    high = lax.slice_in_dim(block, size - RIM, None, axis=at)
    first = lax.axis_index(parity) == 0
    return exchanged(jnp.where(first, high, low), jnp.where(first, low, high), axis)


def placed_rims(inner, outer, parity):
    first = lax.axis_index(parity) == 0
    return jnp.where(first, outer, inner), jnp.where(first, inner, outer)


def shards(fine_qkv, coarse_qkv, grad_coarse, merge_weight, qkv_weight):
    rows, columns, width = fine_qkv.shape[1:]
    own = rows * columns
    coarse_columns, coarse_rows, group = grad_coarse.shape
    tokens = coarse_columns * coarse_rows
    wide = merge_weight.shape[0]

    key_value, query_up = prepare(
        coarse_qkv.reshape(3, tokens, group), grad_coarse.reshape(tokens, group)
    )
    across = swapped(key_value, "zl")
    beside = swapped(key_value, "c")
    beside, query_up, fine_qkv = lax.optimization_barrier((beside, query_up, fine_qkv))
    near = [query_up, swapped(query_up, "y", 1), swapped(query_up, "y", 3)]
    own_qkv = fine_qkv.reshape(3, own, width)
    edges = sent_rims(fine_qkv[1:], ROW, "zh", 1)
    corner = swapped(across, "c")
    near = lax.optimization_barrier(near)
    far = swapped(near[0], "y", 2)
    keys = [key_value, beside, across, corner]
    queries = [near[0], near[1], far, near[2]]

    part = coarse_stats(keys, near, [0, 1, 3], (), 256)
    part, *edges = lax.optimization_barrier((part, *edges))
    low, high = placed_rims(*edges, "zh")
    tall = jnp.concatenate([low, fine_qkv[1:], high], axis=1)
    edges = sent_rims(tall, COL, "c", 2)
    part = coarse_stats(keys, [far], [2], (part,), 256)
    part, merge_weight, *edges = lax.optimization_barrier((part, merge_weight, *edges))
    joint = lax.dot_general(
        qkv_weight, merge_weight, (((1,), (1,)), ((), ())), preferred_element_type=F32
    ).astype(BF16).reshape(3 * group, wide)
    stats = [part] + [swapped(part, "y", step) for step in (1, 3, 2)]
    stats, joint = lax.optimization_barrier((stats, joint))
    kept, sent, *query_grads = coarse_grads(keys, queries, stats)

    query_pieces = [query_grads[0], swapped(query_grads[2], "y", 2)]
    from_core = swapped(sent, "c")
    passed = (kept[1].astype(F32) + from_core[1].astype(F32)).astype(BF16)
    arrived = swapped(passed, "zl")
    for step in (1, 3):
        query_pieces.append(swapped(query_grads[step], "y", step))
    count = lax.axis_size(ROW)
    low, high = placed_rims(*edges, "c")
    ext_kv = [array.reshape(2, -1, width) for array in (tall, low, high)]
    mid_shares, side_shares, out = fine_shares(own_qkv, ext_kv, rows, columns)
    arrived, out = lax.optimization_barrier((arrived, out))
    projected = project(
        query_pieces, kept, from_core, arrived, joint, coarse_columns, count
    )
    pieces = lax.all_to_all(projected.reshape(count, -1, wide), ROW, 0, 0)
    own_up = spread(pieces, coarse_columns)

    query_part, inner, outer = fine_sides(own_qkv, ext_kv[1:], own_up, out, side_shares)
    side_inner, side_outer = exchanged(inner, outer, COL)
    grad_query, top, middle, bottom = fine_middle(
        own_qkv, ext_kv[0], own_up, out, mid_shares, query_part
    )
    strips = add_strips(top, bottom, side_inner, side_outer)
    row_inner, row_outer = exchanged(*strips, ROW)
    grad_key, grad_value = add_all(middle, side_inner, side_outer, row_inner, row_outer)
    shape = (rows, columns, width)
    return grad_query.reshape(shape), grad_key.reshape(shape), grad_value.reshape(shape)


def solution(mesh):
    split = Mesh(mesh.devices.reshape(4, 2, 2, 4, 2), ROW + COL)
    return jax.shard_map(
        shards,
        mesh=split,
        in_specs=(
            P(None, ROW, COL, None),
            P(None, COL, None, ROW),
            P(COL, None, ROW),
            P(),
            P(None, None, ROW),
        ),
        out_specs=(P(ROW, COL, None), P(ROW, COL, None), P(ROW, COL, None)),
        check_vma=False,
    )
```

```python
import jax
import jax.numpy as jnp
from jax import lax
from jax.experimental import pallas as pl
from jax.experimental.pallas import tpu as pltpu
from jax.sharding import Mesh
from jax.sharding import PartitionSpec as P

HD = 64
RADIUS = 7
SCALE = 0.125
SIDE = 32
RIM = 8
HIDDEN = -1e30
ROW = ("x", "zh")
COL = ("zl", "y", "c")
F32 = jnp.float32
BF16 = jnp.bfloat16
VMEM = 24 << 20


def nt(left, right):
    return lax.dot_general(left, right, (((1,), (1,)), ((), ())), preferred_element_type=F32)


def nn(left, right):
    return lax.dot_general(left, right, (((1,), (0,)), ((), ())), preferred_element_type=F32)


def half(pair, which):
    lane = lax.broadcasted_iota(jnp.int32, pair.shape, 1)
    return jnp.where((lane < HD) == (which == 0), pair, jnp.zeros_like(pair))


def cost(flops, bytes_accessed, exps):
    return pl.CostEstimate(flops=flops, bytes_accessed=bytes_accessed, transcendentals=exps)


def prepare(coarse_qkv, grad_coarse):
    _, tokens, group = coarse_qkv.shape
    heads = group // HD

    def body(qkv_ref, up_ref, kv_out, qu_out):
        for head in range(heads):
            lanes = slice(head * HD, head * HD + HD)
            kv_out[head] = jnp.concatenate([qkv_ref[1, :, lanes], qkv_ref[2, :, lanes]], axis=1)
            qu_out[head] = jnp.concatenate([qkv_ref[0, :, lanes], up_ref[:, lanes]], axis=1)

    return whole_call(
        body,
        [jax.ShapeDtypeStruct((heads, tokens, 2 * HD), BF16)] * 2,
        "prepare",
        1 << 20,
        [],
        coarse_qkv,
        grad_coarse,
    )


def own_block(step, tokens):
    owner = lax.axis_index("y") ^ step
    return pl.ds(pl.multiple_of(owner * tokens, tokens), tokens)


def coarse_stats(key_values, query_ups, steps, before, key_tile):
    heads, tokens, _ = key_values[0].shape
    blocks, number = len(key_values), len(query_ups)
    per_block = tokens // key_tile

    def body(*refs):
        kv_refs, qu_refs = refs[:blocks], refs[blocks : blocks + number]
        out_ref, held = refs[-2:]
        if before:

            @pl.when(pl.program_id(1) == 0)
            def _():
                out_ref[...] = refs[blocks + number][...]

        for at in range(number):

            @pl.when(pl.program_id(1) == at)
            def _():
                held[...] = qu_refs[at][0]

        query = half(held[...], 0) * BF16(SCALE)
        upstream = half(held[...], 1)
        peak = jnp.full((1, tokens), -jnp.inf, F32)
        total = jnp.zeros((1, tokens), F32)
        weighted = jnp.zeros((1, tokens), F32)
        for i in range(blocks * per_block):
            start = (i % per_block) * key_tile
            tile = kv_refs[i // per_block][0, start : start + key_tile, :]
            score = nt(tile, query)
            product = nt(tile, upstream)
            new_peak = jnp.maximum(peak, jnp.max(score, axis=0, keepdims=True))
            decay = jnp.exp(peak - new_peak)
            share = jnp.exp(score - new_peak)
            total = total * decay + jnp.sum(share, axis=0, keepdims=True)
            weighted = weighted * decay + jnp.sum(share * product, axis=0, keepdims=True)
            peak = new_peak
        found = jnp.concatenate([peak + jnp.log(total), weighted / total], axis=0)
        for at, step in enumerate(steps):

            @pl.when(pl.program_id(1) == at)
            def _():
                out_ref[0, :, own_block(step, tokens)] = found

    pairs = heads * number * blocks * tokens**2
    return pl.pallas_call(
        body,
        grid=(heads, number),
        in_specs=[pl.BlockSpec((1, tokens, 128), lambda h, q: (h, 0, 0))] * (blocks + number)
        + [pl.BlockSpec((1, 2, blocks * tokens), lambda h, q: (h, 0, 0))] * len(before),
        out_specs=pl.BlockSpec((1, 2, blocks * tokens), lambda h, q: (h, 0, 0)),
        out_shape=jax.ShapeDtypeStruct((heads, 2, blocks * tokens), F32),
        scratch_shapes=[pltpu.VMEM((tokens, 128), BF16)],
        name="coarse_stats",
        cost_estimate=cost(4 * pairs * 256, 2 << 20, pairs),
        compiler_params=pltpu.CompilerParams(vmem_limit_bytes=VMEM),
    )(*key_values, *query_ups, *before)


def coarse_grads(key_values, query_ups, stats):
    heads, tokens, _ = key_values[0].shape
    blocks = len(query_ups)
    parts = len(stats)

    def body(*refs):
        kv_refs, qu_refs = refs[:blocks], refs[blocks : 2 * blocks]
        stats_refs = refs[2 * blocks : 2 * blocks + parts]
        kept_ref, sent_ref = refs[2 * blocks + parts : 2 * blocks + parts + 2]
        q_outs = refs[-blocks - 2 : -2]
        acc, held = refs[-2:]
        step = pl.program_id(1)
        for at in range(blocks):

            @pl.when(step == at // 2)
            def _():
                held[at % 2 * tokens : (at % 2 + 1) * tokens] = qu_refs[at][0]

        @pl.when(pl.program_id(1) == 0)
        def _():
            acc[...] = jnp.zeros_like(acc)

        query = half(held[...], 0) * BF16(SCALE)
        upstream = half(held[...], 1)
        found = [
            jnp.concatenate(
                [ref[0, :, own_block(2 * step + i, tokens)] for i in range(2)], axis=1
            )
            for ref in stats_refs
        ]
        peak = found[0][:1]
        for part in found[1:]:
            peak = jnp.maximum(peak, part[:1])
        shares = [jnp.exp(part[:1] - peak) for part in found]
        total = sum(shares)
        log_total = peak + jnp.log(total)
        delta = sum(share * part[1:] for share, part in zip(shares, found)) / total
        found = jnp.zeros((HD, 2 * tokens), F32)
        both = jnp.concatenate([query, upstream], axis=0)
        for i in range(blocks):
            tile = kv_refs[i][0]
            share = jnp.exp(nt(tile, query) - log_total)
            grads = (share * (nt(tile, upstream) - delta)).astype(BF16)
            acc[i] += nn(jnp.concatenate([grads, share.astype(BF16)], axis=1), both)
            found += nn(tile[:, :HD].T, grads)
        found = (found * SCALE).astype(BF16)
        for at in range(blocks):

            @pl.when(step == at // 2)
            def _():
                q_outs[at][...] = found[:, at % 2 * tokens : (at % 2 + 1) * tokens]

        @pl.when(step == blocks // 2 - 1)
        def _():
            for i in range(blocks // 2):
                kept_ref[i, 0] = acc[2 * i].astype(BF16)
                sent_ref[i, 0] = acc[2 * i + 1].astype(BF16)

    pairs = heads * (blocks * tokens) ** 2
    out_shape = [jax.ShapeDtypeStruct((blocks // 2, heads, tokens, 128), BF16)] * 2
    out_shape += [jax.ShapeDtypeStruct((heads * HD, tokens), BF16)] * blocks
    return pl.pallas_call(
        body,
        grid=(heads, blocks // 2),
        in_specs=[pl.BlockSpec((1, tokens, 128), lambda h, q: (h, 0, 0))] * (2 * blocks)
        + [pl.BlockSpec((1, 2, blocks * tokens), lambda h, q: (h, 0, 0))] * parts,
        out_specs=[pl.BlockSpec((blocks // 2, 1, tokens, 128), lambda h, q: (0, h, 0, 0))] * 2
        + [pl.BlockSpec((HD, tokens), lambda h, q: (h, 0))] * blocks,
        out_shape=out_shape,
        scratch_shapes=[
            pltpu.VMEM((blocks, tokens, 128), F32),
            pltpu.VMEM((2 * tokens, 128), BF16),
        ],
        name="coarse_grads",
        cost_estimate=cost(10 * pairs * 256, 4 << 20, pairs),
        compiler_params=pltpu.CompilerParams(vmem_limit_bytes=VMEM),
    )(*key_values, *query_ups, *stats)


def whole_call(body, out_shape, name, flops, scratch, *operands):
    return pl.pallas_call(
        body,
        out_shape=out_shape,
        scratch_shapes=scratch,
        name=name,
        cost_estimate=cost(flops, 6 << 20, 1 << 20),
        compiler_params=pltpu.CompilerParams(vmem_limit_bytes=VMEM),
    )(*operands)


def pairs_of(width):
    return [(pair, slice(pair * 128, pair * 128 + 128)) for pair in range(width // 128)]


def window_bias(own, rows, columns, part, transposed):
    count = SIDE * SIDE // 2
    shape = (own, count) if transposed else (count, own)
    ext = lax.broadcasted_iota(jnp.int32, shape, 1 if transposed else 0)
    inner = lax.broadcasted_iota(jnp.int32, shape, 0 if transposed else 1)
    if part == 0:
        ext_row, ext_column = ext >> 4, (ext & 15) + RIM
    else:
        ext_row = (ext & 255) >> 3
        ext_column = (ext & 7) + jnp.where(ext >= 256, SIDE - RIM, 0)
    row_gap = ext_row - (inner >> 4) - RIM
    column_gap = ext_column - (inner & 15) - RIM
    row = ext_row + (lax.axis_index(ROW) * rows - RIM)
    column = ext_column + (lax.axis_index(COL) * columns - RIM)
    seen = (jnp.abs(row_gap) <= RADIUS) & (jnp.abs(column_gap) <= RADIUS)
    seen &= (row >= 0) & (row < lax.axis_size(ROW) * rows)
    seen &= (column >= 0) & (column < lax.axis_size(COL) * columns)
    return jnp.where(seen, 0.0, HIDDEN).astype(F32)


def fill_bias(bias_ref, own, rows, columns):
    count = SIDE * SIDE // 2
    for part in range(2):
        bias_ref[part * count : (part + 1) * count, :] = window_bias(
            own, rows, columns, part, False
        )


def stacked(refs, which, lanes):
    return jnp.concatenate([ref[which, :, lanes] for ref in refs], axis=0)


def fine_shares(own_qkv, ext_kv, rows, columns):
    _, own, width = own_qkv.shape
    heads = width // HD
    count = SIDE * SIDE // 2

    def body(q_ref, mid_ref, low_ref, high_ref, mid_out, side_out, o_ref, bias_ref):
        fill_bias(bias_ref, own, rows, columns)
        ext = (mid_ref, low_ref, high_ref)
        for pair, lanes in pairs_of(width):
            key = stacked(ext, 0, lanes)
            value_t = stacked(ext, 1, lanes).T
            parts = []
            for side in range(2):
                query = half(q_ref[0, :, lanes], side) * BF16(SCALE)
                score = nt(key, query) + bias_ref[...]
                share = jnp.exp(score - jnp.max(score, axis=0, keepdims=True))
                total = jnp.sum(share, axis=0, keepdims=True)
                rounded = (share * (1.0 / total)).astype(BF16)
                mid_out[2 * pair + side] = rounded[:count]
                side_out[2 * pair + side] = rounded[count:]
                total = jnp.sum(rounded.astype(F32), axis=0, keepdims=True)
                parts.append(nn(value_t[side * HD : side * HD + HD], rounded) / total)
            o_ref[:, lanes] = jnp.concatenate(parts, axis=0).T

    return whole_call(
        body,
        [jax.ShapeDtypeStruct((heads, count, own), BF16)] * 2
        + [jax.ShapeDtypeStruct((own, width), F32)],
        "fine_shares",
        1 << 30,
        [pltpu.VMEM((SIDE * SIDE, own), F32)],
        own_qkv,
        *ext_kv,
    )


def pair_call(body, out_shape, name, flops, *operands):
    width = 384
    pairs = width // 128

    def spec(array):
        shape = tuple(array.shape)
        rank = len(shape)
        if shape[0] == 2 * pairs:
            return pl.BlockSpec((2,) + shape[1:], lambda p: (p,) + (0,) * (rank - 1))
        return pl.BlockSpec(
            shape[:-1] + (shape[-1] // pairs,), lambda p: (0,) * (rank - 1) + (p,)
        )

    return pl.pallas_call(
        body,
        grid=(pairs,),
        in_specs=[spec(array) for array in operands],
        out_specs=[spec(shape) for shape in out_shape],
        out_shape=out_shape,
        name=name,
        cost_estimate=cost(flops, 6 << 20, 0),
        compiler_params=pltpu.CompilerParams(vmem_limit_bytes=VMEM),
    )(*operands)


def head_sums(up, out):
    head = lax.broadcasted_iota(jnp.int32, (8, up.shape[1]), 0)
    lane = lax.broadcasted_iota(jnp.int32, (8, up.shape[1]), 1)
    pick = jnp.where((lane >> 6) == head, 1.0, 0.0).astype(F32)
    return lax.dot_general(
        pick,
        up * out,
        (((1,), (1,)), ((), ())),
        preferred_element_type=F32,
        precision=lax.Precision.HIGHEST,
    )


def pair_grads(q_ref, ext, up_ref, o_ref, share_ref):
    delta = head_sums(up_ref[...].astype(F32), o_ref[...])
    key = jnp.concatenate([ref[0] for ref in ext], axis=0)
    key_t = key.T
    value = jnp.concatenate([ref[1] for ref in ext], axis=0)
    parts = []
    key_sum = jnp.zeros(key.shape, F32)
    value_sum = jnp.zeros(key.shape, F32)
    for side in range(2):
        query = half(q_ref[0], side) * BF16(SCALE)
        up = half(up_ref[...], side)
        rounded = share_ref[side]
        product = nt(value, up) - delta[side : side + 1]
        grads = (rounded.astype(F32) * product).astype(BF16)
        key_sum += nn(grads, query)
        value_sum += nn(rounded, up)
        parts.append(nn(key_t[side * HD : side * HD + HD], grads))
    return jnp.concatenate(parts, axis=0).T, key_sum, value_sum


def fine_sides(own_qkv, sides, own_up, out, shares):
    _, own, width = own_qkv.shape
    size = sides[0].shape[1]

    def body(q_ref, low_ref, high_ref, up_ref, o_ref, share_ref, q_out, inner_out, outer_out):
        first = lax.axis_index("c") == 0
        q_out[...], *sums = pair_grads(q_ref, (low_ref, high_ref), up_ref, o_ref, share_ref)
        for at, total in zip((slice(0, 128), slice(128, 256)), sums):
            low, high = total[:size].astype(BF16), total[size:].astype(BF16)
            inner_out[:, at] = jnp.where(first, high, low)
            outer_out[:, at] = jnp.where(first, low, high)

    return pair_call(
        body,
        [jax.ShapeDtypeStruct((own, width), F32)]
        + [jax.ShapeDtypeStruct((size, 2 * width), BF16)] * 2,
        "fine_sides",
        1 << 30,
        own_qkv,
        *sides,
        own_up,
        out,
        shares,
    )


def fine_middle(own_qkv, middle, own_up, out, shares, query_part):
    _, own, width = own_qkv.shape
    size = middle.shape[1]
    edge = (size - own) // 2

    def body(q_ref, mid_ref, up_ref, o_ref, share_ref, part_ref, q_out, top, inside, bottom):
        found, *sums = pair_grads(q_ref, (mid_ref,), up_ref, o_ref, share_ref)
        q_out[...] = ((found + part_ref[...]) * SCALE).astype(BF16)
        for at, total in zip((slice(0, 128), slice(128, 256)), sums):
            top[:, at] = total[:edge]
            inside[:, at] = total[edge : edge + own]
            bottom[:, at] = total[edge + own :]

    return pair_call(
        body,
        [jax.ShapeDtypeStruct((own, width), BF16)]
        + [jax.ShapeDtypeStruct((count, 2 * width), F32) for count in (edge, own, edge)],
        "fine_middle",
        1 << 30,
        own_qkv,
        middle,
        own_up,
        out,
        shares,
        query_part,
    )


def beside_each_other(inner, outer):
    first = lax.axis_index("c") == 0
    cells, wide = inner.shape
    inner = inner.astype(F32).reshape(cells // RIM, RIM, wide)
    outer = outer.astype(F32).reshape(cells // RIM, RIM, wide)
    left, right = jnp.where(first, outer, inner), jnp.where(first, inner, outer)
    return jnp.concatenate([left, right], axis=1).reshape(2 * cells, wide)


def add_strips(top, bottom, inner, outer):
    edge, wide = top.shape
    corner = edge // 2
    sent = edge // RIM * RADIUS

    def body(top_ref, bottom_ref, inner_ref, outer_ref, inner_out, outer_out):
        upper = lax.axis_index("zh") == 0
        cells = inner_ref.shape[0]
        above = top_ref[...] + beside_each_other(inner_ref[:corner], outer_ref[:corner])
        below = bottom_ref[...] + beside_each_other(
            inner_ref[cells - corner :], outer_ref[cells - corner :]
        )
        above, below = above[edge - sent :], below[:sent]
        inner_out[...] = jnp.where(upper, below, above).astype(BF16)
        outer_out[...] = jnp.where(upper, above, below).astype(BF16)

    return whole_call(
        body,
        [jax.ShapeDtypeStruct((sent, wide), BF16)] * 2,
        "add_strips",
        1 << 20,
        [],
        top,
        bottom,
        inner,
        outer,
    )


def add_all(own, side_inner, side_outer, row_inner, row_outer):
    cells, wide = own.shape
    width = wide // 2
    half_cells = cells // 2

    def body(own_ref, side_in, side_out, row_in, row_out, k_out, v_out):
        upper = lax.axis_index("zh") == 0
        corner = (side_in.shape[0] - half_cells) // 2
        middle = slice(corner, corner + half_cells)
        inner, outer = row_in[...].astype(F32), row_out[...].astype(F32)
        above, below = jnp.where(upper, outer, inner), jnp.where(upper, inner, outer)
        skipped = jnp.zeros((cells - 2 * above.shape[0], wide), F32)
        total = own_ref[...] + jnp.concatenate([above, skipped, below], axis=0)
        total += beside_each_other(side_in[middle], side_out[middle])
        for pair, lanes in pairs_of(width):
            k_out[:, lanes] = total[:, pair * 256 : pair * 256 + 128].astype(BF16)
            v_out[:, lanes] = total[:, pair * 256 + 128 : pair * 256 + 256].astype(BF16)

    return whole_call(
        body,
        [jax.ShapeDtypeStruct((cells, width), BF16)] * 2,
        "add_all",
        1 << 20,
        [],
        own,
        side_inner,
        side_outer,
        row_inner,
        row_outer,
    )


def project(query_pieces, kept, from_core, arrived, joint, columns, count):
    group, tokens = query_pieces[0].shape
    heads = arrived.shape[0]
    rows = tokens // columns
    each = rows // count
    size = each * columns
    wide = joint.shape[1]
    chunk = 512
    blocks = len(query_pieces)

    def body(*refs):
        pieces = refs[:blocks]
        kept_ref, core_ref, arrived_ref, joint_ref, out, held, packed = refs[blocks:]

        @pl.when(pl.program_id(0) == 0)
        def _():
            for head in range(heads):
                total = kept_ref[0, head].astype(F32) + core_ref[0, head].astype(F32)
                total += arrived_ref[head].astype(F32)
                for part in range(2):
                    at = (1 + part) * group + head * HD
                    held[:, at : at + HD] = total[:, part * HD : (part + 1) * HD]
            total = pieces[0][...].astype(F32)
            for piece in pieces[1:]:
                total += piece[...].astype(F32)
            held[:, :group] = total.T
            for target in range(count):
                taken = []
                for c in range(columns):
                    start = c * rows + target * each
                    taken.append(held[start : start + each, :])
                chosen = jnp.concatenate(taken, axis=0).astype(BF16)
                packed[target * size : (target + 1) * size, :] = chosen

        out[...] = nn(packed[...], joint_ref[...]).astype(BF16)

    half_spec = pl.BlockSpec((1, heads, tokens, 128), lambda n: (0, 0, 0, 0))
    return pl.pallas_call(
        body,
        grid=(wide // chunk,),
        in_specs=[pl.BlockSpec((group, tokens), lambda n: (0, 0))] * blocks
        + [half_spec] * 2
        + [
            pl.BlockSpec(arrived.shape, lambda n: (0, 0, 0)),
            pl.BlockSpec((3 * group, chunk), lambda n: (0, n)),
        ],
        out_specs=pl.BlockSpec((tokens, chunk), lambda n: (0, n)),
        out_shape=jax.ShapeDtypeStruct((tokens, wide), BF16),
        scratch_shapes=[
            pltpu.VMEM((tokens, 3 * group), F32),
            pltpu.VMEM((tokens, 3 * group), BF16),
        ],
        name="project",
        cost_estimate=cost(2 << 30, 6 << 20, 0),
        compiler_params=pltpu.CompilerParams(vmem_limit_bytes=VMEM),
    )(*query_pieces, kept, from_core, arrived, joint)


def spread(pieces, columns):
    count, tokens, wide = pieces.shape
    width = wide // 4

    def body(in_ref, out):
        total = in_ref[0].astype(F32)
        for at in range(1, count):
            total += in_ref[at].astype(F32)
        total = total.astype(BF16)
        cells = 2 * tokens
        fine = lax.broadcasted_iota(jnp.int32, (cells, tokens), 0)
        token = lax.broadcasted_iota(jnp.int32, (cells, tokens), 1)
        cell = (token & 7) * 2 * columns + (token >> 3) * 2
        for a in range(2):
            grid = jnp.zeros((cells, width), F32)
            for b in range(2):
                place = jnp.where(fine == cell + b, 1.0, 0.0).astype(BF16)
                lanes = slice((2 * a + b) * width, (2 * a + b + 1) * width)
                grid += nn(place, total[:, lanes])
            grid = grid.astype(BF16)
            for row in range(tokens // columns):
                at = (2 * row + a) * 2 * columns
                out[at : at + 2 * columns, :] = grid[row * 2 * columns : (row + 1) * 2 * columns]

    return whole_call(
        body,
        jax.ShapeDtypeStruct((4 * tokens, width), BF16),
        "spread",
        1 << 28,
        [],
        pieces,
    )


def swapped(array, axis, flip=1):
    return lax.ppermute(array, axis, [(i, i ^ flip) for i in range(lax.axis_size(axis))])


def exchanged(inner, outer, axis):
    count = lax.axis_size(axis)
    beyond = [(i, ((i + 1) ^ 1) - 1) for i in range(1, count - 1)]
    return swapped(inner, axis), lax.ppermute(outer, axis, beyond)


def sent_rims(block, axis, parity, at):
    far = block.shape[at] - RIM
    first = lax.axis_index(parity) == 0
    inner = lax.dynamic_slice_in_dim(block, jnp.where(first, far, 0), RIM, axis=at)
    outer = lax.dynamic_slice_in_dim(block, jnp.where(first, 0, far), RIM, axis=at)
    return exchanged(inner, outer, axis)


def placed_rims(inner, outer, parity):
    first = lax.axis_index(parity) == 0
    return jnp.where(first, outer, inner), jnp.where(first, inner, outer)


def shards(fine_qkv, coarse_qkv, grad_coarse, merge_weight, qkv_weight):
    rows, columns, width = fine_qkv.shape[1:]
    own = rows * columns
    coarse_columns, coarse_rows, group = grad_coarse.shape
    tokens = coarse_columns * coarse_rows
    wide = merge_weight.shape[0]

    key_value, query_up = prepare(
        coarse_qkv.reshape(3, tokens, group), grad_coarse.reshape(tokens, group)
    )
    across = swapped(key_value, "zl")
    beside = swapped(key_value, "c")
    beside, query_up, fine_qkv = lax.optimization_barrier((beside, query_up, fine_qkv))
    near = [query_up, swapped(query_up, "y", 1), swapped(query_up, "y", 3)]
    own_qkv = fine_qkv.reshape(3, own, width)
    edges = sent_rims(fine_qkv[1:], ROW, "zh", 1)
    corner = swapped(across, "c")
    near = lax.optimization_barrier(near)
    far = swapped(near[0], "y", 2)
    keys = [key_value, beside, across, corner]
    queries = [near[0], near[1], far, near[2]]

    part = coarse_stats(keys, near, [0, 1, 3], (), 256)
    part, *edges = lax.optimization_barrier((part, *edges))
    low, high = placed_rims(*edges, "zh")
    tall = jnp.concatenate([low, fine_qkv[1:], high], axis=1)
    edges = sent_rims(tall, COL, "c", 2)
    part = coarse_stats(keys, [far], [2], (part,), 256)
    part, merge_weight, *edges = lax.optimization_barrier((part, merge_weight, *edges))
    joint = lax.dot_general(
        qkv_weight, merge_weight, (((1,), (1,)), ((), ())), preferred_element_type=F32
    ).astype(BF16).reshape(3 * group, wide)
    stats = [part] + [swapped(part, "y", step) for step in (1, 3, 2)]
    stats, joint = lax.optimization_barrier((stats, joint))
    kept, sent, *query_grads = coarse_grads(keys, queries, stats)

    query_pieces = [query_grads[0], swapped(query_grads[2], "y", 2)]
    from_core = swapped(sent, "c")
    passed = (kept[1].astype(F32) + from_core[1].astype(F32)).astype(BF16)
    arrived = swapped(passed, "zl")
    for step in (1, 3):
        query_pieces.append(swapped(query_grads[step], "y", step))
    count = lax.axis_size(ROW)
    low, high = placed_rims(*edges, "c")
    ext_kv = [array.reshape(2, -1, width) for array in (tall, low, high)]
    mid_shares, side_shares, out = fine_shares(own_qkv, ext_kv, rows, columns)
    arrived, out = lax.optimization_barrier((arrived, out))
    projected = project(
        query_pieces, kept, from_core, arrived, joint, coarse_columns, count
    )
    pieces = lax.all_to_all(projected.reshape(count, -1, wide), ROW, 0, 0)
    own_up = spread(pieces, coarse_columns)

    query_part, inner, outer = fine_sides(own_qkv, ext_kv[1:], own_up, out, side_shares)
    side_inner, side_outer = exchanged(inner, outer, COL)
    grad_query, top, middle, bottom = fine_middle(
        own_qkv, ext_kv[0], own_up, out, mid_shares, query_part
    )
    strips = add_strips(top, bottom, side_inner, side_outer)
    row_inner, row_outer = exchanged(*strips, ROW)
    grad_key, grad_value = add_all(middle, side_inner, side_outer, row_inner, row_outer)
    shape = (rows, columns, width)
    return grad_query.reshape(shape), grad_key.reshape(shape), grad_value.reshape(shape)


def solution(mesh):
    split = Mesh(mesh.devices.reshape(4, 2, 2, 4, 2), ROW + COL)
    return jax.shard_map(
        shards,
        mesh=split,
        in_specs=(
            P(None, ROW, COL, None),
            P(None, COL, None, ROW),
            P(COL, None, ROW),
            P(),
            P(None, None, ROW),
        ),
        out_specs=(P(ROW, COL, None), P(ROW, COL, None), P(ROW, COL, None)),
        check_vma=False,
    )
```
